512 devices in a mesh: gx: 32 (over y, x), gy: 16 (over z, core).
Axes of the slice: x: 4, y: 8, z: 8, core: 2. Of those that a mesh axis runs over, the one named last changes fastest.
Arguments:
- flow_state: float32 [5, 256, 16384], P(None, 'gx', 'gy'), as said below
- x_codes: int32 [2, 512], P(None, 'gy'), may hold values from 0 to 1
- y_codes: int32 [2, 256], P(None, 'gx'), may hold values from 0 to 1
Outputs:
- increment: float32 [5, 256, 16384], P(None, 'gx', 'gy')
The draws below stay inside these ranges and needn't reach their ends.
Inputs may be any that keep to these rules, and one draw needn't show every extreme that they name: `flow_state`: density lies in [0.75, 1.33], each velocity in [-0.5, 0.5], pressure in [0.6, 1.4]. `x_codes`: 0: the increment beyond the face is zero; 1: it equals that of the boundary cell. `y_codes`: 0: the increment beyond the face is zero; 1: it equals that of the boundary cell.
All inputs are finite; a program needn't handle non-finite values.
Results may differ from the reference program's by a relative error of at most 0.0003.
Values sent between devices are 32-bit elements; how exact they have to be, the bound alone decides.
A program may use at most 64 MiB of HBM per device.

```python
import math
import jax
import jax.numpy as jnp
from jax import lax

NZ = 32
NX = 256
NY = 512


def draw_flow_state(key, part):
    subkeys = jax.random.split(jax.random.fold_in(key, 17), 6)
    grid_shape = (NX, NY * NZ)
    phases = jax.random.uniform(subkeys[5], (4,), jnp.float32, 0.0, 2.0 * math.pi)
    rows_at = jnp.arange(NX, dtype=jnp.float32)[:, None] / NX
    columns_at = (jnp.arange(NY * NZ, dtype=jnp.int32) // NZ).astype(jnp.float32)[None, :] / NY
    wave_x = jnp.sin(2.0 * math.pi * rows_at + phases[0])
    wave_y = jnp.sin(2.0 * math.pi * columns_at + phases[1])
    wave_sum = jnp.sin(2.0 * math.pi * (rows_at + columns_at) + phases[2])
    wave_diff = jnp.sin(2.0 * math.pi * (rows_at - columns_at) + phases[3])
    density = jnp.clip(jnp.exp(0.08 * wave_sum + 0.08 * jax.random.normal(subkeys[0], grid_shape, jnp.float32)), 0.75, 1.33)
    vel_u = jnp.clip(0.15 * wave_x + 0.15 * jax.random.normal(subkeys[1], grid_shape, jnp.float32), -0.5, 0.5)
    vel_v = jnp.clip(0.15 * wave_y + 0.15 * jax.random.normal(subkeys[2], grid_shape, jnp.float32), -0.5, 0.5)
    vel_w = jnp.clip(0.2 * jax.random.normal(subkeys[3], grid_shape, jnp.float32), -0.5, 0.5)
    pressure = jnp.clip(jnp.exp(0.12 * wave_diff + 0.15 * jax.random.normal(subkeys[4], grid_shape, jnp.float32)), 0.6, 1.4)
    energy = pressure / 0.4 + 0.5 * density * (vel_u * vel_u + vel_v * vel_v + vel_w * vel_w)
    return jnp.stack([density, density * vel_u, density * vel_v, density * vel_w, energy])


def place_ends(drawn, key, least, largest):
    shape = drawn.shape
    place = [jax.random.randint(jax.random.fold_in(key, axis), (), 0, shape[axis]) for axis in range(len(shape))]
    drawn = drawn.at[tuple(place)].set(least)
    longest = shape.index(max(shape))
    place[longest] = (place[longest] + 1) % shape[longest]
    return drawn.at[tuple(place)].set(largest)


def setup_inputs(seed: int = 0) -> dict:
    arg_keys = jax.random.split(jax.random.key(seed), 4)
    return {
        "flow_state": draw_flow_state(jax.random.fold_in(arg_keys[3], 71), 0),
        "x_codes": place_ends(jax.random.randint(arg_keys[1], (2, NY), 0, 2), jax.random.fold_in(arg_keys[1], 1), 0, 1).astype(jnp.int32),
        "y_codes": place_ends(jax.random.randint(arg_keys[2], (2, NX), 0, 2), jax.random.fold_in(arg_keys[2], 1), 0, 1).astype(jnp.int32),
    }


GAMMA = 1.4
SIGMA = 0.5
DIFFUSE = 400.0

def primitives(conserved):
    density = conserved[0]
    vel_u = conserved[1] / density
    vel_v = conserved[2] / density
    vel_w = conserved[3] / density
    kinetic = 0.5 * (vel_u * vel_u + vel_v * vel_v + vel_w * vel_w)
    pressure = (GAMMA - 1.0) * (conserved[4] - density * kinetic)
    sound_speed = jnp.sqrt(GAMMA * pressure / density)
    return (density, vel_u, vel_v, vel_w, pressure, sound_speed)

def explicit_terms(padded):
    primitive = primitives(padded)
    density, vel_u, vel_v, vel_w, pressure, sound_speed = primitive
    enthalpy = padded[4] + pressure
    flux_x = jnp.stack([padded[1], padded[1] * vel_u + pressure, padded[2] * vel_u, padded[3] * vel_u, vel_u * enthalpy])
    flux_y = jnp.stack([padded[2], padded[1] * vel_v, padded[2] * vel_v + pressure, padded[3] * vel_v, vel_v * enthalpy])
    interior = padded[:, 1:-1, 1:-1]
    inner_speed = vel_w[1:-1, 1:-1]
    inner_pressure = pressure[1:-1, 1:-1]
    flux_z = jnp.stack([interior[3], interior[1] * inner_speed, interior[2] * inner_speed, interior[3] * inner_speed + inner_pressure, inner_speed * (interior[4] + inner_pressure)])
    change = flux_x[:, 2:, 1:-1] - flux_x[:, :-2, 1:-1] + (flux_y[:, 1:-1, 2:] - flux_y[:, 1:-1, :-2]) + (jnp.roll(flux_z, -1, axis=3) - jnp.roll(flux_z, 1, axis=3))
    smooth = padded[:, 2:, 1:-1] + padded[:, :-2, 1:-1] + padded[:, 1:-1, 2:] + padded[:, 1:-1, :-2] - 4.0 * interior
    residual = -0.5 * SIGMA * change + DIFFUSE * smooth
    return (residual, primitive)

def primitive_change(residual, primitive):
    density, vel_u, vel_v, vel_w, pressure, sound_speed = primitive
    change_u = (residual[1] - vel_u * residual[0]) / density
    change_v = (residual[2] - vel_v * residual[0]) / density
    change_w = (residual[3] - vel_w * residual[0]) / density
    kinetic = 0.5 * (vel_u * vel_u + vel_v * vel_v + vel_w * vel_w)
    change_pressure = (GAMMA - 1.0) * (residual[4] - vel_u * residual[1] - vel_v * residual[2] - vel_w * residual[3] + kinetic * residual[0])
    return (residual[0], change_u, change_v, change_w, change_pressure)

def to_characteristic(changes, primitive, normal_index):
    impedance = primitive[0] * primitive[5]
    normal_change = changes[normal_index]
    if normal_index == 1:
        tangent_one, tangent_two = (changes[2], changes[3])
    else:
        tangent_one, tangent_two = (changes[1], changes[3])
    pressure_change = changes[4]
    squared = primitive[5] * primitive[5]
    return jnp.stack([pressure_change - impedance * normal_change, squared * changes[0] - pressure_change, tangent_one, tangent_two, pressure_change + impedance * normal_change])

def from_characteristic(waves, primitive, normal_index):
    impedance = primitive[0] * primitive[5]
    squared = primitive[5] * primitive[5]
    pressure_change = 0.5 * (waves[0] + waves[4])
    normal_change = (waves[4] - waves[0]) / (2.0 * impedance)
    density_change = (waves[1] + pressure_change) / squared
    if normal_index == 1:
        return (density_change, normal_change, waves[2], waves[3], pressure_change)
    return (density_change, waves[2], normal_change, waves[3], pressure_change)

def to_conserved(changes, primitive):
    density, vel_u, vel_v, vel_w, pressure, sound_speed = primitive
    kinetic = 0.5 * (vel_u * vel_u + vel_v * vel_v + vel_w * vel_w)
    energy_change = kinetic * changes[0] + density * (vel_u * changes[1] + vel_v * changes[2] + vel_w * changes[3]) + changes[4] / (GAMMA - 1.0)
    return jnp.stack([changes[0], vel_u * changes[0] + density * changes[1], vel_v * changes[0] + density * changes[2], vel_w * changes[0] + density * changes[3], energy_change])

def eigenvalues(primitive, normal_index):
    normal_speed = primitive[normal_index]
    sound_speed = primitive[5]
    return jnp.stack([normal_speed - sound_speed, normal_speed, normal_speed, normal_speed, normal_speed + sound_speed])

def coefficients(speeds, face_codes, at_start, at_end):
    lower_band = -0.5 * SIGMA * speeds[:, :-2] - DIFFUSE
    upper_band = 0.5 * SIGMA * speeds[:, 2:] - DIFFUSE
    main_band = jnp.full(lower_band.shape, 1.0 + 2.0 * DIFFUSE, jnp.float32)
    first_neumann = jnp.logical_and(at_start, face_codes[0] == 1)
    last_neumann = jnp.logical_and(at_end, face_codes[1] == 1)
    main_band = main_band.at[:, 0].add(jnp.where(first_neumann, lower_band[:, 0], 0.0))
    main_band = main_band.at[:, -1].add(jnp.where(last_neumann, upper_band[:, -1], 0.0))
    lower_band = lower_band.at[:, 0].set(jnp.where(at_start, 0.0, lower_band[:, 0]))
    upper_band = upper_band.at[:, -1].set(jnp.where(at_end, 0.0, upper_band[:, -1]))
    return (lower_band, main_band, upper_band)

def thomas_rows(lower_band, main_band, upper_band, right_side):
    nothing = jnp.zeros_like(right_side[0])

    def forward_step(carry, row_set):
        prev_upper, prev_value = carry
        lower_row, main_row, upper_row, right_row = row_set
        pivot_value = main_row - lower_row * prev_upper
        next_upper = upper_row / pivot_value
        next_value = (right_row - lower_row * prev_value) / pivot_value
        return ((next_upper, next_value), (next_upper, next_value))
    final_carry, (uppers, values) = lax.scan(forward_step, (nothing, nothing), (lower_band, main_band, upper_band, right_side))

    def backward_step(later_value, row_set):
        upper_row, value_row = row_set
        current = value_row - upper_row * later_value
        return (current, current)
    last_carry, result = lax.scan(backward_step, nothing, (uppers, values), reverse=True)
    return result

def whole_lines(band_set, right_side):
    moved_items = [jnp.moveaxis(member, 1, 0) for member in (band_set[0], band_set[1], band_set[2], right_side)]
    solved = thomas_rows(moved_items[0], moved_items[1], moved_items[2], moved_items[3])
    return jnp.moveaxis(solved, 0, 1)

def reference(flow_state, x_codes, y_codes):
    conserved = flow_state.reshape(5, NX, NY, NZ)
    padded = jnp.pad(conserved, ((0, 0), (1, 1), (1, 1), (0, 0)), mode='edge')
    residual, primitive = explicit_terms(padded)
    interior = tuple((member[1:-1, 1:-1] for member in primitive))
    changes = primitive_change(residual, interior)
    speeds_x = eigenvalues(tuple((member[:, 1:-1] for member in primitive)), 1).reshape(5, NX + 2, NY * NZ)
    codes_x = jnp.broadcast_to(x_codes[:, :, None], (2, NY, NZ)).reshape(2, NY * NZ)
    band_set = coefficients(speeds_x, codes_x, True, True)
    right_x = to_characteristic(changes, interior, 1).reshape(5, NX, NY * NZ)
    solved_x = whole_lines(band_set, right_x).reshape(5, NX, NY, NZ)
    changes = from_characteristic(solved_x, interior, 1)
    right_y = jnp.transpose(to_characteristic(changes, interior, 2), (0, 2, 1, 3)).reshape(5, NY, NX * NZ)
    speeds_y = jnp.transpose(eigenvalues(tuple((member[1:-1] for member in primitive)), 2), (0, 2, 1, 3)).reshape(5, NY + 2, NX * NZ)
    codes_y = jnp.broadcast_to(y_codes[:, :, None], (2, NX, NZ)).reshape(2, NX * NZ)
    band_set = coefficients(speeds_y, codes_y, True, True)
    solved_y = jnp.transpose(whole_lines(band_set, right_y).reshape(5, NY, NX, NZ), (0, 2, 1, 3))
    changes = from_characteristic(solved_y, interior, 2)
    return to_conserved(changes, interior).reshape(5, NX, NY * NZ)
```

```python
import functools

import jax
import jax.numpy as jnp
from jax import lax
from jax.experimental import pallas as pl
from jax.experimental.pallas import tpu as pltpu
from jax.sharding import PartitionSpec as P

NZ = 32
SX = 32
SY = 16
TY = 8
MAIN = 801.0
GROUPS = ((0, (0,)), (2, (4,)), (1, (1, 2)), (1, (3,)))
MESH = pl.DeviceIdType.MESH


def roll(value, shift, axis):
    axis = axis % value.ndim
    return pltpu.roll(value, shift % value.shape[axis], axis)


def lane_of(shape):
    return lax.broadcasted_iota(jnp.int32, shape, len(shape) - 1)


def row_of(shape):
    return lax.broadcasted_iota(jnp.int32, shape, len(shape) - 2)


def five(value):
    return jnp.concatenate([value[0:1], value[1:2], value[1:2], value[1:2], value[2:3]])


def primitives(q):
    inv = 1.0 / q[0]
    u, v, w = q[1] * inv, q[2] * inv, q[3] * inv
    p = 0.4 * (q[4] - 0.5 * (q[1] * u + q[2] * v + q[3] * w))
    c2 = 1.4 * p * inv
    return inv, u, v, w, p, c2, c2 * lax.rsqrt(c2)


def up_y(value):
    here, after = value[..., 1:9, :, :], value[..., 2:10, :, :]
    return roll(jnp.where(lane_of(here.shape) < 32, after, here), -32, -1)


def down_y(value):
    before, here = value[..., 0:8, :, :], value[..., 1:9, :, :]
    return roll(jnp.where(lane_of(here.shape) >= 96, before, here), 32, -1)


def z_difference(value):
    z = lane_of(value.shape) & 31
    after = jnp.where(z == 31, roll(value, 31, -1), roll(value, -1, -1))
    before = jnp.where(z == 0, roll(value, -31, -1), roll(value, 1, -1))
    return after - before


def yz_part(q):
    inv, u, v, w, p, c2, c = primitives(q)
    flux = jnp.stack([q[2], q[1] * v, q[2] * v + p, q[3] * v, v * (q[4] + p)])
    smooth = 400.0 * q
    flux = 0.25 * flux
    inner, wi, pi = q[:, 1:9], w[1:9], p[1:9]
    flux_z = jnp.stack(
        [inner[3], inner[1] * wi, inner[2] * wi, inner[3] * wi + pi, wi * (inner[4] + pi)]
    )
    part = up_y(smooth - flux) + down_y(smooth + flux) - 1600.0 * inner
    part = part - 0.25 * z_difference(flux_z)
    speeds = jnp.stack([v, c])
    return part, jnp.concatenate([down_y(speeds), up_y(speeds)])


def x_part(q, prim):
    inv, u, v, w, p, c2, c = prim
    flux = jnp.stack([q[1], q[1] * u + p, q[2] * u, q[3] * u, u * (q[4] + p)])
    smooth = 400.0 * q
    flux = 0.25 * flux
    return (smooth - flux)[:, 2:10] + (smooth + flux)[:, 0:8]


def x_right(res, prim):
    inv, u, v, w, p, c2, c = prim
    kinetic = 0.5 * (u * u + v * v + w * w)
    dp = 0.4 * (res[4] - u * res[1] - v * res[2] - w * res[3] + kinetic * res[0])
    normal = c * (res[1] - u * res[0])
    return jnp.stack(
        [
            dp - normal,
            c2 * res[0] - dp,
            (res[2] - v * res[0]) * inv,
            (res[3] - w * res[0]) * inv,
            dp + normal,
        ]
    )


def eliminate(lower, upper, main_first, main_last):
    n = len(lower)
    m = [1.0 / main_first]
    g = [upper[0] * m[0]]
    p = [-lower[0] * m[0]]
    for k in range(1, n - 1):
        m.append(1.0 / (MAIN - lower[k] * g[k - 1]))
        g.append(upper[k] * m[k])
        p.append(-(lower[k] * p[k - 1]) * m[k])
    q = [None] * (n - 1)
    q[n - 2] = -g[n - 2]
    for k in range(n - 3, -1, -1):
        p[k] = p[k] - g[k] * p[k + 1]
        q[k] = -(g[k] * q[k + 1])
    last = 1.0 / (main_last + lower[n - 1] * q[n - 2])
    m.append(last)
    own = (-(lower[n - 1] * p[n - 2]) * last, -upper[n - 1] * last, p[0], q[0])
    return m, g, p, q, own


def eliminate_right(right, lower, m, g):
    n = len(right)
    d = [right[0] * five(m[0])]
    for k in range(1, n - 1):
        d.append((right[k] - five(lower[k]) * d[k - 1]) * five(m[k]))
    for k in range(n - 3, -1, -1):
        d[k] = d[k] - five(g[k]) * d[k + 1]
    last = (right[n - 1] - five(lower[n - 1]) * d[n - 2]) * five(m[n - 1])
    return d, last


def put_back(d, p, q, before, own):
    cells = [d[k] + five(p[k]) * before + five(q[k]) * own for k in range(len(d))]
    return cells + [own]


def factor(own):
    to_before, to_after, first_before, first_own = own
    rows = to_before.shape[-2]
    den = 1.0 / (1.0 - to_after * roll(first_before, -1, -2))
    a = to_before * den
    c = to_after * roll(first_own, -1, -2) * den
    return den, to_after * den, a, c


def factor_levels(a, c):
    rows = a.shape[-2]
    levels = []
    step = 1
    while step < rows:
        dn = 1.0 / (1.0 - a * roll(c, step, -2) - c * roll(a, -step, -2))
        an, cn = a * dn, c * dn
        levels.append((dn, an, cn))
        a, c = an * roll(a, step, -2), cn * roll(c, -step, -2)
        step *= 2
    return levels


def reduce_levels(d, levels):
    step = 1
    for dn, an, cn in levels:
        d = dn * d + an * roll(d, step, -2) + cn * roll(d, -step, -2)
        step *= 2
    return d


def y_right(s, rc, half_rc_inv):
    dp = 0.5 * (s[0] + s[4])
    normal = rc * s[2]
    return jnp.stack([dp - normal, s[1], (s[4] - s[0]) * half_rc_inv, s[3], dp + normal])


def swap_groups(value):
    lead = value.shape[:-3]
    half = value.reshape(*lead, 2, 2, 2, 8, 128)
    a, b = half[..., 0, :, :, :], half[..., 1, :, :, :]
    low = (lane_of(a.shape) & 64) == 0
    a, b = jnp.where(low, a, roll(b, 64, -1)), jnp.where(low, roll(a, 64, -1), b)
    half = jnp.stack([a, b], axis=len(lead) + 1)
    a, b = half[..., 0, :, :], half[..., 1, :, :]
    low = (lane_of(a.shape) & 32) == 0
    a, b = jnp.where(low, a, roll(b, 32, -1)), jnp.where(low, roll(a, -32, -1), b)
    half = jnp.stack([a, b], axis=len(lead) + 2)
    return half.reshape(*lead, 8, 8, 128)


def y_bands(speeds):
    vm, cm, vp, cp = (speeds[i].reshape(2, 4, 8, 128) for i in range(4))
    low = jnp.stack([vm - cm, vm, vm + cm])
    high = jnp.stack([vp - cp, vp, vp + cp])
    lower = [-0.25 * low[:, :, k] - 400.0 for k in range(4)]
    upper = [0.25 * high[:, :, k] - 400.0 for k in range(4)]
    return lower, upper


def y_join(own):
    row = row_of(own[0].shape)
    den, high, a, c = factor(own)
    p = jnp.where(row == 0, a, 0.0)
    q = jnp.where(row == 7, 1.0, 0.0)
    a = jnp.where((row == 0) | (row == 7), 0.0, a)
    c = jnp.where(row == 7, 0.0, c)
    levels = factor_levels(a, c)
    p = reduce_levels(p, levels)
    q = reduce_levels(q, levels)
    last = 1.0 / (1.0 - own[0] * roll(q, 1, -2))
    joined = (
        own[0] * roll(p, 1, -2) * last,
        own[1] * last,
        own[2] + own[3] * p,
        own[3] * q,
    )
    return den, high, levels, p, q, last, joined


def y_join_right(d0, last_right, own, den, high, levels, last):
    row = row_of(last_right.shape)
    d = five(den) * last_right + five(high) * roll(d0, -1, -2)
    d = jnp.where(row == 7, 0.0, d)
    d = reduce_levels(d, [tuple(five(part) for part in level) for level in levels])
    joined_last = (last_right + five(own[0]) * roll(d, 1, -2)) * five(last)
    joined_first = d0 + five(own[3]) * d
    return d, joined_last, joined_first


def increments(s, prim, r, half_rc_inv, c2_inv):
    inv, u, v, w, p, c2, c = prim
    dp = 0.5 * (s[0] + s[4])
    dv = (s[4] - s[0]) * half_rc_inv
    dr = (s[1] + dp) * c2_inv
    du, dw = s[2], s[3]
    kinetic = 0.5 * (u * u + v * v + w * w)
    return (
        dr,
        u * dr + r * du,
        v * dr + r * dv,
        w * dr + r * dw,
        kinetic * dr + r * (u * du + v * dv + w * dw) + 2.5 * dp,
    )


def x_code_mask(codes, side):
    ones = (codes[side : side + 1] == 1).astype(jnp.float32)
    spread = jnp.where((lane_of((8, 32)) >> 2) == row_of((8, 32)), ones, 0.0)
    place = jnp.where((row_of((32, 128)) & 3) == (lane_of((32, 128)) >> 5), 1.0, 0.0)
    return jnp.dot(spread, place, preferred_element_type=jnp.float32) > 0.5


def y_code_mask(codes, side):
    ones = jnp.broadcast_to((codes[side : side + 1] == 1).astype(jnp.float32), (8, 8))
    halves = []
    for h in range(2):
        place = jnp.where(row_of((8, 128)) == 4 * h + (lane_of((8, 128)) >> 5), 1.0, 0.0)
        halves.append(jnp.dot(ones, place, preferred_element_type=jnp.float32))
    return jnp.stack(halves) > 0.5


def x_bands(u, c, codes, start, end):
    lam = jnp.stack([u - c, u, u + c])
    lower = [-0.25 * lam[:, k] - 400.0 for k in range(8)]
    upper = [0.25 * lam[:, k + 2] - 400.0 for k in range(8)]
    first = MAIN + jnp.where(x_code_mask(codes, 0)[None] & start, lower[0], 0.0)
    last = MAIN + jnp.where(x_code_mask(codes, 1)[None] & end, upper[7], 0.0)
    lower[0] = jnp.where(start, 0.0, lower[0])
    upper[7] = jnp.where(end, 0.0, upper[7])
    return lower, upper, first, last


def y_ends(lower, upper, codes, start, end):
    row = row_of(lower[0].shape)
    at_start = (row == 0) & start
    at_end = (row == 7) & end
    first = MAIN + jnp.where(at_start & y_code_mask(codes, 0)[None], lower[0], 0.0)
    last = MAIN + jnp.where(at_end & y_code_mask(codes, 1)[None], upper[3], 0.0)
    lower, upper = list(lower), list(upper)
    lower[0] = jnp.where(at_start, 0.0, lower[0])
    upper[3] = jnp.where(at_end, 0.0, upper[3])
    return lower, upper, first, last


def wait_all(ref, sem):
    pltpu.make_async_copy(ref, ref, sem).wait()


def kernel(
    flow,
    x_codes,
    y_codes,
    out,
    q_sc,
    part_sc,
    out_sc,
    speed_sc,
    x_send,
    x_low,
    x_high,
    y_low,
    y_high,
    xm_out,
    xr_out,
    xm_in,
    xr_in,
    xs_out,
    xs_in,
    ym_out,
    yr_out,
    ym_in,
    yr_in,
    ys_out,
    ys_in,
    y_levels,
    in_sem,
    out_sem,
    halo_send,
    halo_recv,
    send_sem,
    recv_sem,
):
    gx, gy = lax.axis_index("gx"), lax.axis_index("gy")
    start_x, end_x = gx == 0, gx == SX - 1
    start_y, end_y = gy == 0, gy == SY - 1

    for b in range(8):
        pltpu.make_async_copy(
            flow.at[:, :, pl.ds(128 * b, 128)], q_sc.at[:, pl.ds(8 * b, 8), :], in_sem
        ).start()

    barrier = pltpu.get_barrier_semaphore()

    def greet_x(k, carry):
        pl.semaphore_signal(
            barrier, inc=1, device_id=(lax.rem(gx + k, SX), gy), device_id_type=MESH
        )
        return carry

    def greet_y(k, carry):
        pl.semaphore_signal(
            barrier, inc=1, device_id=(gx, lax.rem(gy + k, SY)), device_id_type=MESH
        )
        return carry

    lax.fori_loop(1, SX, greet_x, 0)
    lax.fori_loop(1, SY, greet_y, 0)
    wait_all(q_sc, in_sem)

    x_send[0] = q_sc[:, pl.ds(7, 8, stride=8), :]
    x_send[1] = q_sc[:, pl.ds(0, 8, stride=8), :]
    pl.semaphore_wait(barrier, SX + SY - 2)

    x_after, x_before = lax.rem(gx + 1, SX), lax.rem(gx + SX - 1, SX)
    y_after, y_before = lax.rem(gy + 1, SY), lax.rem(gy + SY - 1, SY)
    halos = [
        (x_send.at[0], x_low, (x_after, gy)),
        (x_send.at[1], x_high, (x_before, gy)),
        (q_sc.at[:, pl.ds(56, 8), :], y_low, (gx, y_after)),
        (q_sc.at[:, pl.ds(0, 8), :], y_high, (gx, y_before)),
    ]
    copies = []
    for i, (source, target, device) in enumerate(halos):
        copy = pltpu.make_async_remote_copy(
            src_ref=source,
            dst_ref=target,
            send_sem=halo_send.at[i],
            recv_sem=halo_recv.at[i],
            device_id=device,
            device_id_type=MESH,
        )
        copy.start()
        copies.append(copy)

    def send_x(source, target, slot):
        mine = pl.ds(gx * 4, 4)
        pltpu.make_async_copy(source.at[mine], target.at[mine], recv_sem.at[slot]).start()

        def one(k, carry):
            other = lax.rem(gx + k, SX)
            pltpu.make_async_remote_copy(
                src_ref=source.at[pl.ds(other * 4, 4)],
                dst_ref=target.at[mine],
                send_sem=send_sem.at[slot],
                recv_sem=recv_sem.at[slot],
                device_id=(other, gy),
                device_id_type=MESH,
            ).start()
            return carry

        lax.fori_loop(1, SX, one, 0)

    solver_y = lax.rem(gy, 2) == 0
    tile_y = lax.div(gy, 2)

    def send_y(source, target, slot):
        @pl.when(solver_y)
        def _():
            pltpu.make_async_copy(
                source.at[pl.ds(tile_y * 4, 4)], target.at[pl.ds(gy * 4, 4)], recv_sem.at[slot]
            ).start()

        def one(t, carry):
            @pl.when(gy != 2 * t)
            def _():
                pltpu.make_async_remote_copy(
                    src_ref=source.at[pl.ds(t * 4, 4)],
                    dst_ref=target.at[pl.ds(gy * 4, 4)],
                    send_sem=send_sem.at[slot],
                    recv_sem=recv_sem.at[slot],
                    device_id=(gx, 2 * t),
                    device_id_type=MESH,
                ).start()

            return carry

        lax.fori_loop(0, TY, one, 0)

    for copy in copies:
        copy.wait_recv()
    inner = [q_sc[:, pl.ds(k, 8, stride=8), :] for k in range(8)]
    low = jnp.where(start_x, inner[0], x_low[...])
    high = jnp.where(end_x, inner[7], x_high[...])
    q = jnp.stack([low] + inner + [high], axis=1)
    prim_all = primitives(q)

    lower, upper, first, last = x_bands(prim_all[1], prim_all[6], x_codes[...], start_x, end_x)
    xm, xg, xp, xq, x_own = eliminate(lower, upper, first, last)
    for group, (matrix, families) in enumerate(GROUPS):
        for row in range(4):
            xm_out[pl.ds(group * 32 + row, 8, stride=4), :] = x_own[row][matrix]
    send_x(xm_out, xm_in, 0)

    blocks = q_sc[...].reshape(5, 8, 8, 128)
    y_edge_low = jnp.where(start_y, roll(blocks[:, 0], 96, -1), y_low[...])
    y_edge_high = jnp.where(end_y, roll(blocks[:, 7], 32, -1), y_high[...])
    part, speeds = yz_part(
        jnp.concatenate([y_edge_low[:, None], blocks, y_edge_high[:, None]], axis=1)
    )
    part_sc[...] = part.reshape(5, 64, 128)
    speed_sc[...] = speeds.reshape(4, 64, 128)
    prim = tuple(value[1:9] for value in prim_all)
    residual = x_part(q, prim_all) + jnp.stack(
        [part_sc[:, pl.ds(k, 8, stride=8), :] for k in range(8)], axis=1
    )
    right = x_right(residual, prim)
    xd, x_last = eliminate_right([right[:, k] for k in range(8)], lower, xm, xg)
    zero = jnp.zeros((8, 128), jnp.float32)
    for group, (matrix, families) in enumerate(GROUPS):
        for i in range(2):
            at = group * 32 + 2 * i
            some = i < len(families)
            xr_out[pl.ds(at, 8, stride=4), :] = x_last[families[i]] if some else zero
            xr_out[pl.ds(at + 1, 8, stride=4), :] = xd[0][families[i]] if some else zero
    send_x(xr_out, xr_in, 1)

    speeds = jnp.stack([speed_sc[:, pl.ds(k, 8, stride=8), :] for k in range(8)], axis=1)
    y_lower, y_upper = y_bands(swap_groups(speeds))
    y_lower, y_upper, first, last = y_ends(y_lower, y_upper, y_codes[...], start_y, end_y)
    ym, yg, yp, yq, y_own = eliminate(y_lower, y_upper, first, last)
    y_den, y_high_part, y_lev, y_p, y_q, y_joint, joined = y_join(y_own)
    for group, (matrix, families) in enumerate(GROUPS):
        for h in range(2):
            at = (group * 2 + h) * 4
            for row in range(4):
                line = 7 if row < 2 else 0
                ym_out[pl.ds(at + row, 1), :] = joined[row][matrix, h, line : line + 1]
    send_y(ym_out, ym_in, 3)

    wait_all(xm_in, recv_sem.at[0])
    den, high_part, a, c = factor([xm_in[pl.ds(row, SX, stride=4), :] for row in range(4)])
    levels = factor_levels(a, c)
    wait_all(xr_in, recv_sem.at[1])
    for i in range(2):
        own_last = xr_in[pl.ds(2 * i, SX, stride=4), :]
        own_first = xr_in[pl.ds(2 * i + 1, SX, stride=4), :]
        d = den * own_last + high_part * roll(own_first, -1, 0)
        d = reduce_levels(d, levels)
        xs_out[pl.ds(2 * i, SX, stride=4), :] = roll(d, 1, 0)
        xs_out[pl.ds(2 * i + 1, SX, stride=4), :] = d
    send_x(xs_out, xs_in, 2)

    @pl.when(solver_y)
    def _():
        wait_all(ym_in, recv_sem.at[3])
        den, high_part, a, c = factor([ym_in[pl.ds(row, SY, stride=4), :] for row in range(4)])
        y_levels[0], y_levels[1] = den, high_part
        for i, level in enumerate(factor_levels(a, c)):
            for j in range(3):
                y_levels[2 + 3 * i + j] = level[j]

    r = q[0, 1:9]
    rc = r * prim[6]
    half_rc_inv = 0.5 / rc
    c2_inv = 1.0 / prim[5]

    wait_all(xs_in, recv_sem.at[2])

    def x_value(kind):
        rows = []
        for group, i in ((0, 0), (2, 0), (2, 1), (3, 0), (1, 0)):
            rows.append(xs_in[pl.ds(group * 32 + 2 * i + kind, 8, stride=4), :])
        return jnp.stack(rows)

    solved = jnp.stack(put_back(xd, xp, xq, x_value(0), x_value(1)), axis=1)
    right = swap_groups(y_right(solved, rc, half_rc_inv)).reshape(5, 2, 4, 8, 128)
    yd, y_last = eliminate_right([right[:, :, k] for k in range(4)], y_lower, ym, yg)
    y_d, joined_last, joined_first = y_join_right(
        yd[0], y_last, y_own, y_den, y_high_part, y_lev, y_joint
    )
    line_zero = jnp.zeros((1, 128), jnp.float32)
    for group, (matrix, families) in enumerate(GROUPS):
        for h in range(2):
            for i in range(2):
                at = (group * 2 + h) * 4 + 2 * i
                some = i < len(families)
                yr_out[pl.ds(at, 1), :] = joined_last[families[i], h, 7:8] if some else line_zero
                yr_out[pl.ds(at + 1, 1), :] = (
                    joined_first[families[i], h, 0:1] if some else line_zero
                )
    send_y(yr_out, yr_in, 4)

    @pl.when(solver_y)
    def _():
        wait_all(yr_in, recv_sem.at[4])
        levels = [tuple(y_levels[2 + 3 * i + j] for j in range(3)) for i in range(4)]
        for i in range(2):
            own_last = yr_in[pl.ds(2 * i, SY, stride=4), :]
            own_first = yr_in[pl.ds(2 * i + 1, SY, stride=4), :]
            d = y_levels[0] * own_last + y_levels[1] * roll(own_first, -1, 0)
            d = reduce_levels(d, levels)
            ys_out[pl.ds(2 * i, SY, stride=4), :] = roll(d, 1, 0)
            ys_out[pl.ds(2 * i + 1, SY, stride=4), :] = d
        pltpu.make_async_copy(
            ys_out.at[pl.ds(gy * 4, 4)], ys_in.at[pl.ds(tile_y * 4, 4)], recv_sem.at[5]
        ).start()

        def one(k, carry):
            other = lax.rem(gy + k, SY)
            pltpu.make_async_remote_copy(
                src_ref=ys_out.at[pl.ds(other * 4, 4)],
                dst_ref=ys_in.at[pl.ds(tile_y * 4, 4)],
                send_sem=send_sem.at[5],
                recv_sem=recv_sem.at[5],
                device_id=(gx, other),
                device_id_type=MESH,
            ).start()
            return carry

        lax.fori_loop(1, SY, one, 0)

    wait_all(ys_in, recv_sem.at[5])

    def y_value(kind):
        rows = []
        for group, i in ((0, 0), (2, 0), (2, 1), (3, 0), (1, 0)):
            rows.append(
                jnp.stack([ys_in[pl.ds((group * 2 + h) * 4 + 2 * i + kind, 1), :] for h in range(2)])
            )
        return jnp.stack(rows)

    before, own = y_value(0), y_value(1)
    groups = y_d + five(y_p) * before + five(y_q) * own
    previous = jnp.where(row_of(groups.shape) == 0, before, roll(groups, 1, -2))
    solved = jnp.stack(put_back(yd, yp, yq, previous, groups), axis=2)
    solved = swap_groups(solved.reshape(5, 8, 8, 128))
    for field, value in enumerate(increments(solved, prim, r, half_rc_inv, c2_inv)):
        for k in range(8):
            out_sc[field, pl.ds(k, 8, stride=8), :] = value[k]
    for b in range(8):
        pltpu.make_async_copy(
            out_sc.at[:, pl.ds(8 * b, 8), :], out.at[:, :, pl.ds(128 * b, 128)], out_sem
        ).start()

    for copy in copies:
        copy.wait_send()
    for slot in range(3):
        wait_all(xm_out.at[pl.ds(0, 4 * (SX - 1))], send_sem.at[slot])

    @pl.when(solver_y)
    def _():
        for slot in (3, 4):
            wait_all(ym_out.at[pl.ds(0, 4 * (TY - 1))], send_sem.at[slot])
        wait_all(ys_out.at[pl.ds(0, 4 * (SY - 1))], send_sem.at[5])

    @pl.when(jnp.logical_not(solver_y))
    def _():
        for slot in (3, 4):
            wait_all(ym_out, send_sem.at[slot])

    wait_all(out_sc, out_sem)


def local(flow_state, x_codes, y_codes):
    f32 = jnp.float32

    def vmem(*shape):
        return pltpu.VMEM(shape, f32)

    return pl.pallas_call(
        kernel,
        out_shape=jax.ShapeDtypeStruct(flow_state.shape, f32),
        in_specs=[
            pl.BlockSpec(memory_space=pl.ANY),
            pl.BlockSpec(memory_space=pltpu.VMEM),
            pl.BlockSpec(memory_space=pltpu.VMEM),
        ],
        out_specs=pl.BlockSpec(memory_space=pl.ANY),
        scratch_shapes=[
            vmem(5, 64, 128),
            vmem(5, 64, 128),
            vmem(5, 64, 128),
            vmem(4, 64, 128),
            vmem(2, 5, 8, 128),
            vmem(5, 8, 128),
            vmem(5, 8, 128),
            vmem(5, 8, 128),
            vmem(5, 8, 128),
            vmem(4 * SX, 128),
            vmem(4 * SX, 128),
            vmem(4 * SX, 128),
            vmem(4 * SX, 128),
            vmem(4 * SX, 128),
            vmem(4 * SX, 128),
            vmem(4 * TY, 128),
            vmem(4 * TY, 128),
            vmem(4 * SY, 128),
            vmem(4 * SY, 128),
            vmem(4 * SY, 128),
            vmem(4 * TY, 128),
            vmem(14, SY, 128),
            pltpu.SemaphoreType.DMA,
            pltpu.SemaphoreType.DMA,
            pltpu.SemaphoreType.DMA((4,)),
            pltpu.SemaphoreType.DMA((4,)),
            pltpu.SemaphoreType.DMA((6,)),
            pltpu.SemaphoreType.DMA((6,)),
        ],
        compiler_params=pltpu.CompilerParams(
            collective_id=0, has_side_effects=True, vmem_limit_bytes=32 * 1024 * 1024
        ),
        name="step",
    )(flow_state, x_codes, y_codes)


def solution(mesh):
    return jax.shard_map(
        local,
        mesh=mesh,
        in_specs=(P(None, "gx", "gy"), P(None, "gy"), P(None, "gx")),
        out_specs=P(None, "gx", "gy"),
        check_vma=False,
    )
```

```python
import functools

import jax
import jax.numpy as jnp
from jax import lax
from jax.experimental import pallas as pl
from jax.experimental.pallas import tpu as pltpu
from jax.sharding import PartitionSpec as P

NZ = 32
SX = 32
SY = 16
VMEM_LIMIT = 56 * 1024 * 1024
MAIN = 801.0
GROUPS = ((0, (0,)), (2, (4,)), (1, (1, 2)), (1, (3,)))
MESH = pl.DeviceIdType.MESH


def far_first(*lengths):
    offsets = [()]
    for length in lengths:
        offsets = [(*offset, k) for offset in offsets for k in range(length)]
    hops = {
        offset: sum(min(k, length - k) for k, length in zip(offset, lengths)) for offset in offsets
    }
    return sorted((offset for offset in offsets if any(offset)), key=lambda o: (-hops[o], o))


X_ORDER = far_first(8, 4)
Y_ORDER = far_first(8, 2)


def roll(value, shift, axis):
    axis = axis % value.ndim
    return pltpu.roll(value, shift % value.shape[axis], axis)


def lane_of(shape):
    return lax.broadcasted_iota(jnp.int32, shape, len(shape) - 1)


def row_of(shape):
    return lax.broadcasted_iota(jnp.int32, shape, len(shape) - 2)


def five(value):
    return jnp.concatenate([value[0:1], value[1:2], value[1:2], value[1:2], value[2:3]])


def primitives(q):
    inv = 1.0 / q[0]
    u, v, w = q[1] * inv, q[2] * inv, q[3] * inv
    p = 0.4 * (q[4] - 0.5 * (q[1] * u + q[2] * v + q[3] * w))
    c2 = 1.4 * p * inv
    return inv, u, v, w, p, c2, c2 * lax.rsqrt(c2)


def up_y(value):
    here, after = value[..., 1:9, :, :], value[..., 2:10, :, :]
    return roll(jnp.where(lane_of(here.shape) < 32, after, here), -32, -1)


def down_y(value):
    before, here = value[..., 0:8, :, :], value[..., 1:9, :, :]
    return roll(jnp.where(lane_of(here.shape) >= 96, before, here), 32, -1)


def z_difference(value):
    z = lane_of(value.shape) & 31
    after = jnp.where(z == 31, roll(value, 31, -1), roll(value, -1, -1))
    before = jnp.where(z == 0, roll(value, -31, -1), roll(value, 1, -1))
    return after - before


def yz_part(q):
    inv, u, v, w, p, c2, c = primitives(q)
    flux = jnp.stack([q[2], q[1] * v, q[2] * v + p, q[3] * v, v * (q[4] + p)])
    smooth = 400.0 * q
    flux = 0.25 * flux
    inner, wi, pi = q[:, 1:9], w[1:9], p[1:9]
    flux_z = jnp.stack(
        [inner[3], inner[1] * wi, inner[2] * wi, inner[3] * wi + pi, wi * (inner[4] + pi)]
    )
    part = up_y(smooth - flux) + down_y(smooth + flux) - 1600.0 * inner
    part = part - 0.25 * z_difference(flux_z)
    speeds = jnp.stack([v, c])
    return part, jnp.concatenate([down_y(speeds), up_y(speeds)])


def x_part(q, prim):
    inv, u, v, w, p, c2, c = prim
    flux = jnp.stack([q[1], q[1] * u + p, q[2] * u, q[3] * u, u * (q[4] + p)])
    smooth = 400.0 * q
    flux = 0.25 * flux
    return (smooth - flux)[:, 2:10] + (smooth + flux)[:, 0:8]


def x_right(res, prim):
    inv, u, v, w, p, c2, c = prim
    kinetic = 0.5 * (u * u + v * v + w * w)
    dp = 0.4 * (res[4] - u * res[1] - v * res[2] - w * res[3] + kinetic * res[0])
    normal = c * (res[1] - u * res[0])
    return jnp.stack(
        [
            dp - normal,
            c2 * res[0] - dp,
            (res[2] - v * res[0]) * inv,
            (res[3] - w * res[0]) * inv,
            dp + normal,
        ]
    )


def eliminate(lower, upper, main_first, main_last):
    n = len(lower)
    m = [1.0 / main_first]
    g = [upper[0] * m[0]]
    p = [-lower[0] * m[0]]
    for k in range(1, n - 1):
        m.append(1.0 / (MAIN - lower[k] * g[k - 1]))
        g.append(upper[k] * m[k])
        p.append(-(lower[k] * p[k - 1]) * m[k])
    q = [None] * (n - 1)
    q[n - 2] = -g[n - 2]
    for k in range(n - 3, -1, -1):
        p[k] = p[k] - g[k] * p[k + 1]
        q[k] = -(g[k] * q[k + 1])
    last = 1.0 / (main_last + lower[n - 1] * q[n - 2])
    m.append(last)
    own = (-(lower[n - 1] * p[n - 2]) * last, -upper[n - 1] * last, p[0], q[0])
    return m, g, p, q, own


def eliminate_right(right, lower, m, g):
    n = len(right)
    d = [right[0] * five(m[0])]
    for k in range(1, n - 1):
        d.append((right[k] - five(lower[k]) * d[k - 1]) * five(m[k]))
    for k in range(n - 3, -1, -1):
        d[k] = d[k] - five(g[k]) * d[k + 1]
    last = (right[n - 1] - five(lower[n - 1]) * d[n - 2]) * five(m[n - 1])
    return d, last


def put_back(d, p, q, before, own):
    cells = [d[k] + five(p[k]) * before + five(q[k]) * own for k in range(len(d))]
    return cells + [own]


def factor(own):
    to_before, to_after, first_before, first_own = own
    rows = to_before.shape[-2]
    den = 1.0 / (1.0 - to_after * roll(first_before, -1, -2))
    a = to_before * den
    c = to_after * roll(first_own, -1, -2) * den
    return den, to_after * den, a, c


def factor_levels(a, c):
    rows = a.shape[-2]
    levels = []
    step = 1
    while step < rows:
        dn = 1.0 / (1.0 - a * roll(c, step, -2) - c * roll(a, -step, -2))
        an, cn = a * dn, c * dn
        levels.append((dn, an, cn))
        a, c = an * roll(a, step, -2), cn * roll(c, -step, -2)
        step *= 2
    return levels


def reduce_levels(d, levels):
    step = 1
    for dn, an, cn in levels:
        d = dn * d + an * roll(d, step, -2) + cn * roll(d, -step, -2)
        step *= 2
    return d


def y_right(s, rc, half_rc_inv):
    dp = 0.5 * (s[0] + s[4])
    normal = rc * s[2]
    return jnp.stack([dp - normal, s[1], (s[4] - s[0]) * half_rc_inv, s[3], dp + normal])


def swap_groups(value):
    lead = value.shape[:-3]
    half = value.reshape(*lead, 2, 2, 2, 8, 128)
    a, b = half[..., 0, :, :, :], half[..., 1, :, :, :]
    low = (lane_of(a.shape) & 64) == 0
    a, b = jnp.where(low, a, roll(b, 64, -1)), jnp.where(low, roll(a, 64, -1), b)
    half = jnp.stack([a, b], axis=len(lead) + 1)
    a, b = half[..., 0, :, :], half[..., 1, :, :]
    low = (lane_of(a.shape) & 32) == 0
    a, b = jnp.where(low, a, roll(b, 32, -1)), jnp.where(low, roll(a, -32, -1), b)
    half = jnp.stack([a, b], axis=len(lead) + 2)
    return half.reshape(*lead, 8, 8, 128)


def y_bands(speeds):
    vm, cm, vp, cp = (speeds[i].reshape(2, 4, 8, 128) for i in range(4))
    low = jnp.stack([vm - cm, vm, vm + cm])
    high = jnp.stack([vp - cp, vp, vp + cp])
    lower = [-0.25 * low[:, :, k] - 400.0 for k in range(4)]
    upper = [0.25 * high[:, :, k] - 400.0 for k in range(4)]
    return lower, upper


def y_join(own):
    row = row_of(own[0].shape)
    den, high, a, c = factor(own)
    p = jnp.where(row == 0, a, 0.0)
    q = jnp.where(row == 7, 1.0, 0.0)
    a = jnp.where((row == 0) | (row == 7), 0.0, a)
    c = jnp.where(row == 7, 0.0, c)
    levels = factor_levels(a, c)
    p = reduce_levels(p, levels)
    q = reduce_levels(q, levels)
    last = 1.0 / (1.0 - own[0] * roll(q, 1, -2))
    joined = (
        own[0] * roll(p, 1, -2) * last,
        own[1] * last,
        own[2] + own[3] * p,
        own[3] * q,
    )
    return den, high, levels, p, q, last, joined


def y_join_right(d0, last_right, own, den, high, levels, last):
    row = row_of(last_right.shape)
    d = five(den) * last_right + five(high) * roll(d0, -1, -2)
    d = jnp.where(row == 7, 0.0, d)
    d = reduce_levels(d, [tuple(five(part) for part in level) for level in levels])
    joined_last = (last_right + five(own[0]) * roll(d, 1, -2)) * five(last)
    joined_first = d0 + five(own[3]) * d
    return d, joined_last, joined_first


def y_weights(segments):
    n = len(segments)
    ones = jnp.ones_like(segments[0][0])
    zero = jnp.zeros_like(ones)
    den, high, a, c = [], [], [], []
    for j, (to_before, to_after, _, _) in enumerate(segments):
        after = segments[j + 1] if j < n - 1 else (zero,) * 4
        den.append(1.0 / (1.0 - to_after * after[2]))
        high.append(to_after * den[j])
        a.append(to_before * den[j])
        c.append(high[j] * after[3])
    left, right = [None] * n, [None] * n
    for j in range(n):
        left[j] = c[j] / (1.0 - a[j] * left[j - 1]) if j else c[j]
    for j in range(n - 1, -1, -1):
        right[j] = a[j] / (1.0 - c[j] * right[j + 1]) if j < n - 1 else a[j]
    gain = []
    for j in range(n):
        rest = ones
        rest = rest - a[j] * left[j - 1] if j else rest
        rest = rest - c[j] * right[j + 1] if j < n - 1 else rest
        gain.append(1.0 / rest)
    down, up = [ones] * n, [ones] * n
    for j in range(1, n):
        down[j] = down[j - 1] * right[j]
    for j in range(n - 2, -1, -1):
        up[j] = up[j + 1] * left[j]
    weights = []
    for j in range(n):
        own_last = gain[j] * den[j]
        own_first = right[j] * gain[j - 1] * high[j - 1] if j else zero
        before_last = left[j - 1] * own_last if j else zero
        before_first = gain[j - 1] * high[j - 1] if j else zero
        down_inv = 1.0 / down[j]
        up_inv = 1.0 / up[j - 1] if j else ones
        weights.append(
            (
                own_last,
                own_first,
                before_last,
                before_first,
                down_inv,
                up_inv,
                down[j - 1] if j else zero,
                up[j],
                right[j],
                left[j - 1] if j else zero,
            )
        )
    return weights


def y_emit(last, first, w):
    own = w[0] * last + w[1] * first
    before = w[2] * last + w[3] * first
    return own, before, own * w[4], before * w[5]


def y_meet(below, above, own, before, w):
    low, high = w[6] * below, w[7] * above
    return low + w[9] * high + before, w[8] * low + own + high


def increments(s, prim, r, half_rc_inv, c2_inv):
    inv, u, v, w, p, c2, c = prim
    dp = 0.5 * (s[0] + s[4])
    dv = (s[4] - s[0]) * half_rc_inv
    dr = (s[1] + dp) * c2_inv
    du, dw = s[2], s[3]
    kinetic = 0.5 * (u * u + v * v + w * w)
    return (
        dr,
        u * dr + r * du,
        v * dr + r * dv,
        w * dr + r * dw,
        kinetic * dr + r * (u * du + v * dv + w * dw) + 2.5 * dp,
    )


def x_code_mask(codes, side):
    ones = (codes[side : side + 1] == 1).astype(jnp.float32)
    spread = jnp.where((lane_of((8, 32)) >> 2) == row_of((8, 32)), ones, 0.0)
    place = jnp.where((row_of((32, 128)) & 3) == (lane_of((32, 128)) >> 5), 1.0, 0.0)
    return jnp.dot(spread, place, preferred_element_type=jnp.float32) > 0.5


def y_code_mask(codes, side):
    ones = jnp.broadcast_to((codes[side : side + 1] == 1).astype(jnp.float32), (8, 8))
    halves = []
    for h in range(2):
        place = jnp.where(row_of((8, 128)) == 4 * h + (lane_of((8, 128)) >> 5), 1.0, 0.0)
        halves.append(jnp.dot(ones, place, preferred_element_type=jnp.float32))
    return jnp.stack(halves) > 0.5


def x_bands(u, c, codes, start, end):
    lam = jnp.stack([u - c, u, u + c])
    lower = [-0.25 * lam[:, k] - 400.0 for k in range(8)]
    upper = [0.25 * lam[:, k + 2] - 400.0 for k in range(8)]
    first = MAIN + jnp.where(x_code_mask(codes, 0)[None] & start, lower[0], 0.0)
    last = MAIN + jnp.where(x_code_mask(codes, 1)[None] & end, upper[7], 0.0)
    lower[0] = jnp.where(start, 0.0, lower[0])
    upper[7] = jnp.where(end, 0.0, upper[7])
    return lower, upper, first, last


def y_ends(lower, upper, codes, start, end):
    row = row_of(lower[0].shape)
    at_start = (row == 0) & start
    at_end = (row == 7) & end
    first = MAIN + jnp.where(at_start & y_code_mask(codes, 0)[None], lower[0], 0.0)
    last = MAIN + jnp.where(at_end & y_code_mask(codes, 1)[None], upper[3], 0.0)
    lower, upper = list(lower), list(upper)
    lower[0] = jnp.where(at_start, 0.0, lower[0])
    upper[3] = jnp.where(at_end, 0.0, upper[3])
    return lower, upper, first, last


def wait_all(ref, sem):
    pltpu.make_async_copy(ref, ref, sem).wait()


def kernel(
    flow,
    x_codes,
    y_codes,
    out,
    q_sc,
    part_sc,
    speed_sc,
    x_send,
    x_low,
    x_high,
    y_low,
    y_high,
    xm_out,
    xr_out,
    xm_in,
    xr_in,
    xs_out,
    xs_in,
    ym_out,
    ym_in,
    y_weight_sc,
    y_weight,
    yr_sc,
    yf_out,
    yf_in,
    ys_sc,
    x_code_sc,
    y_code_sc,
    in_sem,
    code_sem,
    halo_send,
    halo_recv,
    send_sem,
    recv_sem,
):
    gx, gy = lax.axis_index("gx"), lax.axis_index("gy")
    start_x, end_x = gx == 0, gx == SX - 1
    start_y, end_y = gy == 0, gy == SY - 1

    for b in range(8):
        pltpu.make_async_copy(
            flow.at[:, :, pl.ds(128 * b, 128)], q_sc.at[:, pl.ds(8 * b, 8), :], in_sem
        ).start()
    code_copies = [
        pltpu.make_async_copy(x_codes, x_code_sc, code_sem.at[0]),
        pltpu.make_async_copy(y_codes, y_code_sc, code_sem.at[1]),
    ]
    for copy in code_copies:
        copy.start()

    barrier = pltpu.get_barrier_semaphore()

    def greet_x(k, carry):
        pl.semaphore_signal(
            barrier, inc=1, device_id=(lax.rem(gx + k, SX), gy), device_id_type=MESH
        )
        return carry

    def greet_y(k, carry):
        pl.semaphore_signal(
            barrier, inc=1, device_id=(gx, lax.rem(gy + k, SY)), device_id_type=MESH
        )
        return carry

    lax.fori_loop(1, SX, greet_x, 0)
    lax.fori_loop(1, SY, greet_y, 0)
    wait_all(q_sc, in_sem)
    for copy in code_copies:
        copy.wait()

    x_send[0] = q_sc[:, pl.ds(7, 8, stride=8), :]
    x_send[1] = q_sc[:, pl.ds(0, 8, stride=8), :]
    pl.semaphore_wait(barrier, SX + SY - 2)

    x_after, x_before = lax.rem(gx + 1, SX), lax.rem(gx + SX - 1, SX)
    y_after, y_before = lax.rem(gy + 1, SY), lax.rem(gy + SY - 1, SY)
    halos = [
        (x_send.at[0], x_low, (x_after, gy)),
        (x_send.at[1], x_high, (x_before, gy)),
        (q_sc.at[:, pl.ds(56, 8), :], y_low, (gx, y_after)),
        (q_sc.at[:, pl.ds(0, 8), :], y_high, (gx, y_before)),
    ]
    copies = []
    for i, (source, target, device) in enumerate(halos):
        copy = pltpu.make_async_remote_copy(
            src_ref=source,
            dst_ref=target,
            send_sem=halo_send.at[i],
            recv_sem=halo_recv.at[i],
            device_id=device,
            device_id_type=MESH,
        )
        copy.start()
        copies.append(copy)

    def send_x(source, target, slot):
        mine = pl.ds(gx * 4, 4)
        pltpu.make_async_copy(source.at[mine], target.at[mine], recv_sem.at[slot]).start()

        for dy, dx in X_ORDER:
            other = 4 * lax.rem(lax.div(gx, 4) + dy, 8) + lax.rem(lax.rem(gx, 4) + dx, 4)
            pltpu.make_async_remote_copy(
                src_ref=source.at[pl.ds(other * 4, 4)],
                dst_ref=target.at[mine],
                send_sem=send_sem.at[slot],
                recv_sem=recv_sem.at[slot],
                device_id=(other, gy),
                device_id_type=MESH,
            ).start()

    def others_y():
        for dz, dc in Y_ORDER:
            yield 2 * lax.rem(lax.div(gy, 2) + dz, 8) + lax.rem(lax.rem(gy, 2) + dc, 2)

    for copy in copies:
        copy.wait_recv()
    inner = [q_sc[:, pl.ds(k, 8, stride=8), :] for k in range(8)]
    low = jnp.where(start_x, inner[0], x_low[...])
    high = jnp.where(end_x, inner[7], x_high[...])
    q = jnp.stack([low] + inner + [high], axis=1)
    prim_all = primitives(q)

    lower, upper, first, last = x_bands(prim_all[1], prim_all[6], x_code_sc[...], start_x, end_x)
    xm, xg, xp, xq, x_own = eliminate(lower, upper, first, last)
    for group, (matrix, families) in enumerate(GROUPS):
        for row in range(4):
            xm_out[pl.ds(group * 32 + row, 8, stride=4), :] = x_own[row][matrix]
    send_x(xm_out, xm_in, 0)

    blocks = q_sc[...].reshape(5, 8, 8, 128)
    y_edge_low = jnp.where(start_y, roll(blocks[:, 0], 96, -1), y_low[...])
    y_edge_high = jnp.where(end_y, roll(blocks[:, 7], 32, -1), y_high[...])
    part, speeds = yz_part(
        jnp.concatenate([y_edge_low[:, None], blocks, y_edge_high[:, None]], axis=1)
    )
    part_sc[...] = part.reshape(5, 64, 128)
    speed_sc[...] = speeds.reshape(4, 64, 128)
    prim = tuple(value[1:9] for value in prim_all)
    residual = x_part(q, prim_all) + jnp.stack(
        [part_sc[:, pl.ds(k, 8, stride=8), :] for k in range(8)], axis=1
    )
    right = x_right(residual, prim)
    xd, x_last = eliminate_right([right[:, k] for k in range(8)], lower, xm, xg)
    zero = jnp.zeros((8, 128), jnp.float32)
    for group, (matrix, families) in enumerate(GROUPS):
        for i in range(2):
            at = group * 32 + 2 * i
            some = i < len(families)
            xr_out[pl.ds(at, 8, stride=4), :] = x_last[families[i]] if some else zero
            xr_out[pl.ds(at + 1, 8, stride=4), :] = xd[0][families[i]] if some else zero
    send_x(xr_out, xr_in, 1)

    speeds = jnp.stack([speed_sc[:, pl.ds(k, 8, stride=8), :] for k in range(8)], axis=1)
    y_lower, y_upper = y_bands(swap_groups(speeds))
    y_lower, y_upper, first, last = y_ends(y_lower, y_upper, y_code_sc[...], start_y, end_y)
    ym, yg, yp, yq, y_own = eliminate(y_lower, y_upper, first, last)
    y_den, y_high_part, y_lev, y_p, y_q, y_joint, joined = y_join(y_own)
    ym_out[...] = jnp.zeros((32, 128), jnp.float32)
    for kind in range(4):
        line = 7 if kind < 2 else 0
        for matrix in range(3):
            for h in range(2):
                at = kind * 8 + matrix * 2 + h
                ym_out[pl.ds(at, 1), :] = joined[kind][matrix, h, line : line + 1]
    pltpu.make_async_copy(ym_out, ym_in.at[gy], recv_sem.at[3]).start()
    for other in others_y():
        pltpu.make_async_remote_copy(
            src_ref=ym_out,
            dst_ref=ym_in.at[gy],
            send_sem=send_sem.at[3],
            recv_sem=recv_sem.at[3],
            device_id=(gx, other),
            device_id_type=MESH,
        ).start()

    wait_all(xm_in, recv_sem.at[0])
    den, high_part, a, c = factor([xm_in[pl.ds(row, SX, stride=4), :] for row in range(4)])
    levels = factor_levels(a, c)
    wait_all(xr_in, recv_sem.at[1])
    for i in range(2):
        own_last = xr_in[pl.ds(2 * i, SX, stride=4), :]
        own_first = xr_in[pl.ds(2 * i + 1, SX, stride=4), :]
        d = den * own_last + high_part * roll(own_first, -1, 0)
        d = reduce_levels(d, levels)
        xs_out[pl.ds(2 * i, SX, stride=4), :] = roll(d, 1, 0)
        xs_out[pl.ds(2 * i + 1, SX, stride=4), :] = d
    send_x(xs_out, xs_in, 2)

    wait_all(ym_in, recv_sem.at[3])
    segments = [
        tuple(ym_in[j, pl.ds(8 * kind, 8), :] for kind in range(4)) for j in range(SY)
    ]
    for j, weights in enumerate(y_weights(segments)):
        for i, weight in enumerate(weights):
            y_weight_sc[j, i] = weight
    for i in range(10):
        for family, matrix in enumerate((0, 1, 1, 1, 2)):
            y_weight[i, pl.ds(2 * family, 2), :] = y_weight_sc[gy, i, pl.ds(2 * matrix, 2), :]

    r = q[0, 1:9]
    rc = r * prim[6]
    half_rc_inv = 0.5 / rc
    c2_inv = 1.0 / prim[5]

    wait_all(xs_in, recv_sem.at[2])

    def x_value(kind):
        rows = []
        for group, i in ((0, 0), (2, 0), (2, 1), (3, 0), (1, 0)):
            rows.append(xs_in[pl.ds(group * 32 + 2 * i + kind, 8, stride=4), :])
        return jnp.stack(rows)

    solved = jnp.stack(put_back(xd, xp, xq, x_value(0), x_value(1)), axis=1)
    right = swap_groups(y_right(solved, rc, half_rc_inv)).reshape(5, 2, 4, 8, 128)
    yd, y_last = eliminate_right([right[:, :, k] for k in range(4)], y_lower, ym, yg)
    y_d, joined_last, joined_first = y_join_right(
        yd[0], y_last, y_own, y_den, y_high_part, y_lev, y_joint
    )
    for family in range(5):
        for h in range(2):
            yr_sc[0, pl.ds(2 * family + h, 1), :] = joined_last[family, h, 7:8]
            yr_sc[1, pl.ds(2 * family + h, 1), :] = joined_first[family, h, 0:1]
    weights = [y_weight[i] for i in range(10)]
    own_add, before_add, own_out, before_out = y_emit(yr_sc[0], yr_sc[1], weights)
    yf_out[0], yf_out[1] = own_out, before_out
    for other in others_y():
        pltpu.make_async_remote_copy(
            src_ref=yf_out.at[jnp.where(other < gy, 1, 0), pl.ds(0, 10)],
            dst_ref=yf_in.at[gy, pl.ds(0, 10)],
            send_sem=send_sem.at[4],
            recv_sem=recv_sem.at[4],
            device_id=(gx, other),
            device_id_type=MESH,
        ).start()
    wait_all(yf_in.at[pl.ds(0, SY - 1), pl.ds(0, 10)], recv_sem.at[4])
    zero = jnp.zeros((16, 128), jnp.float32)
    below = sum((jnp.where(j < gy, yf_in[j], 0.0) for j in range(SY - 1)), zero)
    above = sum((jnp.where(j > gy, yf_in[j], 0.0) for j in range(1, SY)), zero)
    ys_sc[0], ys_sc[1] = y_meet(below, above, own_add, before_add, weights)

    def y_value(kind):
        return jnp.stack(
            [
                jnp.stack([ys_sc[kind, pl.ds(2 * family + h, 1), :] for h in range(2)])
                for family in range(5)
            ]
        )

    before, own = y_value(0), y_value(1)
    groups = y_d + five(y_p) * before + five(y_q) * own
    previous = jnp.where(row_of(groups.shape) == 0, before, roll(groups, 1, -2))
    solved = jnp.stack(put_back(yd, yp, yq, previous, groups), axis=2)
    solved = swap_groups(solved.reshape(5, 8, 8, 128))
    for field, value in enumerate(increments(solved, prim, r, half_rc_inv, c2_inv)):
        for k in range(8):
            out[field, pl.ds(k, 8, stride=8), :] = value[k]

    for copy in copies:
        copy.wait_send()
    for slot in range(3):
        wait_all(xm_out.at[pl.ds(0, 4 * (SX - 1))], send_sem.at[slot])
    wait_all(ym_in.at[pl.ds(0, SY - 1)], send_sem.at[3])
    wait_all(yf_in.at[pl.ds(0, SY - 1), pl.ds(0, 10)], send_sem.at[4])


def local(flow_state, x_codes, y_codes):
    f32 = jnp.float32

    def vmem(*shape):
        return pltpu.VMEM(shape, f32)

    result = pl.pallas_call(
        kernel,
        out_shape=jax.ShapeDtypeStruct((5, 64, 128), f32),
        in_specs=[pl.BlockSpec(memory_space=pltpu.HBM)] * 3,
        out_specs=pl.BlockSpec(memory_space=pltpu.VMEM),
        scratch_shapes=[
            vmem(5, 64, 128),
            vmem(5, 64, 128),
            vmem(4, 64, 128),
            vmem(2, 5, 8, 128),
            vmem(5, 8, 128),
            vmem(5, 8, 128),
            vmem(5, 8, 128),
            vmem(5, 8, 128),
            vmem(4 * SX, 128),
            vmem(4 * SX, 128),
            vmem(4 * SX, 128),
            vmem(4 * SX, 128),
            vmem(4 * SX, 128),
            vmem(4 * SX, 128),
            vmem(32, 128),
            vmem(SY, 32, 128),
            vmem(SY, 10, 8, 128),
            vmem(10, 16, 128),
            vmem(2, 16, 128),
            vmem(2, 16, 128),
            vmem(SY, 16, 128),
            vmem(2, 16, 128),
            pltpu.VMEM((2, 32), jnp.int32),
            pltpu.VMEM((2, 8), jnp.int32),
            pltpu.SemaphoreType.DMA,
            pltpu.SemaphoreType.DMA((2,)),
            pltpu.SemaphoreType.DMA((4,)),
            pltpu.SemaphoreType.DMA((4,)),
            pltpu.SemaphoreType.DMA((5,)),
            pltpu.SemaphoreType.DMA((5,)),
        ],
        compiler_params=pltpu.CompilerParams(
            collective_id=0, has_side_effects=True, vmem_limit_bytes=VMEM_LIMIT
        ),
        name="step",
    )(flow_state, x_codes, y_codes)
    result = jnp.transpose(result.reshape(5, 8, 8, 128), (0, 2, 1, 3))
    return result.reshape(flow_state.shape)


def solution(mesh):
    return jax.shard_map(
        local,
        mesh=mesh,
        in_specs=(P(None, "gx", "gy"), P(None, "gy"), P(None, "gx")),
        out_specs=P(None, "gx", "gy"),
        check_vma=False,
    )
```

```python
import functools

import jax
import jax.numpy as jnp
from jax import lax
from jax.experimental import pallas as pl
from jax.experimental.pallas import tpu as pltpu
from jax.sharding import PartitionSpec as P

NZ = 32
SX = 32
SY = 16
VMEM_LIMIT = 56 * 1024 * 1024
MAIN = 801.0
GROUPS = ((0, (0,)), (2, (4,)), (1, (1, 2)), (1, (3,)))
MESH = pl.DeviceIdType.MESH


def far_first(*lengths):
    offsets = [()]
    for length in lengths:
        offsets = [(*offset, k) for offset in offsets for k in range(length)]
    hops = {
        offset: sum(min(k, length - k) for k, length in zip(offset, lengths)) for offset in offsets
    }
    return sorted((offset for offset in offsets if any(offset)), key=lambda o: (-hops[o], o))


X_ORDER = far_first(8, 4)
Y_ORDER = far_first(8, 2)


def roll(value, shift, axis):
    axis = axis % value.ndim
    return pltpu.roll(value, shift % value.shape[axis], axis)


def lane_of(shape):
    return lax.broadcasted_iota(jnp.int32, shape, len(shape) - 1)


def row_of(shape):
    return lax.broadcasted_iota(jnp.int32, shape, len(shape) - 2)


def five(value):
    return jnp.concatenate([value[0:1], value[1:2], value[1:2], value[1:2], value[2:3]])


def primitives(q):
    inv = 1.0 / q[0]
    u, v, w = q[1] * inv, q[2] * inv, q[3] * inv
    p = 0.4 * (q[4] - 0.5 * (q[1] * u + q[2] * v + q[3] * w))
    c2 = 1.4 * p * inv
    return inv, u, v, w, p, c2, c2 * lax.rsqrt(c2)


def up_y(value):
    here, after = value[..., 1:9, :, :], value[..., 2:10, :, :]
    return roll(jnp.where(lane_of(here.shape) < 32, after, here), -32, -1)


def down_y(value):
    before, here = value[..., 0:8, :, :], value[..., 1:9, :, :]
    return roll(jnp.where(lane_of(here.shape) >= 96, before, here), 32, -1)


def z_difference(value):
    z = lane_of(value.shape) & 31
    after = jnp.where(z == 31, roll(value, 31, -1), roll(value, -1, -1))
    before = jnp.where(z == 0, roll(value, -31, -1), roll(value, 1, -1))
    return after - before


def yz_part(q):
    inv, u, v, w, p, c2, c = primitives(q)
    flux = jnp.stack([q[2], q[1] * v, q[2] * v + p, q[3] * v, v * (q[4] + p)])
    smooth = 400.0 * q
    flux = 0.25 * flux
    inner, wi, pi = q[:, 1:9], w[1:9], p[1:9]
    flux_z = jnp.stack(
        [inner[3], inner[1] * wi, inner[2] * wi, inner[3] * wi + pi, wi * (inner[4] + pi)]
    )
    part = up_y(smooth - flux) + down_y(smooth + flux) - 1600.0 * inner
    part = part - 0.25 * z_difference(flux_z)
    speeds = jnp.stack([v, c])
    return part, jnp.concatenate([down_y(speeds), up_y(speeds)])


def x_part(q, prim):
    inv, u, v, w, p, c2, c = prim
    flux = jnp.stack([q[1], q[1] * u + p, q[2] * u, q[3] * u, u * (q[4] + p)])
    smooth = 400.0 * q
    flux = 0.25 * flux
    return (smooth - flux)[:, 2:10] + (smooth + flux)[:, 0:8]


def x_right(res, prim):
    inv, u, v, w, p, c2, c = prim
    kinetic = 0.5 * (u * u + v * v + w * w)
    dp = 0.4 * (res[4] - u * res[1] - v * res[2] - w * res[3] + kinetic * res[0])
    normal = c * (res[1] - u * res[0])
    return jnp.stack(
        [
            dp - normal,
            c2 * res[0] - dp,
            (res[2] - v * res[0]) * inv,
            (res[3] - w * res[0]) * inv,
            dp + normal,
        ]
    )


def eliminate(lower, upper, main_first, main_last):
    n = len(lower)
    m = [1.0 / main_first]
    g = [upper[0] * m[0]]
    p = [-lower[0] * m[0]]
    for k in range(1, n - 1):
        m.append(1.0 / (MAIN - lower[k] * g[k - 1]))
        g.append(upper[k] * m[k])
        p.append(-(lower[k] * p[k - 1]) * m[k])
    q = [None] * (n - 1)
    q[n - 2] = -g[n - 2]
    for k in range(n - 3, -1, -1):
        p[k] = p[k] - g[k] * p[k + 1]
        q[k] = -(g[k] * q[k + 1])
    last = 1.0 / (main_last + lower[n - 1] * q[n - 2])
    m.append(last)
    own = (-(lower[n - 1] * p[n - 2]) * last, -upper[n - 1] * last, p[0], q[0])
    return m, g, p, q, own


def eliminate_right(right, lower, m, g):
    n = len(right)
    d = [right[0] * five(m[0])]
    for k in range(1, n - 1):
        d.append((right[k] - five(lower[k]) * d[k - 1]) * five(m[k]))
    for k in range(n - 3, -1, -1):
        d[k] = d[k] - five(g[k]) * d[k + 1]
    last = (right[n - 1] - five(lower[n - 1]) * d[n - 2]) * five(m[n - 1])
    return d, last


def put_back(d, p, q, before, own):
    cells = [d[k] + five(p[k]) * before + five(q[k]) * own for k in range(len(d))]
    return cells + [own]


def factor(own):
    to_before, to_after, first_before, first_own = own
    rows = to_before.shape[-2]
    den = 1.0 / (1.0 - to_after * roll(first_before, -1, -2))
    a = to_before * den
    c = to_after * roll(first_own, -1, -2) * den
    return den, to_after * den, a, c


def factor_levels(a, c):
    rows = a.shape[-2]
    levels = []
    step = 1
    while step < rows:
        dn = 1.0 / (1.0 - a * roll(c, step, -2) - c * roll(a, -step, -2))
        an, cn = a * dn, c * dn
        levels.append((dn, an, cn))
        a, c = an * roll(a, step, -2), cn * roll(c, -step, -2)
        step *= 2
    return levels


def reduce_levels(d, levels):
    step = 1
    for dn, an, cn in levels:
        d = dn * d + an * roll(d, step, -2) + cn * roll(d, -step, -2)
        step *= 2
    return d


def y_right(s, rc, half_rc_inv):
    dp = 0.5 * (s[0] + s[4])
    normal = rc * s[2]
    return jnp.stack([dp - normal, s[1], (s[4] - s[0]) * half_rc_inv, s[3], dp + normal])


def swap_groups(value):
    lead = value.shape[:-3]
    half = value.reshape(*lead, 2, 2, 2, 8, 128)
    a, b = half[..., 0, :, :, :], half[..., 1, :, :, :]
    low = (lane_of(a.shape) & 64) == 0
    a, b = jnp.where(low, a, roll(b, 64, -1)), jnp.where(low, roll(a, 64, -1), b)
    half = jnp.stack([a, b], axis=len(lead) + 1)
    a, b = half[..., 0, :, :], half[..., 1, :, :]
    low = (lane_of(a.shape) & 32) == 0
    a, b = jnp.where(low, a, roll(b, 32, -1)), jnp.where(low, roll(a, -32, -1), b)
    half = jnp.stack([a, b], axis=len(lead) + 2)
    return half.reshape(*lead, 8, 8, 128)


def y_bands(speeds):
    vm, cm, vp, cp = (speeds[i].reshape(2, 4, 8, 128) for i in range(4))
    low = jnp.stack([vm - cm, vm, vm + cm])
    high = jnp.stack([vp - cp, vp, vp + cp])
    lower = [-0.25 * low[:, :, k] - 400.0 for k in range(4)]
    upper = [0.25 * high[:, :, k] - 400.0 for k in range(4)]
    return lower, upper


def y_join(own):
    row = row_of(own[0].shape)
    den, high, a, c = factor(own)
    p = jnp.where(row == 0, a, 0.0)
    q = jnp.where(row == 7, 1.0, 0.0)
    a = jnp.where((row == 0) | (row == 7), 0.0, a)
    c = jnp.where(row == 7, 0.0, c)
    levels = factor_levels(a, c)
    p = reduce_levels(p, levels)
    q = reduce_levels(q, levels)
    last = 1.0 / (1.0 - own[0] * roll(q, 1, -2))
    joined = (
        own[0] * roll(p, 1, -2) * last,
        own[1] * last,
        own[2] + own[3] * p,
        own[3] * q,
    )
    return den, high, levels, p, q, last, joined


def y_join_right(d0, last_right, own, den, high, levels, last):
    row = row_of(last_right.shape)
    d = five(den) * last_right + five(high) * roll(d0, -1, -2)
    d = jnp.where(row == 7, 0.0, d)
    d = reduce_levels(d, [tuple(five(part) for part in level) for level in levels])
    joined_last = (last_right + five(own[0]) * roll(d, 1, -2)) * five(last)
    joined_first = d0 + five(own[3]) * d
    return d, joined_last, joined_first


def y_weights(segments):
    n = len(segments)
    ones = jnp.ones_like(segments[0][0])
    zero = jnp.zeros_like(ones)
    den, high, a, c = [], [], [], []
    for j, (to_before, to_after, _, _) in enumerate(segments):
        after = segments[j + 1] if j < n - 1 else (zero,) * 4
        den.append(1.0 / (1.0 - to_after * after[2]))
        high.append(to_after * den[j])
        a.append(to_before * den[j])
        c.append(high[j] * after[3])
    left, right = [None] * n, [None] * n
    for j in range(n):
        left[j] = c[j] / (1.0 - a[j] * left[j - 1]) if j else c[j]
    for j in range(n - 1, -1, -1):
        right[j] = a[j] / (1.0 - c[j] * right[j + 1]) if j < n - 1 else a[j]
    gain = []
    for j in range(n):
        rest = ones
        rest = rest - a[j] * left[j - 1] if j else rest
        rest = rest - c[j] * right[j + 1] if j < n - 1 else rest
        gain.append(1.0 / rest)
    down, up = [ones] * n, [ones] * n
    for j in range(1, n):
        down[j] = down[j - 1] * right[j]
    for j in range(n - 2, -1, -1):
        up[j] = up[j + 1] * left[j]
    weights = []
    for j in range(n):
        own_last = gain[j] * den[j]
        own_first = right[j] * gain[j - 1] * high[j - 1] if j else zero
        before_last = left[j - 1] * own_last if j else zero
        before_first = gain[j - 1] * high[j - 1] if j else zero
        down_inv = 1.0 / down[j]
        up_inv = 1.0 / up[j - 1] if j else ones
        weights.append(
            (
                own_last,
                own_first,
                before_last,
                before_first,
                down_inv,
                up_inv,
                down[j - 1] if j else zero,
                up[j],
                right[j],
                left[j - 1] if j else zero,
            )
        )
    return weights


def y_emit(last, first, w):
    own = w[0] * last + w[1] * first
    before = w[2] * last + w[3] * first
    return own, before, own * w[4], before * w[5]


def y_meet(below, above, own, before, w):
    low, high = w[6] * below, w[7] * above
    return low + w[9] * high + before, w[8] * low + own + high


def increments(s, prim, r, half_rc_inv, c2_inv):
    inv, u, v, w, p, c2, c = prim
    dp = 0.5 * (s[0] + s[4])
    dv = (s[4] - s[0]) * half_rc_inv
    dr = (s[1] + dp) * c2_inv
    du, dw = s[2], s[3]
    kinetic = 0.5 * (u * u + v * v + w * w)
    return (
        dr,
        u * dr + r * du,
        v * dr + r * dv,
        w * dr + r * dw,
        kinetic * dr + r * (u * du + v * dv + w * dw) + 2.5 * dp,
    )


def x_code_mask(codes, side):
    ones = (codes[side : side + 1] == 1).astype(jnp.float32)
    spread = jnp.where((lane_of((8, 32)) >> 2) == row_of((8, 32)), ones, 0.0)
    place = jnp.where((row_of((32, 128)) & 3) == (lane_of((32, 128)) >> 5), 1.0, 0.0)
    return jnp.dot(spread, place, preferred_element_type=jnp.float32) > 0.5


def y_code_mask(codes, side):
    ones = jnp.broadcast_to((codes[side : side + 1] == 1).astype(jnp.float32), (8, 8))
    halves = []
    for h in range(2):
        place = jnp.where(row_of((8, 128)) == 4 * h + (lane_of((8, 128)) >> 5), 1.0, 0.0)
        halves.append(jnp.dot(ones, place, preferred_element_type=jnp.float32))
    return jnp.stack(halves) > 0.5


def x_bands(u, c, codes, start, end):
    lam = jnp.stack([u - c, u, u + c])
    lower = [-0.25 * lam[:, k] - 400.0 for k in range(8)]
    upper = [0.25 * lam[:, k + 2] - 400.0 for k in range(8)]
    first = MAIN + jnp.where(x_code_mask(codes, 0)[None] & start, lower[0], 0.0)
    last = MAIN + jnp.where(x_code_mask(codes, 1)[None] & end, upper[7], 0.0)
    lower[0] = jnp.where(start, 0.0, lower[0])
    upper[7] = jnp.where(end, 0.0, upper[7])
    return lower, upper, first, last


def y_ends(lower, upper, codes, start, end):
    row = row_of(lower[0].shape)
    at_start = (row == 0) & start
    at_end = (row == 7) & end
    first = MAIN + jnp.where(at_start & y_code_mask(codes, 0)[None], lower[0], 0.0)
    last = MAIN + jnp.where(at_end & y_code_mask(codes, 1)[None], upper[3], 0.0)
    lower, upper = list(lower), list(upper)
    lower[0] = jnp.where(at_start, 0.0, lower[0])
    upper[3] = jnp.where(at_end, 0.0, upper[3])
    return lower, upper, first, last


def wait_all(ref, sem):
    pltpu.make_async_copy(ref, ref, sem).wait()


def kernel(
    flow,
    x_codes,
    y_codes,
    out,
    q_sc,
    part_sc,
    speed_sc,
    x_send,
    x_low,
    x_high,
    y_low,
    y_high,
    xm_out,
    xr_out,
    xm_in,
    xr_in,
    xs_out,
    xs_in,
    ym_out,
    ym_in,
    y_weight_sc,
    y_weight,
    yr_sc,
    yf_out,
    yf_in,
    ys_sc,
    x_code_sc,
    y_code_sc,
    word,
    in_sem,
    code_sem,
    halo_send,
    halo_recv,
    send_sem,
    recv_sem,
):
    gx, gy = lax.axis_index("gx"), lax.axis_index("gy")
    start_x, end_x = gx == 0, gx == SX - 1
    start_y, end_y = gy == 0, gy == SY - 1

    for b in range(8):
        pltpu.make_async_copy(
            flow.at[:, :, pl.ds(128 * b, 128)], q_sc.at[:, pl.ds(8 * b, 8), :], in_sem
        ).start()
    code_copies = [
        pltpu.make_async_copy(x_codes, x_code_sc, code_sem.at[0]),
        pltpu.make_async_copy(y_codes, y_code_sc, code_sem.at[1]),
    ]
    for copy in code_copies:
        copy.start()

    chip_y, chip_x = lax.div(gx, 4), lax.rem(gx, 4)
    chip_z, core = lax.div(gy, 2), lax.rem(gy, 2)
    x_after, x_before = lax.rem(gx + 1, SX), lax.rem(gx + SX - 1, SX)
    y_after, y_before = lax.rem(gy + 1, SY), lax.rem(gy + SY - 1, SY)
    ring = [
        (4 * lax.rem(chip_y + 1, 8) + chip_x, gy),
        (4 * lax.rem(chip_y + 7, 8) + chip_x, gy),
        (gx, 2 * lax.rem(chip_z + 1, 8) + core),
        (gx, 2 * lax.rem(chip_z + 7, 8) + core),
    ]
    near = [(4 * chip_y + lax.rem(chip_x + k, 4), gy) for k in range(1, 4)]
    near += [(gx, 2 * chip_z + 1 - core), (gx, y_after), (gx, y_before)]
    near += [(x_after, gy), (x_before, gy)] + ring
    barrier = pltpu.get_barrier_semaphore()
    for device in near:
        pl.semaphore_signal(barrier, inc=1, device_id=device, device_id_type=MESH)

    def tell(step):
        for device in ring:
            pl.semaphore_signal(word.at[step], inc=1, device_id=device, device_id_type=MESH)

    def heard(step):
        pl.semaphore_wait(word.at[step], len(ring))

    wait_all(q_sc, in_sem)
    for copy in code_copies:
        copy.wait()

    x_send[0] = q_sc[:, pl.ds(7, 8, stride=8), :]
    x_send[1] = q_sc[:, pl.ds(0, 8, stride=8), :]
    pl.semaphore_wait(barrier, len(near))
    halos = [
        (x_send.at[0], x_low, (x_after, gy)),
        (x_send.at[1], x_high, (x_before, gy)),
        (q_sc.at[:, pl.ds(56, 8), :], y_low, (gx, y_after)),
        (q_sc.at[:, pl.ds(0, 8), :], y_high, (gx, y_before)),
    ]
    copies = []
    for i, (source, target, device) in enumerate(halos):
        copy = pltpu.make_async_remote_copy(
            src_ref=source,
            dst_ref=target,
            send_sem=halo_send.at[i],
            recv_sem=halo_recv.at[i],
            device_id=device,
            device_id_type=MESH,
        )
        copy.start()
        copies.append(copy)
    for step in range(3):
        tell(step)
        heard(step)
    tell(3)

    def send_x(source, target, slot):
        mine = pl.ds(gx * 4, 4)
        pltpu.make_async_copy(source.at[mine], target.at[mine], recv_sem.at[slot]).start()

        for dy, dx in X_ORDER:
            other = 4 * lax.rem(lax.div(gx, 4) + dy, 8) + lax.rem(lax.rem(gx, 4) + dx, 4)
            pltpu.make_async_remote_copy(
                src_ref=source.at[pl.ds(other * 4, 4)],
                dst_ref=target.at[mine],
                send_sem=send_sem.at[slot],
                recv_sem=recv_sem.at[slot],
                device_id=(other, gy),
                device_id_type=MESH,
            ).start()

    def others_y():
        for dz, dc in Y_ORDER:
            yield 2 * lax.rem(lax.div(gy, 2) + dz, 8) + lax.rem(lax.rem(gy, 2) + dc, 2)

    for copy in copies:
        copy.wait_recv()
    inner = [q_sc[:, pl.ds(k, 8, stride=8), :] for k in range(8)]
    low = jnp.where(start_x, inner[0], x_low[...])
    high = jnp.where(end_x, inner[7], x_high[...])
    q = jnp.stack([low] + inner + [high], axis=1)
    prim_all = primitives(q)

    lower, upper, first, last = x_bands(prim_all[1], prim_all[6], x_code_sc[...], start_x, end_x)
    xm, xg, xp, xq, x_own = eliminate(lower, upper, first, last)
    for group, (matrix, families) in enumerate(GROUPS):
        for row in range(4):
            xm_out[pl.ds(group * 32 + row, 8, stride=4), :] = x_own[row][matrix]
    heard(3)
    send_x(xm_out, xm_in, 0)

    blocks = q_sc[...].reshape(5, 8, 8, 128)
    y_edge_low = jnp.where(start_y, roll(blocks[:, 0], 96, -1), y_low[...])
    y_edge_high = jnp.where(end_y, roll(blocks[:, 7], 32, -1), y_high[...])
    part, speeds = yz_part(
        jnp.concatenate([y_edge_low[:, None], blocks, y_edge_high[:, None]], axis=1)
    )
    part_sc[...] = part.reshape(5, 64, 128)
    speed_sc[...] = speeds.reshape(4, 64, 128)
    prim = tuple(value[1:9] for value in prim_all)
    residual = x_part(q, prim_all) + jnp.stack(
        [part_sc[:, pl.ds(k, 8, stride=8), :] for k in range(8)], axis=1
    )
    right = x_right(residual, prim)
    xd, x_last = eliminate_right([right[:, k] for k in range(8)], lower, xm, xg)
    zero = jnp.zeros((8, 128), jnp.float32)
    for group, (matrix, families) in enumerate(GROUPS):
        for i in range(2):
            at = group * 32 + 2 * i
            some = i < len(families)
            xr_out[pl.ds(at, 8, stride=4), :] = x_last[families[i]] if some else zero
            xr_out[pl.ds(at + 1, 8, stride=4), :] = xd[0][families[i]] if some else zero
    send_x(xr_out, xr_in, 1)

    speeds = jnp.stack([speed_sc[:, pl.ds(k, 8, stride=8), :] for k in range(8)], axis=1)
    y_lower, y_upper = y_bands(swap_groups(speeds))
    y_lower, y_upper, first, last = y_ends(y_lower, y_upper, y_code_sc[...], start_y, end_y)
    ym, yg, yp, yq, y_own = eliminate(y_lower, y_upper, first, last)
    y_den, y_high_part, y_lev, y_p, y_q, y_joint, joined = y_join(y_own)
    ym_out[...] = jnp.zeros((32, 128), jnp.float32)
    for kind in range(4):
        line = 7 if kind < 2 else 0
        for matrix in range(3):
            for h in range(2):
                at = kind * 8 + matrix * 2 + h
                ym_out[pl.ds(at, 1), :] = joined[kind][matrix, h, line : line + 1]
    pltpu.make_async_copy(ym_out, ym_in.at[gy], recv_sem.at[3]).start()
    for other in others_y():
        pltpu.make_async_remote_copy(
            src_ref=ym_out,
            dst_ref=ym_in.at[gy],
            send_sem=send_sem.at[3],
            recv_sem=recv_sem.at[3],
            device_id=(gx, other),
            device_id_type=MESH,
        ).start()

    wait_all(xm_in, recv_sem.at[0])
    den, high_part, a, c = factor([xm_in[pl.ds(row, SX, stride=4), :] for row in range(4)])
    levels = factor_levels(a, c)
    wait_all(xr_in, recv_sem.at[1])
    for i in range(2):
        own_last = xr_in[pl.ds(2 * i, SX, stride=4), :]
        own_first = xr_in[pl.ds(2 * i + 1, SX, stride=4), :]
        d = den * own_last + high_part * roll(own_first, -1, 0)
        d = reduce_levels(d, levels)
        xs_out[pl.ds(2 * i, SX, stride=4), :] = roll(d, 1, 0)
        xs_out[pl.ds(2 * i + 1, SX, stride=4), :] = d
    send_x(xs_out, xs_in, 2)

    wait_all(ym_in, recv_sem.at[3])
    segments = [
        tuple(ym_in[j, pl.ds(8 * kind, 8), :] for kind in range(4)) for j in range(SY)
    ]
    for j, weights in enumerate(y_weights(segments)):
        for i, weight in enumerate(weights):
            y_weight_sc[j, i] = weight
    for i in range(10):
        for family, matrix in enumerate((0, 1, 1, 1, 2)):
            y_weight[i, pl.ds(2 * family, 2), :] = y_weight_sc[gy, i, pl.ds(2 * matrix, 2), :]

    r = q[0, 1:9]
    rc = r * prim[6]
    half_rc_inv = 0.5 / rc
    c2_inv = 1.0 / prim[5]

    wait_all(xs_in, recv_sem.at[2])

    def x_value(kind):
        rows = []
        for group, i in ((0, 0), (2, 0), (2, 1), (3, 0), (1, 0)):
            rows.append(xs_in[pl.ds(group * 32 + 2 * i + kind, 8, stride=4), :])
        return jnp.stack(rows)

    solved = jnp.stack(put_back(xd, xp, xq, x_value(0), x_value(1)), axis=1)
    right = swap_groups(y_right(solved, rc, half_rc_inv)).reshape(5, 2, 4, 8, 128)
    yd, y_last = eliminate_right([right[:, :, k] for k in range(4)], y_lower, ym, yg)
    y_d, joined_last, joined_first = y_join_right(
        yd[0], y_last, y_own, y_den, y_high_part, y_lev, y_joint
    )
    for family in range(5):
        for h in range(2):
            yr_sc[0, pl.ds(2 * family + h, 1), :] = joined_last[family, h, 7:8]
            yr_sc[1, pl.ds(2 * family + h, 1), :] = joined_first[family, h, 0:1]
    weights = [y_weight[i] for i in range(10)]
    own_add, before_add, own_out, before_out = y_emit(yr_sc[0], yr_sc[1], weights)
    yf_out[0], yf_out[1] = own_out, before_out
    for other in others_y():
        pltpu.make_async_remote_copy(
            src_ref=yf_out.at[jnp.where(other < gy, 1, 0), pl.ds(0, 10)],
            dst_ref=yf_in.at[gy, pl.ds(0, 10)],
            send_sem=send_sem.at[4],
            recv_sem=recv_sem.at[4],
            device_id=(gx, other),
            device_id_type=MESH,
        ).start()
    wait_all(yf_in.at[pl.ds(0, SY - 1), pl.ds(0, 10)], recv_sem.at[4])
    zero = jnp.zeros((16, 128), jnp.float32)
    below = sum((jnp.where(j < gy, yf_in[j], 0.0) for j in range(SY - 1)), zero)
    above = sum((jnp.where(j > gy, yf_in[j], 0.0) for j in range(1, SY)), zero)
    ys_sc[0], ys_sc[1] = y_meet(below, above, own_add, before_add, weights)

    def y_value(kind):
        return jnp.stack(
            [
                jnp.stack([ys_sc[kind, pl.ds(2 * family + h, 1), :] for h in range(2)])
                for family in range(5)
            ]
        )

    before, own = y_value(0), y_value(1)
    groups = y_d + five(y_p) * before + five(y_q) * own
    previous = jnp.where(row_of(groups.shape) == 0, before, roll(groups, 1, -2))
    solved = jnp.stack(put_back(yd, yp, yq, previous, groups), axis=2)
    solved = swap_groups(solved.reshape(5, 8, 8, 128))
    for field, value in enumerate(increments(solved, prim, r, half_rc_inv, c2_inv)):
        for k in range(8):
            out[field, pl.ds(k, 8, stride=8), :] = value[k]

    for copy in copies:
        copy.wait_send()
    for slot in range(3):
        wait_all(xm_out.at[pl.ds(0, 4 * (SX - 1))], send_sem.at[slot])
    wait_all(ym_in.at[pl.ds(0, SY - 1)], send_sem.at[3])
    wait_all(yf_in.at[pl.ds(0, SY - 1), pl.ds(0, 10)], send_sem.at[4])


def local(flow_state, x_codes, y_codes):
    f32 = jnp.float32

    def vmem(*shape):
        return pltpu.VMEM(shape, f32)

    result = pl.pallas_call(
        kernel,
        out_shape=jax.ShapeDtypeStruct((5, 64, 128), f32),
        in_specs=[pl.BlockSpec(memory_space=pltpu.HBM)] * 3,
        out_specs=pl.BlockSpec(memory_space=pltpu.VMEM),
        scratch_shapes=[
            vmem(5, 64, 128),
            vmem(5, 64, 128),
            vmem(4, 64, 128),
            vmem(2, 5, 8, 128),
            vmem(5, 8, 128),
            vmem(5, 8, 128),
            vmem(5, 8, 128),
            vmem(5, 8, 128),
            vmem(4 * SX, 128),
            vmem(4 * SX, 128),
            vmem(4 * SX, 128),
            vmem(4 * SX, 128),
            vmem(4 * SX, 128),
            vmem(4 * SX, 128),
            vmem(32, 128),
            vmem(SY, 32, 128),
            vmem(SY, 10, 8, 128),
            vmem(10, 16, 128),
            vmem(2, 16, 128),
            vmem(2, 16, 128),
            vmem(SY, 16, 128),
            vmem(2, 16, 128),
            pltpu.VMEM((2, 32), jnp.int32),
            pltpu.VMEM((2, 8), jnp.int32),
            pltpu.SemaphoreType.REGULAR((4,)),
            pltpu.SemaphoreType.DMA,
            pltpu.SemaphoreType.DMA((2,)),
            pltpu.SemaphoreType.DMA((4,)),
            pltpu.SemaphoreType.DMA((4,)),
            pltpu.SemaphoreType.DMA((5,)),
            pltpu.SemaphoreType.DMA((5,)),
        ],
        compiler_params=pltpu.CompilerParams(
            collective_id=0, has_side_effects=True, vmem_limit_bytes=VMEM_LIMIT
        ),
        name="step",
    )(flow_state, x_codes, y_codes)
    result = jnp.transpose(result.reshape(5, 8, 8, 128), (0, 2, 1, 3))
    return result.reshape(flow_state.shape)


def solution(mesh):
    return jax.shard_map(
        local,
        mesh=mesh,
        in_specs=(P(None, "gx", "gy"), P(None, "gy"), P(None, "gx")),
        out_specs=P(None, "gx", "gy"),
        check_vma=False,
    )
```

```python
import functools

import jax
import jax.numpy as jnp
from jax import lax
from jax.experimental import pallas as pl
from jax.experimental.pallas import tpu as pltpu
from jax.sharding import PartitionSpec as P

NZ = 32
SX = 32
SY = 16
VMEM_LIMIT = 56 * 1024 * 1024
MAIN = 801.0
GROUPS = ((0, (0,)), (2, (4,)), (1, (1, 2)), (1, (3,)))
MESH = pl.DeviceIdType.MESH


def far_first(*lengths):
    offsets = [()]
    for length in lengths:
        offsets = [(*offset, k) for offset in offsets for k in range(length)]
    hops = {
        offset: sum(min(k, length - k) for k, length in zip(offset, lengths)) for offset in offsets
    }
    return sorted((offset for offset in offsets if any(offset)), key=lambda o: (-hops[o], o))


NEAR = (0, 1, 7)
X_ORDER = far_first(8, 4)
Y_ORDER = far_first(8, 2)


def roll(value, shift, axis):
    axis = axis % value.ndim
    return pltpu.roll(value, shift % value.shape[axis], axis)


def lane_of(shape):
    return lax.broadcasted_iota(jnp.int32, shape, len(shape) - 1)


def row_of(shape):
    return lax.broadcasted_iota(jnp.int32, shape, len(shape) - 2)


def five(value):
    return jnp.concatenate([value[0:1], value[1:2], value[1:2], value[1:2], value[2:3]])


def primitives(q):
    inv = 1.0 / q[0]
    u, v, w = q[1] * inv, q[2] * inv, q[3] * inv
    p = 0.4 * (q[4] - 0.5 * (q[1] * u + q[2] * v + q[3] * w))
    c2 = 1.4 * p * inv
    return inv, u, v, w, p, c2, c2 * lax.rsqrt(c2)


def up_y(value):
    here, after = value[..., 1:9, :, :], value[..., 2:10, :, :]
    return roll(jnp.where(lane_of(here.shape) < 32, after, here), -32, -1)


def down_y(value):
    before, here = value[..., 0:8, :, :], value[..., 1:9, :, :]
    return roll(jnp.where(lane_of(here.shape) >= 96, before, here), 32, -1)


def z_difference(value):
    z = lane_of(value.shape) & 31
    after = jnp.where(z == 31, roll(value, 31, -1), roll(value, -1, -1))
    before = jnp.where(z == 0, roll(value, -31, -1), roll(value, 1, -1))
    return after - before


def yz_part(q):
    inv, u, v, w, p, c2, c = primitives(q)
    flux = jnp.stack([q[2], q[1] * v, q[2] * v + p, q[3] * v, v * (q[4] + p)])
    smooth = 400.0 * q
    flux = 0.25 * flux
    inner, wi, pi = q[:, 1:9], w[1:9], p[1:9]
    flux_z = jnp.stack(
        [inner[3], inner[1] * wi, inner[2] * wi, inner[3] * wi + pi, wi * (inner[4] + pi)]
    )
    part = up_y(smooth - flux) + down_y(smooth + flux) - 1600.0 * inner
    part = part - 0.25 * z_difference(flux_z)
    speeds = jnp.stack([v, c])
    return part, jnp.concatenate([down_y(speeds), up_y(speeds)])


def x_part(q, prim):
    inv, u, v, w, p, c2, c = prim
    flux = jnp.stack([q[1], q[1] * u + p, q[2] * u, q[3] * u, u * (q[4] + p)])
    smooth = 400.0 * q
    flux = 0.25 * flux
    return (smooth - flux)[:, 2:10] + (smooth + flux)[:, 0:8]


def x_right(res, prim):
    inv, u, v, w, p, c2, c = prim
    kinetic = 0.5 * (u * u + v * v + w * w)
    dp = 0.4 * (res[4] - u * res[1] - v * res[2] - w * res[3] + kinetic * res[0])
    normal = c * (res[1] - u * res[0])
    return jnp.stack(
        [
            dp - normal,
            c2 * res[0] - dp,
            (res[2] - v * res[0]) * inv,
            (res[3] - w * res[0]) * inv,
            dp + normal,
        ]
    )


def eliminate(lower, upper, main_first, main_last):
    n = len(lower)
    m = [1.0 / main_first]
    g = [upper[0] * m[0]]
    p = [-lower[0] * m[0]]
    for k in range(1, n - 1):
        m.append(1.0 / (MAIN - lower[k] * g[k - 1]))
        g.append(upper[k] * m[k])
        p.append(-(lower[k] * p[k - 1]) * m[k])
    q = [None] * (n - 1)
    q[n - 2] = -g[n - 2]
    for k in range(n - 3, -1, -1):
        p[k] = p[k] - g[k] * p[k + 1]
        q[k] = -(g[k] * q[k + 1])
    last = 1.0 / (main_last + lower[n - 1] * q[n - 2])
    m.append(last)
    own = (-(lower[n - 1] * p[n - 2]) * last, -upper[n - 1] * last, p[0], q[0])
    return m, g, p, q, own


def eliminate_right(right, lower, m, g):
    n = len(right)
    d = [right[0] * five(m[0])]
    for k in range(1, n - 1):
        d.append((right[k] - five(lower[k]) * d[k - 1]) * five(m[k]))
    for k in range(n - 3, -1, -1):
        d[k] = d[k] - five(g[k]) * d[k + 1]
    last = (right[n - 1] - five(lower[n - 1]) * d[n - 2]) * five(m[n - 1])
    return d, last


def put_back(d, p, q, before, own):
    cells = [d[k] + five(p[k]) * before + five(q[k]) * own for k in range(len(d))]
    return cells + [own]


def factor(own):
    to_before, to_after, first_before, first_own = own
    rows = to_before.shape[-2]
    den = 1.0 / (1.0 - to_after * roll(first_before, -1, -2))
    a = to_before * den
    c = to_after * roll(first_own, -1, -2) * den
    return den, to_after * den, a, c


def factor_levels(a, c):
    rows = a.shape[-2]
    levels = []
    step = 1
    while step < rows:
        dn = 1.0 / (1.0 - a * roll(c, step, -2) - c * roll(a, -step, -2))
        an, cn = a * dn, c * dn
        levels.append((dn, an, cn))
        a, c = an * roll(a, step, -2), cn * roll(c, -step, -2)
        step *= 2
    return levels


def reduce_levels(d, levels):
    step = 1
    for dn, an, cn in levels:
        d = dn * d + an * roll(d, step, -2) + cn * roll(d, -step, -2)
        step *= 2
    return d


def y_right(s, rc, half_rc_inv):
    dp = 0.5 * (s[0] + s[4])
    normal = rc * s[2]
    return jnp.stack([dp - normal, s[1], (s[4] - s[0]) * half_rc_inv, s[3], dp + normal])


def swap_groups(value):
    lead = value.shape[:-3]
    half = value.reshape(*lead, 2, 2, 2, 8, 128)
    a, b = half[..., 0, :, :, :], half[..., 1, :, :, :]
    low = (lane_of(a.shape) & 64) == 0
    a, b = jnp.where(low, a, roll(b, 64, -1)), jnp.where(low, roll(a, 64, -1), b)
    half = jnp.stack([a, b], axis=len(lead) + 1)
    a, b = half[..., 0, :, :], half[..., 1, :, :]
    low = (lane_of(a.shape) & 32) == 0
    a, b = jnp.where(low, a, roll(b, 32, -1)), jnp.where(low, roll(a, -32, -1), b)
    half = jnp.stack([a, b], axis=len(lead) + 2)
    return half.reshape(*lead, 8, 8, 128)


def y_bands(speeds):
    vm, cm, vp, cp = (speeds[i].reshape(2, 4, 8, 128) for i in range(4))
    low = jnp.stack([vm - cm, vm, vm + cm])
    high = jnp.stack([vp - cp, vp, vp + cp])
    lower = [-0.25 * low[:, :, k] - 400.0 for k in range(4)]
    upper = [0.25 * high[:, :, k] - 400.0 for k in range(4)]
    return lower, upper


def y_join(own):
    row = row_of(own[0].shape)
    den, high, a, c = factor(own)
    p = jnp.where(row == 0, a, 0.0)
    q = jnp.where(row == 7, 1.0, 0.0)
    a = jnp.where((row == 0) | (row == 7), 0.0, a)
    c = jnp.where(row == 7, 0.0, c)
    levels = factor_levels(a, c)
    p = reduce_levels(p, levels)
    q = reduce_levels(q, levels)
    last = 1.0 / (1.0 - own[0] * roll(q, 1, -2))
    joined = (
        own[0] * roll(p, 1, -2) * last,
        own[1] * last,
        own[2] + own[3] * p,
        own[3] * q,
    )
    return den, high, levels, p, q, last, joined


def y_join_right(d0, last_right, own, den, high, levels, last):
    row = row_of(last_right.shape)
    d = five(den) * last_right + five(high) * roll(d0, -1, -2)
    d = jnp.where(row == 7, 0.0, d)
    d = reduce_levels(d, [tuple(five(part) for part in level) for level in levels])
    joined_last = (last_right + five(own[0]) * roll(d, 1, -2)) * five(last)
    joined_first = d0 + five(own[3]) * d
    return d, joined_last, joined_first


def y_weights(segments):
    n = len(segments)
    ones = jnp.ones_like(segments[0][0])
    zero = jnp.zeros_like(ones)
    den, high, a, c = [], [], [], []
    for j, (to_before, to_after, _, _) in enumerate(segments):
        after = segments[j + 1] if j < n - 1 else (zero,) * 4
        den.append(1.0 / (1.0 - to_after * after[2]))
        high.append(to_after * den[j])
        a.append(to_before * den[j])
        c.append(high[j] * after[3])
    left, right = [None] * n, [None] * n
    for j in range(n):
        left[j] = c[j] / (1.0 - a[j] * left[j - 1]) if j else c[j]
    for j in range(n - 1, -1, -1):
        right[j] = a[j] / (1.0 - c[j] * right[j + 1]) if j < n - 1 else a[j]
    gain = []
    for j in range(n):
        rest = ones
        rest = rest - a[j] * left[j - 1] if j else rest
        rest = rest - c[j] * right[j + 1] if j < n - 1 else rest
        gain.append(1.0 / rest)
    down, up = [ones] * n, [ones] * n
    for j in range(1, n):
        down[j] = down[j - 1] * right[j]
    for j in range(n - 2, -1, -1):
        up[j] = up[j + 1] * left[j]
    weights = []
    for j in range(n):
        own_last = gain[j] * den[j]
        own_first = right[j] * gain[j - 1] * high[j - 1] if j else zero
        before_last = left[j - 1] * own_last if j else zero
        before_first = gain[j - 1] * high[j - 1] if j else zero
        down_inv = 1.0 / down[j]
        up_inv = 1.0 / up[j - 1] if j else ones
        weights.append(
            (
                own_last,
                own_first,
                before_last,
                before_first,
                down_inv,
                up_inv,
                down[j - 1] if j else zero,
                up[j],
                right[j],
                left[j - 1] if j else zero,
            )
        )
    return weights


def y_emit(last, first, w):
    own = w[0] * last + w[1] * first
    before = w[2] * last + w[3] * first
    return own, before, own * w[4], before * w[5]


def y_meet(below, above, own, before, w):
    low, high = w[6] * below, w[7] * above
    return low + w[9] * high + before, w[8] * low + own + high


def increments(s, prim, r, half_rc_inv, c2_inv):
    inv, u, v, w, p, c2, c = prim
    dp = 0.5 * (s[0] + s[4])
    dv = (s[4] - s[0]) * half_rc_inv
    dr = (s[1] + dp) * c2_inv
    du, dw = s[2], s[3]
    kinetic = 0.5 * (u * u + v * v + w * w)
    return (
        dr,
        u * dr + r * du,
        v * dr + r * dv,
        w * dr + r * dw,
        kinetic * dr + r * (u * du + v * dv + w * dw) + 2.5 * dp,
    )


def x_code_mask(codes, side):
    ones = (codes[side : side + 1] == 1).astype(jnp.float32)
    spread = jnp.where((lane_of((8, 32)) >> 2) == row_of((8, 32)), ones, 0.0)
    place = jnp.where((row_of((32, 128)) & 3) == (lane_of((32, 128)) >> 5), 1.0, 0.0)
    return jnp.dot(spread, place, preferred_element_type=jnp.float32) > 0.5


def y_code_mask(codes, side):
    ones = jnp.broadcast_to((codes[side : side + 1] == 1).astype(jnp.float32), (8, 8))
    halves = []
    for h in range(2):
        place = jnp.where(row_of((8, 128)) == 4 * h + (lane_of((8, 128)) >> 5), 1.0, 0.0)
        halves.append(jnp.dot(ones, place, preferred_element_type=jnp.float32))
    return jnp.stack(halves) > 0.5


def x_bands(u, c, codes, start, end):
    lam = jnp.stack([u - c, u, u + c])
    lower = [-0.25 * lam[:, k] - 400.0 for k in range(8)]
    upper = [0.25 * lam[:, k + 2] - 400.0 for k in range(8)]
    first = MAIN + jnp.where(x_code_mask(codes, 0)[None] & start, lower[0], 0.0)
    last = MAIN + jnp.where(x_code_mask(codes, 1)[None] & end, upper[7], 0.0)
    lower[0] = jnp.where(start, 0.0, lower[0])
    upper[7] = jnp.where(end, 0.0, upper[7])
    return lower, upper, first, last


def y_ends(lower, upper, codes, start, end):
    row = row_of(lower[0].shape)
    at_start = (row == 0) & start
    at_end = (row == 7) & end
    first = MAIN + jnp.where(at_start & y_code_mask(codes, 0)[None], lower[0], 0.0)
    last = MAIN + jnp.where(at_end & y_code_mask(codes, 1)[None], upper[3], 0.0)
    lower, upper = list(lower), list(upper)
    lower[0] = jnp.where(at_start, 0.0, lower[0])
    upper[3] = jnp.where(at_end, 0.0, upper[3])
    return lower, upper, first, last


def wait_all(ref, sem):
    pltpu.make_async_copy(ref, ref, sem).wait()


def kernel(
    flow,
    x_codes,
    y_codes,
    out,
    q_sc,
    part_sc,
    speed_sc,
    x_send,
    x_low,
    x_high,
    y_low,
    y_high,
    xm_out,
    xr_out,
    xm_in,
    xr_in,
    xs_out,
    xs_in,
    ym_out,
    ym_in,
    y_weight_sc,
    y_weight,
    yr_sc,
    yf_out,
    yf_in,
    ys_sc,
    x_code_sc,
    y_code_sc,
    word,
    in_sem,
    code_sem,
    halo_send,
    halo_recv,
    send_sem,
    recv_sem,
):
    gx, gy = lax.axis_index("gx"), lax.axis_index("gy")
    start_x, end_x = gx == 0, gx == SX - 1
    start_y, end_y = gy == 0, gy == SY - 1

    for b in range(8):
        pltpu.make_async_copy(
            flow.at[:, :, pl.ds(128 * b, 128)], q_sc.at[:, pl.ds(8 * b, 8), :], in_sem
        ).start()
    code_copies = [
        pltpu.make_async_copy(x_codes, x_code_sc, code_sem.at[0]),
        pltpu.make_async_copy(y_codes, y_code_sc, code_sem.at[1]),
    ]
    for copy in code_copies:
        copy.start()

    chip_y, chip_x = lax.div(gx, 4), lax.rem(gx, 4)
    chip_z, core = lax.div(gy, 2), lax.rem(gy, 2)
    x_after, x_before = lax.rem(gx + 1, SX), lax.rem(gx + SX - 1, SX)
    y_after, y_before = lax.rem(gy + 1, SY), lax.rem(gy + SY - 1, SY)

    def x_at(dy, dx):
        return 4 * lax.rem(chip_y + dy, 8) + lax.rem(chip_x + dx, 4), gy

    def y_at(dz, dc):
        return gx, 2 * lax.rem(chip_z + dz, 8) + lax.rem(core + dc, 2)

    near = [x_at(dy, dx) for dy, dx in X_ORDER if dy in NEAR]
    near += [y_at(dz, dc) for dz, dc in Y_ORDER if dz in NEAR]
    barrier = pltpu.get_barrier_semaphore()
    for device in near:
        pl.semaphore_signal(barrier, inc=1, device_id=device, device_id_type=MESH)

    def tell(step):
        for k in (step + 1, 7 - step):
            for device in (x_at(k, 0), y_at(k, 0)):
                pl.semaphore_signal(word.at[step], inc=1, device_id=device, device_id_type=MESH)

    def heard(step):
        pl.semaphore_wait(word.at[step], 4)

    wait_all(q_sc, in_sem)
    for copy in code_copies:
        copy.wait()

    x_send[0] = q_sc[:, pl.ds(7, 8, stride=8), :]
    x_send[1] = q_sc[:, pl.ds(0, 8, stride=8), :]
    pl.semaphore_wait(barrier, len(near))
    halos = [
        (x_send.at[0], x_low, (x_after, gy)),
        (x_send.at[1], x_high, (x_before, gy)),
        (q_sc.at[:, pl.ds(56, 8), :], y_low, (gx, y_after)),
        (q_sc.at[:, pl.ds(0, 8), :], y_high, (gx, y_before)),
    ]
    copies = []
    for i, (source, target, device) in enumerate(halos):
        copy = pltpu.make_async_remote_copy(
            src_ref=source,
            dst_ref=target,
            send_sem=halo_send.at[i],
            recv_sem=halo_recv.at[i],
            device_id=device,
            device_id_type=MESH,
        )
        copy.start()
        copies.append(copy)
    tell(0)
    heard(0)
    tell(1)

    def send_x(source, target, slot):
        mine = pl.ds(gx * 4, 4)
        pltpu.make_async_copy(source.at[mine], target.at[mine], recv_sem.at[slot]).start()

        for dy, dx in X_ORDER:
            other = 4 * lax.rem(lax.div(gx, 4) + dy, 8) + lax.rem(lax.rem(gx, 4) + dx, 4)
            pltpu.make_async_remote_copy(
                src_ref=source.at[pl.ds(other * 4, 4)],
                dst_ref=target.at[mine],
                send_sem=send_sem.at[slot],
                recv_sem=recv_sem.at[slot],
                device_id=(other, gy),
                device_id_type=MESH,
            ).start()

    def others_y():
        for dz, dc in Y_ORDER:
            yield 2 * lax.rem(lax.div(gy, 2) + dz, 8) + lax.rem(lax.rem(gy, 2) + dc, 2)

    for copy in copies:
        copy.wait_recv()
    inner = [q_sc[:, pl.ds(k, 8, stride=8), :] for k in range(8)]
    low = jnp.where(start_x, inner[0], x_low[...])
    high = jnp.where(end_x, inner[7], x_high[...])
    q = jnp.stack([low] + inner + [high], axis=1)
    prim_all = primitives(q)

    lower, upper, first, last = x_bands(prim_all[1], prim_all[6], x_code_sc[...], start_x, end_x)
    xm, xg, xp, xq, x_own = eliminate(lower, upper, first, last)
    for group, (matrix, families) in enumerate(GROUPS):
        for row in range(4):
            xm_out[pl.ds(group * 32 + row, 8, stride=4), :] = x_own[row][matrix]
    heard(1)
    send_x(xm_out, xm_in, 0)

    blocks = q_sc[...].reshape(5, 8, 8, 128)
    y_edge_low = jnp.where(start_y, roll(blocks[:, 0], 96, -1), y_low[...])
    y_edge_high = jnp.where(end_y, roll(blocks[:, 7], 32, -1), y_high[...])
    part, speeds = yz_part(
        jnp.concatenate([y_edge_low[:, None], blocks, y_edge_high[:, None]], axis=1)
    )
    part_sc[...] = part.reshape(5, 64, 128)
    speed_sc[...] = speeds.reshape(4, 64, 128)
    prim = tuple(value[1:9] for value in prim_all)
    residual = x_part(q, prim_all) + jnp.stack(
        [part_sc[:, pl.ds(k, 8, stride=8), :] for k in range(8)], axis=1
    )
    right = x_right(residual, prim)
    xd, x_last = eliminate_right([right[:, k] for k in range(8)], lower, xm, xg)
    zero = jnp.zeros((8, 128), jnp.float32)
    for group, (matrix, families) in enumerate(GROUPS):
        for i in range(2):
            at = group * 32 + 2 * i
            some = i < len(families)
            xr_out[pl.ds(at, 8, stride=4), :] = x_last[families[i]] if some else zero
            xr_out[pl.ds(at + 1, 8, stride=4), :] = xd[0][families[i]] if some else zero
    send_x(xr_out, xr_in, 1)

    speeds = jnp.stack([speed_sc[:, pl.ds(k, 8, stride=8), :] for k in range(8)], axis=1)
    y_lower, y_upper = y_bands(swap_groups(speeds))
    y_lower, y_upper, first, last = y_ends(y_lower, y_upper, y_code_sc[...], start_y, end_y)
    ym, yg, yp, yq, y_own = eliminate(y_lower, y_upper, first, last)
    y_den, y_high_part, y_lev, y_p, y_q, y_joint, joined = y_join(y_own)
    ym_out[...] = jnp.zeros((32, 128), jnp.float32)
    for kind in range(4):
        line = 7 if kind < 2 else 0
        for matrix in range(3):
            for h in range(2):
                at = kind * 8 + matrix * 2 + h
                ym_out[pl.ds(at, 1), :] = joined[kind][matrix, h, line : line + 1]
    pltpu.make_async_copy(ym_out, ym_in.at[gy], recv_sem.at[3]).start()
    for other in others_y():
        pltpu.make_async_remote_copy(
            src_ref=ym_out,
            dst_ref=ym_in.at[gy],
            send_sem=send_sem.at[3],
            recv_sem=recv_sem.at[3],
            device_id=(gx, other),
            device_id_type=MESH,
        ).start()

    wait_all(xm_in, recv_sem.at[0])
    den, high_part, a, c = factor([xm_in[pl.ds(row, SX, stride=4), :] for row in range(4)])
    levels = factor_levels(a, c)
    wait_all(xr_in, recv_sem.at[1])
    for i in range(2):
        own_last = xr_in[pl.ds(2 * i, SX, stride=4), :]
        own_first = xr_in[pl.ds(2 * i + 1, SX, stride=4), :]
        d = den * own_last + high_part * roll(own_first, -1, 0)
        d = reduce_levels(d, levels)
        xs_out[pl.ds(2 * i, SX, stride=4), :] = roll(d, 1, 0)
        xs_out[pl.ds(2 * i + 1, SX, stride=4), :] = d
    send_x(xs_out, xs_in, 2)

    wait_all(ym_in, recv_sem.at[3])
    segments = [
        tuple(ym_in[j, pl.ds(8 * kind, 8), :] for kind in range(4)) for j in range(SY)
    ]
    for j, weights in enumerate(y_weights(segments)):
        for i, weight in enumerate(weights):
            y_weight_sc[j, i] = weight
    for i in range(10):
        for family, matrix in enumerate((0, 1, 1, 1, 2)):
            y_weight[i, pl.ds(2 * family, 2), :] = y_weight_sc[gy, i, pl.ds(2 * matrix, 2), :]

    r = q[0, 1:9]
    rc = r * prim[6]
    half_rc_inv = 0.5 / rc
    c2_inv = 1.0 / prim[5]

    wait_all(xs_in, recv_sem.at[2])

    def x_value(kind):
        rows = []
        for group, i in ((0, 0), (2, 0), (2, 1), (3, 0), (1, 0)):
            rows.append(xs_in[pl.ds(group * 32 + 2 * i + kind, 8, stride=4), :])
        return jnp.stack(rows)

    solved = jnp.stack(put_back(xd, xp, xq, x_value(0), x_value(1)), axis=1)
    right = swap_groups(y_right(solved, rc, half_rc_inv)).reshape(5, 2, 4, 8, 128)
    yd, y_last = eliminate_right([right[:, :, k] for k in range(4)], y_lower, ym, yg)
    y_d, joined_last, joined_first = y_join_right(
        yd[0], y_last, y_own, y_den, y_high_part, y_lev, y_joint
    )
    for family in range(5):
        for h in range(2):
            yr_sc[0, pl.ds(2 * family + h, 1), :] = joined_last[family, h, 7:8]
            yr_sc[1, pl.ds(2 * family + h, 1), :] = joined_first[family, h, 0:1]
    weights = [y_weight[i] for i in range(10)]
    own_add, before_add, own_out, before_out = y_emit(yr_sc[0], yr_sc[1], weights)
    yf_out[0], yf_out[1] = own_out, before_out
    for other in others_y():
        pltpu.make_async_remote_copy(
            src_ref=yf_out.at[jnp.where(other < gy, 1, 0), pl.ds(0, 10)],
            dst_ref=yf_in.at[gy, pl.ds(0, 10)],
            send_sem=send_sem.at[4],
            recv_sem=recv_sem.at[4],
            device_id=(gx, other),
            device_id_type=MESH,
        ).start()
    wait_all(yf_in.at[pl.ds(0, SY - 1), pl.ds(0, 10)], recv_sem.at[4])
    zero = jnp.zeros((16, 128), jnp.float32)
    below = sum((jnp.where(j < gy, yf_in[j], 0.0) for j in range(SY - 1)), zero)
    above = sum((jnp.where(j > gy, yf_in[j], 0.0) for j in range(1, SY)), zero)
    ys_sc[0], ys_sc[1] = y_meet(below, above, own_add, before_add, weights)

    def y_value(kind):
        return jnp.stack(
            [
                jnp.stack([ys_sc[kind, pl.ds(2 * family + h, 1), :] for h in range(2)])
                for family in range(5)
            ]
        )

    before, own = y_value(0), y_value(1)
    groups = y_d + five(y_p) * before + five(y_q) * own
    previous = jnp.where(row_of(groups.shape) == 0, before, roll(groups, 1, -2))
    solved = jnp.stack(put_back(yd, yp, yq, previous, groups), axis=2)
    solved = swap_groups(solved.reshape(5, 8, 8, 128))
    for field, value in enumerate(increments(solved, prim, r, half_rc_inv, c2_inv)):
        for k in range(8):
            out[field, pl.ds(k, 8, stride=8), :] = value[k]

    for copy in copies:
        copy.wait_send()
    for slot in range(3):
        wait_all(xm_out.at[pl.ds(0, 4 * (SX - 1))], send_sem.at[slot])
    wait_all(ym_in.at[pl.ds(0, SY - 1)], send_sem.at[3])
    wait_all(yf_in.at[pl.ds(0, SY - 1), pl.ds(0, 10)], send_sem.at[4])


def local(flow_state, x_codes, y_codes):
    f32 = jnp.float32

    def vmem(*shape):
        return pltpu.VMEM(shape, f32)

    result = pl.pallas_call(
        kernel,
        out_shape=jax.ShapeDtypeStruct((5, 64, 128), f32),
        in_specs=[pl.BlockSpec(memory_space=pltpu.HBM)] * 3,
        out_specs=pl.BlockSpec(memory_space=pltpu.VMEM),
        scratch_shapes=[
            vmem(5, 64, 128),
            vmem(5, 64, 128),
            vmem(4, 64, 128),
            vmem(2, 5, 8, 128),
            vmem(5, 8, 128),
            vmem(5, 8, 128),
            vmem(5, 8, 128),
            vmem(5, 8, 128),
            vmem(4 * SX, 128),
            vmem(4 * SX, 128),
            vmem(4 * SX, 128),
            vmem(4 * SX, 128),
            vmem(4 * SX, 128),
            vmem(4 * SX, 128),
            vmem(32, 128),
            vmem(SY, 32, 128),
            vmem(SY, 10, 8, 128),
            vmem(10, 16, 128),
            vmem(2, 16, 128),
            vmem(2, 16, 128),
            vmem(SY, 16, 128),
            vmem(2, 16, 128),
            pltpu.VMEM((2, 32), jnp.int32),
            pltpu.VMEM((2, 8), jnp.int32),
            pltpu.SemaphoreType.REGULAR((2,)),
            pltpu.SemaphoreType.DMA,
            pltpu.SemaphoreType.DMA((2,)),
            pltpu.SemaphoreType.DMA((4,)),
            pltpu.SemaphoreType.DMA((4,)),
            pltpu.SemaphoreType.DMA((5,)),
            pltpu.SemaphoreType.DMA((5,)),
        ],
        compiler_params=pltpu.CompilerParams(
            collective_id=0, has_side_effects=True, vmem_limit_bytes=VMEM_LIMIT
        ),
        name="step",
    )(flow_state, x_codes, y_codes)
    result = jnp.transpose(result.reshape(5, 8, 8, 128), (0, 2, 1, 3))
    return result.reshape(flow_state.shape)


def solution(mesh):
    return jax.shard_map(
        local,
        mesh=mesh,
        in_specs=(P(None, "gx", "gy"), P(None, "gy"), P(None, "gx")),
        out_specs=P(None, "gx", "gy"),
        check_vma=False,
    )
```

```python
import functools

import jax
import jax.numpy as jnp
from jax import lax
from jax.experimental import pallas as pl
from jax.experimental.pallas import tpu as pltpu
from jax.sharding import PartitionSpec as P

NZ = 32
SX = 32
SY = 16
VMEM_LIMIT = 54950 * 1024
MAIN = 801.0
GROUPS = ((0, (0,)), (2, (4,)), (1, (1, 2)), (1, (3,)))
MESH = pl.DeviceIdType.MESH


def far_first(*lengths):
    offsets = [()]
    for length in lengths:
        offsets = [(*offset, k) for offset in offsets for k in range(length)]
    hops = {
        offset: sum(min(k, length - k) for k, length in zip(offset, lengths)) for offset in offsets
    }
    return sorted((offset for offset in offsets if any(offset)), key=lambda o: (-hops[o], o))


NEAR = (0, 1, 7)
X_ORDER = far_first(8, 4)
Y_ORDER = far_first(8, 2)


def roll(value, shift, axis):
    axis = axis % value.ndim
    return pltpu.roll(value, shift % value.shape[axis], axis)


def lane_of(shape):
    return lax.broadcasted_iota(jnp.int32, shape, len(shape) - 1)


def row_of(shape):
    return lax.broadcasted_iota(jnp.int32, shape, len(shape) - 2)


def five(value):
    return jnp.concatenate([value[0:1], value[1:2], value[1:2], value[1:2], value[2:3]])


def primitives(q):
    inv = 1.0 / q[0]
    u, v, w = q[1] * inv, q[2] * inv, q[3] * inv
    p = 0.4 * (q[4] - 0.5 * (q[1] * u + q[2] * v + q[3] * w))
    c2 = 1.4 * p * inv
    return inv, u, v, w, p, c2, c2 * lax.rsqrt(c2)


def up_y(value):
    here, after = value[..., 1:9, :, :], value[..., 2:10, :, :]
    return roll(jnp.where(lane_of(here.shape) < 32, after, here), -32, -1)


def down_y(value):
    before, here = value[..., 0:8, :, :], value[..., 1:9, :, :]
    return roll(jnp.where(lane_of(here.shape) >= 96, before, here), 32, -1)


def z_difference(value):
    z = lane_of(value.shape) & 31
    after = jnp.where(z == 31, roll(value, 31, -1), roll(value, -1, -1))
    before = jnp.where(z == 0, roll(value, -31, -1), roll(value, 1, -1))
    return after - before


def y_terms(q, prim):
    inv, u, v, w, p, c2, c = prim
    flux = 0.25 * jnp.stack([q[2], q[1] * v, q[2] * v + p, q[3] * v, v * (q[4] + p)])
    smooth = 400.0 * q
    return smooth - flux, smooth + flux, jnp.stack([v, c])


def z_terms(q, prim):
    inv, u, v, w, p, c2, c = prim
    flux = jnp.stack([q[3], q[1] * w, q[2] * w, q[3] * w + p, w * (q[4] + p)])
    return -1600.0 * q - 0.25 * z_difference(flux)


def x_terms(q, prim):
    inv, u, v, w, p, c2, c = prim
    flux = 0.25 * jnp.stack([q[1], q[1] * u + p, q[2] * u, q[3] * u, u * (q[4] + p)])
    smooth = 400.0 * q
    return smooth - flux, smooth + flux


def join(low, inner, high):
    return jnp.concatenate([low[:, None], inner, high[:, None]], axis=1)


def x_right(res, prim):
    inv, u, v, w, p, c2, c = prim
    kinetic = 0.5 * (u * u + v * v + w * w)
    dp = 0.4 * (res[4] - u * res[1] - v * res[2] - w * res[3] + kinetic * res[0])
    normal = c * (res[1] - u * res[0])
    return jnp.stack(
        [
            dp - normal,
            c2 * res[0] - dp,
            (res[2] - v * res[0]) * inv,
            (res[3] - w * res[0]) * inv,
            dp + normal,
        ]
    )


def eliminate(lower, upper, main_first, main_last):
    n = len(lower)
    m = [1.0 / main_first]
    g = [upper[0] * m[0]]
    p = [-lower[0] * m[0]]
    for k in range(1, n - 1):
        m.append(1.0 / (MAIN - lower[k] * g[k - 1]))
        g.append(upper[k] * m[k])
        p.append(-(lower[k] * p[k - 1]) * m[k])
    q = [None] * (n - 1)
    q[n - 2] = -g[n - 2]
    for k in range(n - 3, -1, -1):
        p[k] = p[k] - g[k] * p[k + 1]
        q[k] = -(g[k] * q[k + 1])
    last = 1.0 / (main_last + lower[n - 1] * q[n - 2])
    m.append(last)
    own = (-(lower[n - 1] * p[n - 2]) * last, -upper[n - 1] * last, p[0], q[0])
    return m, g, p, q, own


def eliminate_right(right, lower, m, g):
    n = len(right)
    d = [right[0] * five(m[0])]
    for k in range(1, n - 1):
        d.append((right[k] - five(lower[k]) * d[k - 1]) * five(m[k]))
    for k in range(n - 3, -1, -1):
        d[k] = d[k] - five(g[k]) * d[k + 1]
    last = (right[n - 1] - five(lower[n - 1]) * d[n - 2]) * five(m[n - 1])
    return d, last


def put_back(d, p, q, before, own):
    cells = [d[k] + five(p[k]) * before + five(q[k]) * own for k in range(len(d))]
    return cells + [own]


def factor(own):
    to_before, to_after, first_before, first_own = own
    rows = to_before.shape[-2]
    den = 1.0 / (1.0 - to_after * roll(first_before, -1, -2))
    a = to_before * den
    c = to_after * roll(first_own, -1, -2) * den
    return den, to_after * den, a, c


def factor_levels(a, c):
    rows = a.shape[-2]
    levels = []
    step = 1
    while step < rows:
        dn = 1.0 / (1.0 - a * roll(c, step, -2) - c * roll(a, -step, -2))
        an, cn = a * dn, c * dn
        levels.append((dn, an, cn))
        a, c = an * roll(a, step, -2), cn * roll(c, -step, -2)
        step *= 2
    return levels


def reduce_levels(d, levels):
    step = 1
    for dn, an, cn in levels:
        d = dn * d + an * roll(d, step, -2) + cn * roll(d, -step, -2)
        step *= 2
    return d


def y_right(s, rc, half_rc_inv):
    dp = 0.5 * (s[0] + s[4])
    normal = rc * s[2]
    return jnp.stack([dp - normal, s[1], (s[4] - s[0]) * half_rc_inv, s[3], dp + normal])


def swap_groups(value):
    lead = value.shape[:-3]
    half = value.reshape(*lead, 2, 2, 2, 8, 128)
    a, b = half[..., 0, :, :, :], half[..., 1, :, :, :]
    low = (lane_of(a.shape) & 64) == 0
    a, b = jnp.where(low, a, roll(b, 64, -1)), jnp.where(low, roll(a, 64, -1), b)
    half = jnp.stack([a, b], axis=len(lead) + 1)
    a, b = half[..., 0, :, :], half[..., 1, :, :]
    low = (lane_of(a.shape) & 32) == 0
    a, b = jnp.where(low, a, roll(b, 32, -1)), jnp.where(low, roll(a, -32, -1), b)
    half = jnp.stack([a, b], axis=len(lead) + 2)
    return half.reshape(*lead, 8, 8, 128)


def y_bands(speeds):
    vm, cm, vp, cp = (speeds[i].reshape(2, 4, 8, 128) for i in range(4))
    low = jnp.stack([vm - cm, vm, vm + cm])
    high = jnp.stack([vp - cp, vp, vp + cp])
    lower = [-0.25 * low[:, :, k] - 400.0 for k in range(4)]
    upper = [0.25 * high[:, :, k] - 400.0 for k in range(4)]
    return lower, upper


def y_join(own):
    row = row_of(own[0].shape)
    den, high, a, c = factor(own)
    p = jnp.where(row == 0, a, 0.0)
    q = jnp.where(row == 7, 1.0, 0.0)
    a = jnp.where((row == 0) | (row == 7), 0.0, a)
    c = jnp.where(row == 7, 0.0, c)
    levels = factor_levels(a, c)
    p = reduce_levels(p, levels)
    q = reduce_levels(q, levels)
    last = 1.0 / (1.0 - own[0] * roll(q, 1, -2))
    joined = (
        own[0] * roll(p, 1, -2) * last,
        own[1] * last,
        own[2] + own[3] * p,
        own[3] * q,
    )
    return den, high, levels, p, q, last, joined


def y_join_right(d0, last_right, own, den, high, levels, last):
    row = row_of(last_right.shape)
    d = five(den) * last_right + five(high) * roll(d0, -1, -2)
    d = jnp.where(row == 7, 0.0, d)
    d = reduce_levels(d, [tuple(five(part) for part in level) for level in levels])
    joined_last = (last_right + five(own[0]) * roll(d, 1, -2)) * five(last)
    joined_first = d0 + five(own[3]) * d
    return d, joined_last, joined_first


def y_weights(segments):
    n = len(segments)
    ones = jnp.ones_like(segments[0][0])
    zero = jnp.zeros_like(ones)
    den, high, a, c = [], [], [], []
    for j, (to_before, to_after, _, _) in enumerate(segments):
        after = segments[j + 1] if j < n - 1 else (zero,) * 4
        den.append(1.0 / (1.0 - to_after * after[2]))
        high.append(to_after * den[j])
        a.append(to_before * den[j])
        c.append(high[j] * after[3])
    left, right = [None] * n, [None] * n
    for j in range(n):
        left[j] = c[j] / (1.0 - a[j] * left[j - 1]) if j else c[j]
    for j in range(n - 1, -1, -1):
        right[j] = a[j] / (1.0 - c[j] * right[j + 1]) if j < n - 1 else a[j]
    gain = []
    for j in range(n):
        rest = ones
        rest = rest - a[j] * left[j - 1] if j else rest
        rest = rest - c[j] * right[j + 1] if j < n - 1 else rest
        gain.append(1.0 / rest)
    down, up = [ones] * n, [ones] * n
    for j in range(1, n):
        down[j] = down[j - 1] * right[j]
    for j in range(n - 2, -1, -1):
        up[j] = up[j + 1] * left[j]
    weights = []
    for j in range(n):
        own_last = gain[j] * den[j]
        own_first = right[j] * gain[j - 1] * high[j - 1] if j else zero
        before_last = left[j - 1] * own_last if j else zero
        before_first = gain[j - 1] * high[j - 1] if j else zero
        down_inv = 1.0 / down[j]
        up_inv = 1.0 / up[j - 1] if j else ones
        weights.append(
            (
                own_last,
                own_first,
                before_last,
                before_first,
                down_inv,
                up_inv,
                down[j - 1] if j else zero,
                up[j],
                right[j],
                left[j - 1] if j else zero,
            )
        )
    return weights


def y_emit(last, first, w):
    own = w[0] * last + w[1] * first
    before = w[2] * last + w[3] * first
    return own, before, own * w[4], before * w[5]


def y_meet(below, above, own, before, w):
    low, high = w[6] * below, w[7] * above
    return low + w[9] * high + before, w[8] * low + own + high


def increments(s, prim, r, half_rc_inv, c2_inv):
    inv, u, v, w, p, c2, c = prim
    dp = 0.5 * (s[0] + s[4])
    dv = (s[4] - s[0]) * half_rc_inv
    dr = (s[1] + dp) * c2_inv
    du, dw = s[2], s[3]
    kinetic = 0.5 * (u * u + v * v + w * w)
    return (
        dr,
        u * dr + r * du,
        v * dr + r * dv,
        w * dr + r * dw,
        kinetic * dr + r * (u * du + v * dv + w * dw) + 2.5 * dp,
    )


def x_code_mask(codes, side):
    ones = (codes[side : side + 1] == 1).astype(jnp.float32)
    spread = jnp.where((lane_of((8, 32)) >> 2) == row_of((8, 32)), ones, 0.0)
    place = jnp.where((row_of((32, 128)) & 3) == (lane_of((32, 128)) >> 5), 1.0, 0.0)
    return jnp.dot(spread, place, preferred_element_type=jnp.float32) > 0.5


def y_code_mask(codes, side):
    ones = jnp.broadcast_to((codes[side : side + 1] == 1).astype(jnp.float32), (8, 8))
    halves = []
    for h in range(2):
        place = jnp.where(row_of((8, 128)) == 4 * h + (lane_of((8, 128)) >> 5), 1.0, 0.0)
        halves.append(jnp.dot(ones, place, preferred_element_type=jnp.float32))
    return jnp.stack(halves) > 0.5


def x_bands(u, c, codes, start, end):
    lam = jnp.stack([u - c, u, u + c])
    lower = [-0.25 * lam[:, k] - 400.0 for k in range(8)]
    upper = [0.25 * lam[:, k + 2] - 400.0 for k in range(8)]
    first = MAIN + jnp.where(x_code_mask(codes, 0)[None] & start, lower[0], 0.0)
    last = MAIN + jnp.where(x_code_mask(codes, 1)[None] & end, upper[7], 0.0)
    lower[0] = jnp.where(start, 0.0, lower[0])
    upper[7] = jnp.where(end, 0.0, upper[7])
    return lower, upper, first, last


def y_ends(lower, upper, codes, start, end):
    row = row_of(lower[0].shape)
    at_start = (row == 0) & start
    at_end = (row == 7) & end
    first = MAIN + jnp.where(at_start & y_code_mask(codes, 0)[None], lower[0], 0.0)
    last = MAIN + jnp.where(at_end & y_code_mask(codes, 1)[None], upper[3], 0.0)
    lower, upper = list(lower), list(upper)
    lower[0] = jnp.where(at_start, 0.0, lower[0])
    upper[3] = jnp.where(at_end, 0.0, upper[3])
    return lower, upper, first, last


def wait_all(ref, sem):
    pltpu.make_async_copy(ref, ref, sem).wait()


def kernel(
    flow,
    codes,
    out,
    q_sc,
    part_sc,
    speed_sc,
    x_send,
    x_low,
    x_high,
    y_low,
    y_high,
    xm_out,
    xr_out,
    xm_in,
    xr_in,
    xs_out,
    xs_in,
    ym_out,
    ym_in,
    y_weight_sc,
    y_weight,
    yr_sc,
    yf_out,
    yc_in,
    yb_out,
    yf_in,
    ys_sc,
    code_sc,
    word,
    in_sem,
    code_sem,
    halo_send,
    halo_recv,
    send_sem,
    recv_sem,
):
    gx, gy = lax.axis_index("gx"), lax.axis_index("gy")
    start_x, end_x = gx == 0, gx == SX - 1
    start_y, end_y = gy == 0, gy == SY - 1

    chip_y, chip_x = lax.div(gx, 4), lax.rem(gx, 4)
    chip_z, core = lax.div(gy, 2), lax.rem(gy, 2)
    x_after, x_before = lax.rem(gx + 1, SX), lax.rem(gx + SX - 1, SX)
    y_after, y_before = lax.rem(gy + 1, SY), lax.rem(gy + SY - 1, SY)

    def x_at(dy, dx):
        return 4 * lax.rem(chip_y + dy, 8) + lax.rem(chip_x + dx, 4), gy

    def y_at(dz, dc):
        return gx, 2 * lax.rem(chip_z + dz, 8) + lax.rem(core + dc, 2)

    near = [x_at(dy, dx) for dy, dx in X_ORDER if dy in NEAR]
    near += [y_at(dz, dc) for dz, dc in Y_ORDER if dz in NEAR]
    barrier = pltpu.get_barrier_semaphore()
    for device in near:
        pl.semaphore_signal(barrier, inc=1, device_id=device, device_id_type=MESH)

    for b in range(8):
        pltpu.make_async_copy(
            flow.at[:, :, pl.ds(128 * b, 128)], q_sc.at[:, pl.ds(8 * b, 8), :], in_sem
        ).start()
    code_copy = pltpu.make_async_copy(codes, code_sc, code_sem)
    code_copy.start()

    def tell(step):
        for k in (step + 1, 7 - step):
            for device in (x_at(k, 0), y_at(k, 0)):
                pl.semaphore_signal(word.at[step], inc=1, device_id=device, device_id_type=MESH)

    def heard(step):
        pl.semaphore_wait(word.at[step], 4)

    pl.semaphore_wait(barrier, len(near))
    tell(0)
    wait_all(q_sc, in_sem)
    code_copy.wait()

    x_send[0] = q_sc[:, pl.ds(7, 8, stride=8), :]
    x_send[1] = q_sc[:, pl.ds(0, 8, stride=8), :]
    halos = [
        (x_send.at[0], x_low, (x_after, gy)),
        (x_send.at[1], x_high, (x_before, gy)),
        (q_sc.at[:, pl.ds(56, 8), :], y_low, (gx, y_after)),
        (q_sc.at[:, pl.ds(0, 8), :], y_high, (gx, y_before)),
    ]
    copies = []
    for i, (source, target, device) in enumerate(halos):
        copy = pltpu.make_async_remote_copy(
            src_ref=source,
            dst_ref=target,
            send_sem=halo_send.at[i],
            recv_sem=halo_recv.at[i],
            device_id=device,
            device_id_type=MESH,
        )
        copy.start()
        copies.append(copy)
    heard(0)
    tell(1)

    def send_x(source, target, slot):
        mine = pl.ds(gx * 4, 4)
        pltpu.make_async_copy(source.at[mine], target.at[mine], recv_sem.at[slot]).start()

        for dy, dx in X_ORDER:
            other = 4 * lax.rem(lax.div(gx, 4) + dy, 8) + lax.rem(lax.rem(gx, 4) + dx, 4)
            pltpu.make_async_remote_copy(
                src_ref=source.at[pl.ds(other * 4, 4)],
                dst_ref=target.at[mine],
                send_sem=send_sem.at[slot],
                recv_sem=recv_sem.at[slot],
                device_id=(other, gy),
                device_id_type=MESH,
            ).start()

    def others_y():
        for dz, dc in Y_ORDER:
            yield 2 * lax.rem(lax.div(gy, 2) + dz, 8) + lax.rem(lax.rem(gy, 2) + dc, 2)

    blocks = q_sc[...].reshape(5, 8, 8, 128)
    prim_o = primitives(blocks)
    to_before_y, to_after_y, speeds_y = y_terms(blocks, prim_o)
    part_z = z_terms(blocks, prim_o)
    q = jnp.stack([q_sc[:, pl.ds(k, 8, stride=8), :] for k in range(8)], axis=1)
    prim = primitives(q)
    to_before_x, to_after_x = x_terms(q, prim)

    for copy in copies:
        copy.wait_recv()
    low = jnp.where(start_x, q[:, 0], x_low[...])
    high = jnp.where(end_x, q[:, 7], x_high[...])
    prim_low, prim_high = primitives(low), primitives(high)
    u, c = (
        jnp.concatenate([prim_low[i][None], prim[i], prim_high[i][None]]) for i in (1, 6)
    )

    lower, upper, first, last = x_bands(u, c, code_sc[:, 0:32], start_x, end_x)
    xm, xg, xp, xq, x_own = eliminate(lower, upper, first, last)
    for group, (matrix, families) in enumerate(GROUPS):
        for row in range(4):
            xm_out[pl.ds(group * 32 + row, 8, stride=4), :] = x_own[row][matrix]
    heard(1)
    send_x(xm_out, xm_in, 0)

    y_edge_low = jnp.where(start_y, roll(blocks[:, 0], 96, -1), y_low[...])
    y_edge_high = jnp.where(end_y, roll(blocks[:, 7], 32, -1), y_high[...])
    low_terms = y_terms(y_edge_low, primitives(y_edge_low))
    high_terms = y_terms(y_edge_high, primitives(y_edge_high))
    part = (
        up_y(join(low_terms[0], to_before_y, high_terms[0]))
        + down_y(join(low_terms[1], to_after_y, high_terms[1]))
        + part_z
    )
    part_sc[...] = part.reshape(5, 64, 128)
    residual = (
        jnp.concatenate([to_before_x[:, 1:], x_terms(high, prim_high)[0][:, None]], axis=1)
        + jnp.concatenate([x_terms(low, prim_low)[1][:, None], to_after_x[:, :7]], axis=1)
        + jnp.stack([part_sc[:, pl.ds(k, 8, stride=8), :] for k in range(8)], axis=1)
    )
    right = x_right(residual, prim)
    xd, x_last = eliminate_right([right[:, k] for k in range(8)], lower, xm, xg)
    zero = jnp.zeros((8, 128), jnp.float32)
    for group, (matrix, families) in enumerate(GROUPS):
        for i in range(2):
            at = group * 32 + 2 * i
            some = i < len(families)
            xr_out[pl.ds(at, 8, stride=4), :] = x_last[families[i]] if some else zero
            xr_out[pl.ds(at + 1, 8, stride=4), :] = xd[0][families[i]] if some else zero
    send_x(xr_out, xr_in, 1)

    speeds_y = join(low_terms[2], speeds_y, high_terms[2])
    speed_sc[...] = jnp.concatenate([down_y(speeds_y), up_y(speeds_y)]).reshape(4, 64, 128)
    speeds = jnp.stack([speed_sc[:, pl.ds(k, 8, stride=8), :] for k in range(8)], axis=1)
    y_lower, y_upper = y_bands(swap_groups(speeds))
    y_lower, y_upper, first, last = y_ends(y_lower, y_upper, code_sc[:, 32:40], start_y, end_y)
    ym, yg, yp, yq, y_own = eliminate(y_lower, y_upper, first, last)
    y_den, y_high_part, y_lev, y_p, y_q, y_joint, joined = y_join(y_own)
    ym_out[...] = jnp.zeros((32, 128), jnp.float32)
    for kind in range(4):
        line = 7 if kind < 2 else 0
        for matrix in range(3):
            for h in range(2):
                at = kind * 8 + matrix * 2 + h
                ym_out[pl.ds(at, 1), :] = joined[kind][matrix, h, line : line + 1]
    pltpu.make_async_copy(ym_out, ym_in.at[gy], recv_sem.at[3]).start()
    for other in others_y():
        pltpu.make_async_remote_copy(
            src_ref=ym_out,
            dst_ref=ym_in.at[gy],
            send_sem=send_sem.at[3],
            recv_sem=recv_sem.at[3],
            device_id=(gx, other),
            device_id_type=MESH,
        ).start()

    wait_all(xm_in, recv_sem.at[0])
    den, high_part, a, c = factor([xm_in[pl.ds(row, SX, stride=4), :] for row in range(4)])
    levels = factor_levels(a, c)
    wait_all(xr_in, recv_sem.at[1])
    for i in range(2):
        own_last = xr_in[pl.ds(2 * i, SX, stride=4), :]
        own_first = xr_in[pl.ds(2 * i + 1, SX, stride=4), :]
        d = den * own_last + high_part * roll(own_first, -1, 0)
        d = reduce_levels(d, levels)
        xs_out[pl.ds(2 * i, SX, stride=4), :] = roll(d, 1, 0)
        xs_out[pl.ds(2 * i + 1, SX, stride=4), :] = d
    send_x(xs_out, xs_in, 2)

    wait_all(ym_in, recv_sem.at[3])
    segments = [
        tuple(ym_in[j, pl.ds(8 * kind, 8), :] for kind in range(4)) for j in range(SY)
    ]
    for j, weights in enumerate(y_weights(segments)):
        for i, weight in enumerate(weights):
            y_weight_sc[j, i] = weight
    for i in range(10):
        for family, matrix in enumerate((0, 1, 1, 1, 2)):
            y_weight[i, pl.ds(2 * family, 2), :] = y_weight_sc[gy, i, pl.ds(2 * matrix, 2), :]

    r = q[0]
    rc = r * prim[6]
    half_rc_inv = 0.5 / rc
    c2_inv = 1.0 / prim[5]

    wait_all(xs_in, recv_sem.at[2])

    def x_value(kind):
        rows = []
        for group, i in ((0, 0), (2, 0), (2, 1), (3, 0), (1, 0)):
            rows.append(xs_in[pl.ds(group * 32 + 2 * i + kind, 8, stride=4), :])
        return jnp.stack(rows)

    solved = jnp.stack(put_back(xd, xp, xq, x_value(0), x_value(1)), axis=1)
    right = swap_groups(y_right(solved, rc, half_rc_inv)).reshape(5, 2, 4, 8, 128)
    yd, y_last = eliminate_right([right[:, :, k] for k in range(4)], y_lower, ym, yg)
    y_d, joined_last, joined_first = y_join_right(
        yd[0], y_last, y_own, y_den, y_high_part, y_lev, y_joint
    )
    for family in range(5):
        for h in range(2):
            yr_sc[0, pl.ds(2 * family + h, 1), :] = joined_last[family, h, 7:8]
            yr_sc[1, pl.ds(2 * family + h, 1), :] = joined_first[family, h, 0:1]
    weights = [y_weight[i] for i in range(10)]
    own_add, before_add, own_out, before_out = y_emit(yr_sc[0], yr_sc[1], weights)
    yf_out[0], yf_out[1] = own_out, before_out
    core_copy = pltpu.make_async_remote_copy(
        src_ref=yf_out.at[:, pl.ds(0, 10)],
        dst_ref=yc_in.at[:, pl.ds(0, 10)],
        send_sem=send_sem.at[5],
        recv_sem=recv_sem.at[5],
        device_id=(gx, 2 * chip_z + 1 - core),
        device_id_type=MESH,
    )
    core_copy.start()
    core_copy.wait_recv()
    yb_out[0], yb_out[1] = own_out + yc_in[0], before_out + yc_in[1]
    for dz, dc in Y_ORDER:
        if dc == 0:
            other = lax.rem(chip_z + dz, 8)
            pltpu.make_async_remote_copy(
                src_ref=yb_out.at[jnp.where(other < chip_z, 1, 0), pl.ds(0, 10)],
                dst_ref=yf_in.at[chip_z, pl.ds(0, 10)],
                send_sem=send_sem.at[4],
                recv_sem=recv_sem.at[4],
                device_id=(gx, 2 * other + core),
                device_id_type=MESH,
            ).start()
    below = jnp.where(core == 1, yc_in[0], 0.0)
    above = jnp.where(core == 0, yc_in[1], 0.0)
    wait_all(yf_in.at[pl.ds(0, 7), pl.ds(0, 10)], recv_sem.at[4])
    for j in range(8):
        below = below + jnp.where(j < chip_z, yf_in[j], 0.0)
        above = above + jnp.where(j > chip_z, yf_in[j], 0.0)
    ys_sc[0], ys_sc[1] = y_meet(below, above, own_add, before_add, weights)

    def y_value(kind):
        return jnp.stack(
            [
                jnp.stack([ys_sc[kind, pl.ds(2 * family + h, 1), :] for h in range(2)])
                for family in range(5)
            ]
        )

    before, own = y_value(0), y_value(1)
    groups = y_d + five(y_p) * before + five(y_q) * own
    previous = jnp.where(row_of(groups.shape) == 0, before, roll(groups, 1, -2))
    solved = jnp.stack(put_back(yd, yp, yq, previous, groups), axis=2)
    solved = swap_groups(solved.reshape(5, 8, 8, 128))
    for field, value in enumerate(increments(solved, prim, r, half_rc_inv, c2_inv)):
        for k in range(8):
            out[field, pl.ds(k, 8, stride=8), :] = value[k]

    for copy in copies:
        copy.wait_send()
    for slot in range(3):
        wait_all(xm_out.at[pl.ds(0, 4 * (SX - 1))], send_sem.at[slot])
    wait_all(ym_in.at[pl.ds(0, SY - 1)], send_sem.at[3])
    wait_all(yf_in.at[pl.ds(0, 7), pl.ds(0, 10)], send_sem.at[4])
    core_copy.wait_send()


def local(flow_state, x_codes, y_codes):
    f32 = jnp.float32

    def vmem(*shape):
        return pltpu.VMEM(shape, f32)

    result = pl.pallas_call(
        kernel,
        out_shape=jax.ShapeDtypeStruct((5, 64, 128), f32),
        in_specs=[pl.BlockSpec(memory_space=pl.ANY)] * 2,
        out_specs=pl.BlockSpec(memory_space=pltpu.VMEM),
        scratch_shapes=[
            vmem(5, 64, 128),
            vmem(5, 64, 128),
            vmem(4, 64, 128),
            vmem(2, 5, 8, 128),
            vmem(5, 8, 128),
            vmem(5, 8, 128),
            vmem(5, 8, 128),
            vmem(5, 8, 128),
            vmem(4 * SX, 128),
            vmem(4 * SX, 128),
            vmem(4 * SX, 128),
            vmem(4 * SX, 128),
            vmem(4 * SX, 128),
            vmem(4 * SX, 128),
            vmem(32, 128),
            vmem(SY, 32, 128),
            vmem(SY, 10, 8, 128),
            vmem(10, 16, 128),
            vmem(2, 16, 128),
            vmem(2, 16, 128),
            vmem(2, 16, 128),
            vmem(2, 16, 128),
            vmem(8, 16, 128),
            vmem(2, 16, 128),
            pltpu.VMEM((2, 40), jnp.int32),
            pltpu.SemaphoreType.REGULAR((2,)),
            pltpu.SemaphoreType.DMA,
            pltpu.SemaphoreType.DMA,
            pltpu.SemaphoreType.DMA((4,)),
            pltpu.SemaphoreType.DMA((4,)),
            pltpu.SemaphoreType.DMA((6,)),
            pltpu.SemaphoreType.DMA((6,)),
        ],
        compiler_params=pltpu.CompilerParams(
            collective_id=0, has_side_effects=True, vmem_limit_bytes=VMEM_LIMIT
        ),
        name="step",
    )(flow_state, jnp.concatenate([x_codes, y_codes], axis=1))
    result = jnp.transpose(result.reshape(5, 8, 8, 128), (0, 2, 1, 3))
    return result.reshape(flow_state.shape)


def solution(mesh):
    return jax.shard_map(
        local,
        mesh=mesh,
        in_specs=(P(None, "gx", "gy"), P(None, "gy"), P(None, "gx")),
        out_specs=P(None, "gx", "gy"),
        check_vma=False,
    )
```

```python
import functools

import jax
import jax.numpy as jnp
from jax import lax
from jax.experimental import pallas as pl
from jax.experimental.pallas import tpu as pltpu
from jax.sharding import PartitionSpec as P

NZ = 32
SX = 32
SY = 16
VMEM_LIMIT = 32 * 1024 * 1024
MAIN = 801.0
GROUPS = ((0, (0,)), (2, (4,)), (1, (1, 2)), (1, (3,)))
MESH = pl.DeviceIdType.MESH


def far_first(*lengths):
    offsets = [()]
    for length in lengths:
        offsets = [(*offset, k) for offset in offsets for k in range(length)]
    hops = {
        offset: sum(min(k, length - k) for k, length in zip(offset, lengths)) for offset in offsets
    }
    return sorted((offset for offset in offsets if any(offset)), key=lambda o: (-hops[o], o))


NEAR = (0, 1, 7)
X_ORDER = far_first(8, 4)
Y_ORDER = far_first(8, 2)


def roll(value, shift, axis):
    axis = axis % value.ndim
    return pltpu.roll(value, shift % value.shape[axis], axis)


def lane_of(shape):
    return lax.broadcasted_iota(jnp.int32, shape, len(shape) - 1)


def row_of(shape):
    return lax.broadcasted_iota(jnp.int32, shape, len(shape) - 2)


def five(value):
    return jnp.concatenate([value[0:1], value[1:2], value[1:2], value[1:2], value[2:3]])


def primitives(q):
    inv = 1.0 / q[0]
    u, v, w = q[1] * inv, q[2] * inv, q[3] * inv
    p = 0.4 * (q[4] - 0.5 * (q[1] * u + q[2] * v + q[3] * w))
    c2 = 1.4 * p * inv
    return inv, u, v, w, p, c2, c2 * lax.rsqrt(c2)


def up_y(value):
    here, after = value[..., 1:9, :, :], value[..., 2:10, :, :]
    return roll(jnp.where(lane_of(here.shape) < 32, after, here), -32, -1)


def down_y(value):
    before, here = value[..., 0:8, :, :], value[..., 1:9, :, :]
    return roll(jnp.where(lane_of(here.shape) >= 96, before, here), 32, -1)


def z_difference(value):
    z = lane_of(value.shape) & 31
    after = jnp.where(z == 31, roll(value, 31, -1), roll(value, -1, -1))
    before = jnp.where(z == 0, roll(value, -31, -1), roll(value, 1, -1))
    return after - before


def y_terms(q, prim):
    inv, u, v, w, p, c2, c = prim
    flux = 0.25 * jnp.stack([q[2], q[1] * v, q[2] * v + p, q[3] * v, v * (q[4] + p)])
    smooth = 400.0 * q
    return smooth - flux, smooth + flux, jnp.stack([v, c])


def z_terms(q, prim):
    inv, u, v, w, p, c2, c = prim
    flux = jnp.stack([q[3], q[1] * w, q[2] * w, q[3] * w + p, w * (q[4] + p)])
    return -1600.0 * q - 0.25 * z_difference(flux)


def x_terms(q, prim):
    inv, u, v, w, p, c2, c = prim
    flux = 0.25 * jnp.stack([q[1], q[1] * u + p, q[2] * u, q[3] * u, u * (q[4] + p)])
    smooth = 400.0 * q
    return smooth - flux, smooth + flux


def join(low, inner, high):
    return jnp.concatenate([low[:, None], inner, high[:, None]], axis=1)


def x_right(res, prim):
    inv, u, v, w, p, c2, c = prim
    kinetic = 0.5 * (u * u + v * v + w * w)
    dp = 0.4 * (res[4] - u * res[1] - v * res[2] - w * res[3] + kinetic * res[0])
    normal = c * (res[1] - u * res[0])
    return jnp.stack(
        [
            dp - normal,
            c2 * res[0] - dp,
            (res[2] - v * res[0]) * inv,
            (res[3] - w * res[0]) * inv,
            dp + normal,
        ]
    )


def eliminate(lower, upper, main_first, main_last):
    n = len(lower)
    m = [1.0 / main_first]
    g = [upper[0] * m[0]]
    p = [-lower[0] * m[0]]
    for k in range(1, n - 1):
        m.append(1.0 / (MAIN - lower[k] * g[k - 1]))
        g.append(upper[k] * m[k])
        p.append(-(lower[k] * p[k - 1]) * m[k])
    q = [None] * (n - 1)
    q[n - 2] = -g[n - 2]
    for k in range(n - 3, -1, -1):
        p[k] = p[k] - g[k] * p[k + 1]
        q[k] = -(g[k] * q[k + 1])
    last = 1.0 / (main_last + lower[n - 1] * q[n - 2])
    m.append(last)
    own = (-(lower[n - 1] * p[n - 2]) * last, -upper[n - 1] * last, p[0], q[0])
    return m, g, p, q, own


def eliminate_right(right, lower, m, g):
    n = len(right)
    d = [right[0] * five(m[0])]
    for k in range(1, n - 1):
        d.append((right[k] - five(lower[k]) * d[k - 1]) * five(m[k]))
    for k in range(n - 3, -1, -1):
        d[k] = d[k] - five(g[k]) * d[k + 1]
    last = (right[n - 1] - five(lower[n - 1]) * d[n - 2]) * five(m[n - 1])
    return d, last


def put_back(d, p, q, before, own):
    cells = [d[k] + five(p[k]) * before + five(q[k]) * own for k in range(len(d))]
    return cells + [own]


def factor(own):
    to_before, to_after, first_before, first_own = own
    rows = to_before.shape[-2]
    den = 1.0 / (1.0 - to_after * roll(first_before, -1, -2))
    a = to_before * den
    c = to_after * roll(first_own, -1, -2) * den
    return den, to_after * den, a, c


def factor_levels(a, c):
    rows = a.shape[-2]
    levels = []
    step = 1
    while step < rows:
        dn = 1.0 / (1.0 - a * roll(c, step, -2) - c * roll(a, -step, -2))
        an, cn = a * dn, c * dn
        levels.append((dn, an, cn))
        a, c = an * roll(a, step, -2), cn * roll(c, -step, -2)
        step *= 2
    return levels


def reduce_levels(d, levels):
    step = 1
    for dn, an, cn in levels:
        d = dn * d + an * roll(d, step, -2) + cn * roll(d, -step, -2)
        step *= 2
    return d


def y_right(s, rc, half_rc_inv):
    dp = 0.5 * (s[0] + s[4])
    normal = rc * s[2]
    return jnp.stack([dp - normal, s[1], (s[4] - s[0]) * half_rc_inv, s[3], dp + normal])


def swap_groups(value):
    lead = value.shape[:-3]
    half = value.reshape(*lead, 2, 2, 2, 8, 128)
    a, b = half[..., 0, :, :, :], half[..., 1, :, :, :]
    low = (lane_of(a.shape) & 64) == 0
    a, b = jnp.where(low, a, roll(b, 64, -1)), jnp.where(low, roll(a, 64, -1), b)
    half = jnp.stack([a, b], axis=len(lead) + 1)
    a, b = half[..., 0, :, :], half[..., 1, :, :]
    low = (lane_of(a.shape) & 32) == 0
    a, b = jnp.where(low, a, roll(b, 32, -1)), jnp.where(low, roll(a, -32, -1), b)
    half = jnp.stack([a, b], axis=len(lead) + 2)
    return half.reshape(*lead, 8, 8, 128)


def y_bands(speeds):
    vm, cm, vp, cp = (speeds[i].reshape(2, 4, 8, 128) for i in range(4))
    low = jnp.stack([vm - cm, vm, vm + cm])
    high = jnp.stack([vp - cp, vp, vp + cp])
    lower = [-0.25 * low[:, :, k] - 400.0 for k in range(4)]
    upper = [0.25 * high[:, :, k] - 400.0 for k in range(4)]
    return lower, upper


def y_join(own):
    row = row_of(own[0].shape)
    den, high, a, c = factor(own)
    p = jnp.where(row == 0, a, 0.0)
    q = jnp.where(row == 7, 1.0, 0.0)
    a = jnp.where((row == 0) | (row == 7), 0.0, a)
    c = jnp.where(row == 7, 0.0, c)
    levels = factor_levels(a, c)
    p = reduce_levels(p, levels)
    q = reduce_levels(q, levels)
    last = 1.0 / (1.0 - own[0] * roll(q, 1, -2))
    joined = (
        own[0] * roll(p, 1, -2) * last,
        own[1] * last,
        own[2] + own[3] * p,
        own[3] * q,
    )
    return den, high, levels, p, q, last, joined


def y_join_right(d0, last_right, own, den, high, levels, last):
    row = row_of(last_right.shape)
    d = five(den) * last_right + five(high) * roll(d0, -1, -2)
    d = jnp.where(row == 7, 0.0, d)
    d = reduce_levels(d, [tuple(five(part) for part in level) for level in levels])
    joined_last = (last_right + five(own[0]) * roll(d, 1, -2)) * five(last)
    joined_first = d0 + five(own[3]) * d
    return d, joined_last, joined_first


def y_weights(segments):
    n = len(segments)
    ones = jnp.ones_like(segments[0][0])
    zero = jnp.zeros_like(ones)
    den, high, a, c = [], [], [], []
    for j, (to_before, to_after, _, _) in enumerate(segments):
        after = segments[j + 1] if j < n - 1 else (zero,) * 4
        den.append(1.0 / (1.0 - to_after * after[2]))
        high.append(to_after * den[j])
        a.append(to_before * den[j])
        c.append(high[j] * after[3])
    left, right = [None] * n, [None] * n
    for j in range(n):
        left[j] = c[j] / (1.0 - a[j] * left[j - 1]) if j else c[j]
    for j in range(n - 1, -1, -1):
        right[j] = a[j] / (1.0 - c[j] * right[j + 1]) if j < n - 1 else a[j]
    gain = []
    for j in range(n):
        rest = ones
        rest = rest - a[j] * left[j - 1] if j else rest
        rest = rest - c[j] * right[j + 1] if j < n - 1 else rest
        gain.append(1.0 / rest)
    down, up = [ones] * n, [ones] * n
    for j in range(1, n):
        down[j] = down[j - 1] * right[j]
    for j in range(n - 2, -1, -1):
        up[j] = up[j + 1] * left[j]
    weights = []
    for j in range(n):
        own_last = gain[j] * den[j]
        own_first = right[j] * gain[j - 1] * high[j - 1] if j else zero
        before_last = left[j - 1] * own_last if j else zero
        before_first = gain[j - 1] * high[j - 1] if j else zero
        down_inv = 1.0 / down[j]
        up_inv = 1.0 / up[j - 1] if j else ones
        weights.append(
            (
                own_last,
                own_first,
                before_last,
                before_first,
                down_inv,
                up_inv,
                down[j - 1] if j else zero,
                up[j],
                right[j],
                left[j - 1] if j else zero,
            )
        )
    return weights


def y_emit(last, first, w):
    own = w[0] * last + w[1] * first
    before = w[2] * last + w[3] * first
    return own, before, own * w[4], before * w[5]


def y_meet(below, above, own, before, w):
    low, high = w[6] * below, w[7] * above
    return low + w[9] * high + before, w[8] * low + own + high


def increments(s, prim, r, half_rc_inv, c2_inv):
    inv, u, v, w, p, c2, c = prim
    dp = 0.5 * (s[0] + s[4])
    dv = (s[4] - s[0]) * half_rc_inv
    dr = (s[1] + dp) * c2_inv
    du, dw = s[2], s[3]
    kinetic = 0.5 * (u * u + v * v + w * w)
    return (
        dr,
        u * dr + r * du,
        v * dr + r * dv,
        w * dr + r * dw,
        kinetic * dr + r * (u * du + v * dv + w * dw) + 2.5 * dp,
    )


def x_code_mask(codes, side):
    ones = (codes[side : side + 1] == 1).astype(jnp.float32)
    spread = jnp.where((lane_of((8, 32)) >> 2) == row_of((8, 32)), ones, 0.0)
    place = jnp.where((row_of((32, 128)) & 3) == (lane_of((32, 128)) >> 5), 1.0, 0.0)
    return jnp.dot(spread, place, preferred_element_type=jnp.float32) > 0.5


def y_code_mask(codes, side):
    ones = jnp.broadcast_to((codes[side : side + 1] == 1).astype(jnp.float32), (8, 8))
    halves = []
    for h in range(2):
        place = jnp.where(row_of((8, 128)) == 4 * h + (lane_of((8, 128)) >> 5), 1.0, 0.0)
        halves.append(jnp.dot(ones, place, preferred_element_type=jnp.float32))
    return jnp.stack(halves) > 0.5


def x_bands(u, c, codes, start, end):
    lam = jnp.stack([u - c, u, u + c])
    lower = [-0.25 * lam[:, k] - 400.0 for k in range(8)]
    upper = [0.25 * lam[:, k + 2] - 400.0 for k in range(8)]
    first = MAIN + jnp.where(x_code_mask(codes, 0)[None] & start, lower[0], 0.0)
    last = MAIN + jnp.where(x_code_mask(codes, 1)[None] & end, upper[7], 0.0)
    lower[0] = jnp.where(start, 0.0, lower[0])
    upper[7] = jnp.where(end, 0.0, upper[7])
    return lower, upper, first, last


def y_ends(lower, upper, codes, start, end):
    row = row_of(lower[0].shape)
    at_start = (row == 0) & start
    at_end = (row == 7) & end
    first = MAIN + jnp.where(at_start & y_code_mask(codes, 0)[None], lower[0], 0.0)
    last = MAIN + jnp.where(at_end & y_code_mask(codes, 1)[None], upper[3], 0.0)
    lower, upper = list(lower), list(upper)
    lower[0] = jnp.where(at_start, 0.0, lower[0])
    upper[3] = jnp.where(at_end, 0.0, upper[3])
    return lower, upper, first, last


def wait_all(ref, sem):
    pltpu.make_async_copy(ref, ref, sem).wait()


def kernel(
    flow,
    x_codes,
    y_codes,
    out,
    q_sc,
    part_sc,
    speed_sc,
    x_send,
    x_low,
    x_high,
    y_low,
    y_high,
    xm_out,
    xr_out,
    xm_in,
    xr_in,
    xs_out,
    xs_in,
    ym_out,
    ym_in,
    y_weight_sc,
    y_weight,
    yr_sc,
    yf_out,
    yc_in,
    yb_out,
    yf_in,
    ys_sc,
    x_code_sc,
    y_code_sc,
    word,
    in_sem,
    code_sem,
    halo_send,
    halo_recv,
    send_sem,
    recv_sem,
):
    gx, gy = lax.axis_index("gx"), lax.axis_index("gy")
    start_x, end_x = gx == 0, gx == SX - 1
    start_y, end_y = gy == 0, gy == SY - 1

    chip_y, chip_x = lax.div(gx, 4), lax.rem(gx, 4)
    chip_z, core = lax.div(gy, 2), lax.rem(gy, 2)
    x_after, x_before = lax.rem(gx + 1, SX), lax.rem(gx + SX - 1, SX)
    y_after, y_before = lax.rem(gy + 1, SY), lax.rem(gy + SY - 1, SY)

    def x_at(dy, dx):
        return 4 * lax.rem(chip_y + dy, 8) + lax.rem(chip_x + dx, 4), gy

    def y_at(dz, dc):
        return gx, 2 * lax.rem(chip_z + dz, 8) + lax.rem(core + dc, 2)

    near = [x_at(dy, dx) for dy, dx in X_ORDER if dy in NEAR]
    near += [y_at(dz, dc) for dz, dc in Y_ORDER if dz in NEAR]
    barrier = pltpu.get_barrier_semaphore()
    for device in near:
        pl.semaphore_signal(barrier, inc=1, device_id=device, device_id_type=MESH)

    for b in range(8):
        pltpu.make_async_copy(
            flow.at[:, :, pl.ds(128 * b, 128)], q_sc.at[:, pl.ds(8 * b, 8), :], in_sem
        ).start()
    code_copies = [
        pltpu.make_async_copy(x_codes, x_code_sc, code_sem.at[0]),
        pltpu.make_async_copy(y_codes, y_code_sc, code_sem.at[1]),
    ]
    for copy in code_copies:
        copy.start()

    def tell(step):
        for k in (step + 1, 7 - step):
            for device in (x_at(k, 0), y_at(k, 0)):
                pl.semaphore_signal(word.at[step], inc=1, device_id=device, device_id_type=MESH)

    def heard(step):
        pl.semaphore_wait(word.at[step], 4)

    pl.semaphore_wait(barrier, len(near))
    tell(0)
    wait_all(q_sc, in_sem)
    for copy in code_copies:
        copy.wait()

    x_send[0] = q_sc[:, pl.ds(7, 8, stride=8), :]
    x_send[1] = q_sc[:, pl.ds(0, 8, stride=8), :]
    halos = [
        (x_send.at[0], x_low, (x_after, gy)),
        (x_send.at[1], x_high, (x_before, gy)),
        (q_sc.at[:, pl.ds(56, 8), :], y_low, (gx, y_after)),
        (q_sc.at[:, pl.ds(0, 8), :], y_high, (gx, y_before)),
    ]
    copies = []
    for i, (source, target, device) in enumerate(halos):
        copy = pltpu.make_async_remote_copy(
            src_ref=source,
            dst_ref=target,
            send_sem=halo_send.at[i],
            recv_sem=halo_recv.at[i],
            device_id=device,
            device_id_type=MESH,
        )
        copy.start()
        copies.append(copy)
    heard(0)
    tell(1)

    def send_x(source, target, slot):
        mine = pl.ds(gx * 4, 4)
        pltpu.make_async_copy(source.at[mine], target.at[mine], recv_sem.at[slot]).start()

        for dy, dx in X_ORDER:
            other = 4 * lax.rem(lax.div(gx, 4) + dy, 8) + lax.rem(lax.rem(gx, 4) + dx, 4)
            pltpu.make_async_remote_copy(
                src_ref=source.at[pl.ds(other * 4, 4)],
                dst_ref=target.at[mine],
                send_sem=send_sem.at[slot],
                recv_sem=recv_sem.at[slot],
                device_id=(other, gy),
                device_id_type=MESH,
            ).start()

    def others_y():
        for dz, dc in Y_ORDER:
            yield 2 * lax.rem(lax.div(gy, 2) + dz, 8) + lax.rem(lax.rem(gy, 2) + dc, 2)

    blocks = q_sc[...].reshape(5, 8, 8, 128)
    prim_o = primitives(blocks)
    to_before_y, to_after_y, speeds_y = y_terms(blocks, prim_o)
    part_z = z_terms(blocks, prim_o)
    q = jnp.stack([q_sc[:, pl.ds(k, 8, stride=8), :] for k in range(8)], axis=1)
    prim = primitives(q)
    to_before_x, to_after_x = x_terms(q, prim)

    for copy in copies:
        copy.wait_recv()
    low = jnp.where(start_x, q[:, 0], x_low[...])
    high = jnp.where(end_x, q[:, 7], x_high[...])
    prim_low, prim_high = primitives(low), primitives(high)
    u, c = (
        jnp.concatenate([prim_low[i][None], prim[i], prim_high[i][None]]) for i in (1, 6)
    )

    lower, upper, first, last = x_bands(u, c, x_code_sc[...], start_x, end_x)
    xm, xg, xp, xq, x_own = eliminate(lower, upper, first, last)
    for group, (matrix, families) in enumerate(GROUPS):
        for row in range(4):
            xm_out[pl.ds(group * 32 + row, 8, stride=4), :] = x_own[row][matrix]
    heard(1)
    send_x(xm_out, xm_in, 0)

    y_edge_low = jnp.where(start_y, roll(blocks[:, 0], 96, -1), y_low[...])
    y_edge_high = jnp.where(end_y, roll(blocks[:, 7], 32, -1), y_high[...])
    low_terms = y_terms(y_edge_low, primitives(y_edge_low))
    high_terms = y_terms(y_edge_high, primitives(y_edge_high))
    part = (
        up_y(join(low_terms[0], to_before_y, high_terms[0]))
        + down_y(join(low_terms[1], to_after_y, high_terms[1]))
        + part_z
    )
    part_sc[...] = part.reshape(5, 64, 128)
    residual = (
        jnp.concatenate([to_before_x[:, 1:], x_terms(high, prim_high)[0][:, None]], axis=1)
        + jnp.concatenate([x_terms(low, prim_low)[1][:, None], to_after_x[:, :7]], axis=1)
        + jnp.stack([part_sc[:, pl.ds(k, 8, stride=8), :] for k in range(8)], axis=1)
    )
    right = x_right(residual, prim)
    xd, x_last = eliminate_right([right[:, k] for k in range(8)], lower, xm, xg)
    zero = jnp.zeros((8, 128), jnp.float32)
    for group, (matrix, families) in enumerate(GROUPS):
        for i in range(2):
            at = group * 32 + 2 * i
            some = i < len(families)
            xr_out[pl.ds(at, 8, stride=4), :] = x_last[families[i]] if some else zero
            xr_out[pl.ds(at + 1, 8, stride=4), :] = xd[0][families[i]] if some else zero
    send_x(xr_out, xr_in, 1)

    speeds_y = join(low_terms[2], speeds_y, high_terms[2])
    speed_sc[...] = jnp.concatenate([down_y(speeds_y), up_y(speeds_y)]).reshape(4, 64, 128)
    speeds = jnp.stack([speed_sc[:, pl.ds(k, 8, stride=8), :] for k in range(8)], axis=1)
    y_lower, y_upper = y_bands(swap_groups(speeds))
    y_lower, y_upper, first, last = y_ends(y_lower, y_upper, y_code_sc[...], start_y, end_y)
    ym, yg, yp, yq, y_own = eliminate(y_lower, y_upper, first, last)
    y_den, y_high_part, y_lev, y_p, y_q, y_joint, joined = y_join(y_own)
    ym_out[...] = jnp.zeros((32, 128), jnp.float32)
    for kind in range(4):
        line = 7 if kind < 2 else 0
        for matrix in range(3):
            for h in range(2):
                at = kind * 8 + matrix * 2 + h
                ym_out[pl.ds(at, 1), :] = joined[kind][matrix, h, line : line + 1]
    pltpu.make_async_copy(ym_out, ym_in.at[gy], recv_sem.at[3]).start()
    for other in others_y():
        pltpu.make_async_remote_copy(
            src_ref=ym_out,
            dst_ref=ym_in.at[gy],
            send_sem=send_sem.at[3],
            recv_sem=recv_sem.at[3],
            device_id=(gx, other),
            device_id_type=MESH,
        ).start()

    wait_all(xm_in, recv_sem.at[0])
    den, high_part, a, c = factor([xm_in[pl.ds(row, SX, stride=4), :] for row in range(4)])
    levels = factor_levels(a, c)
    wait_all(xr_in, recv_sem.at[1])
    for i in range(2):
        own_last = xr_in[pl.ds(2 * i, SX, stride=4), :]
        own_first = xr_in[pl.ds(2 * i + 1, SX, stride=4), :]
        d = den * own_last + high_part * roll(own_first, -1, 0)
        d = reduce_levels(d, levels)
        xs_out[pl.ds(2 * i, SX, stride=4), :] = roll(d, 1, 0)
        xs_out[pl.ds(2 * i + 1, SX, stride=4), :] = d
    send_x(xs_out, xs_in, 2)

    wait_all(ym_in, recv_sem.at[3])
    segments = [
        tuple(ym_in[j, pl.ds(8 * kind, 8), :] for kind in range(4)) for j in range(SY)
    ]
    for j, weights in enumerate(y_weights(segments)):
        for i, weight in enumerate(weights):
            y_weight_sc[j, i] = weight
    for i in range(10):
        for family, matrix in enumerate((0, 1, 1, 1, 2)):
            y_weight[i, pl.ds(2 * family, 2), :] = y_weight_sc[gy, i, pl.ds(2 * matrix, 2), :]

    r = q[0]
    rc = r * prim[6]
    half_rc_inv = 0.5 / rc
    c2_inv = 1.0 / prim[5]

    wait_all(xs_in, recv_sem.at[2])

    def x_value(kind):
        rows = []
        for group, i in ((0, 0), (2, 0), (2, 1), (3, 0), (1, 0)):
            rows.append(xs_in[pl.ds(group * 32 + 2 * i + kind, 8, stride=4), :])
        return jnp.stack(rows)

    solved = jnp.stack(put_back(xd, xp, xq, x_value(0), x_value(1)), axis=1)
    right = swap_groups(y_right(solved, rc, half_rc_inv)).reshape(5, 2, 4, 8, 128)
    yd, y_last = eliminate_right([right[:, :, k] for k in range(4)], y_lower, ym, yg)
    y_d, joined_last, joined_first = y_join_right(
        yd[0], y_last, y_own, y_den, y_high_part, y_lev, y_joint
    )
    for family in range(5):
        for h in range(2):
            yr_sc[0, pl.ds(2 * family + h, 1), :] = joined_last[family, h, 7:8]
            yr_sc[1, pl.ds(2 * family + h, 1), :] = joined_first[family, h, 0:1]
    weights = [y_weight[i] for i in range(10)]
    own_add, before_add, own_out, before_out = y_emit(yr_sc[0], yr_sc[1], weights)
    yf_out[0], yf_out[1] = own_out, before_out
    core_copy = pltpu.make_async_remote_copy(
        src_ref=yf_out.at[:, pl.ds(0, 10)],
        dst_ref=yc_in.at[:, pl.ds(0, 10)],
        send_sem=send_sem.at[5],
        recv_sem=recv_sem.at[5],
        device_id=(gx, 2 * chip_z + 1 - core),
        device_id_type=MESH,
    )
    core_copy.start()
    core_copy.wait_recv()
    yb_out[0], yb_out[1] = own_out + yc_in[0], before_out + yc_in[1]
    for dz, dc in Y_ORDER:
        if dc == 0:
            other = lax.rem(chip_z + dz, 8)
            pltpu.make_async_remote_copy(
                src_ref=yb_out.at[jnp.where(other < chip_z, 1, 0), pl.ds(0, 10)],
                dst_ref=yf_in.at[chip_z, pl.ds(0, 10)],
                send_sem=send_sem.at[4],
                recv_sem=recv_sem.at[4],
                device_id=(gx, 2 * other + core),
                device_id_type=MESH,
            ).start()
    below = jnp.where(core == 1, yc_in[0], 0.0)
    above = jnp.where(core == 0, yc_in[1], 0.0)
    wait_all(yf_in.at[pl.ds(0, 7), pl.ds(0, 10)], recv_sem.at[4])
    for j in range(8):
        below = below + jnp.where(j < chip_z, yf_in[j], 0.0)
        above = above + jnp.where(j > chip_z, yf_in[j], 0.0)
    ys_sc[0], ys_sc[1] = y_meet(below, above, own_add, before_add, weights)

    def y_value(kind):
        return jnp.stack(
            [
                jnp.stack([ys_sc[kind, pl.ds(2 * family + h, 1), :] for h in range(2)])
                for family in range(5)
            ]
        )

    before, own = y_value(0), y_value(1)
    groups = y_d + five(y_p) * before + five(y_q) * own
    previous = jnp.where(row_of(groups.shape) == 0, before, roll(groups, 1, -2))
    solved = jnp.stack(put_back(yd, yp, yq, previous, groups), axis=2)
    solved = swap_groups(solved.reshape(5, 8, 8, 128))
    for field, value in enumerate(increments(solved, prim, r, half_rc_inv, c2_inv)):
        for k in range(8):
            out[field, pl.ds(k, 8, stride=8), :] = value[k]

    for copy in copies:
        copy.wait_send()
    for slot in range(3):
        wait_all(xm_out.at[pl.ds(0, 4 * (SX - 1))], send_sem.at[slot])
    wait_all(ym_in.at[pl.ds(0, SY - 1)], send_sem.at[3])
    wait_all(yf_in.at[pl.ds(0, 7), pl.ds(0, 10)], send_sem.at[4])
    core_copy.wait_send()


def local(flow_state, x_codes, y_codes):
    f32 = jnp.float32

    def vmem(*shape):
        return pltpu.VMEM(shape, f32)

    result = pl.pallas_call(
        kernel,
        out_shape=jax.ShapeDtypeStruct((5, 64, 128), f32),
        in_specs=[pl.BlockSpec(memory_space=pltpu.HBM)] * 3,
        out_specs=pl.BlockSpec(memory_space=pltpu.VMEM),
        scratch_shapes=[
            vmem(5, 64, 128),
            vmem(5, 64, 128),
            vmem(4, 64, 128),
            vmem(2, 5, 8, 128),
            vmem(5, 8, 128),
            vmem(5, 8, 128),
            vmem(5, 8, 128),
            vmem(5, 8, 128),
            vmem(4 * SX, 128),
            vmem(4 * SX, 128),
            vmem(4 * SX, 128),
            vmem(4 * SX, 128),
            vmem(4 * SX, 128),
            vmem(4 * SX, 128),
            vmem(32, 128),
            vmem(SY, 32, 128),
            vmem(SY, 10, 8, 128),
            vmem(10, 16, 128),
            vmem(2, 16, 128),
            vmem(2, 16, 128),
            vmem(2, 16, 128),
            vmem(2, 16, 128),
            vmem(8, 16, 128),
            vmem(2, 16, 128),
            pltpu.VMEM((2, 32), jnp.int32),
            pltpu.VMEM((2, 8), jnp.int32),
            pltpu.SemaphoreType.REGULAR((2,)),
            pltpu.SemaphoreType.DMA,
            pltpu.SemaphoreType.DMA((2,)),
            pltpu.SemaphoreType.DMA((4,)),
            pltpu.SemaphoreType.DMA((4,)),
            pltpu.SemaphoreType.DMA((6,)),
            pltpu.SemaphoreType.DMA((6,)),
        ],
        compiler_params=pltpu.CompilerParams(
            collective_id=0, has_side_effects=True, vmem_limit_bytes=VMEM_LIMIT
        ),
        name="step",
    )(*(pltpu.with_memory_space_constraint(v, pltpu.HBM) for v in (flow_state, x_codes, y_codes)))
    result = jnp.transpose(result.reshape(5, 8, 8, 128), (0, 2, 1, 3))
    return result.reshape(flow_state.shape)


def solution(mesh):
    return jax.shard_map(
        local,
        mesh=mesh,
        in_specs=(P(None, "gx", "gy"), P(None, "gy"), P(None, "gx")),
        out_specs=P(None, "gx", "gy"),
        check_vma=False,
    )
```

```python
import functools

import jax
import jax.numpy as jnp
from jax import lax
from jax.experimental import pallas as pl
from jax.experimental.pallas import tpu as pltpu
from jax.sharding import PartitionSpec as P

NZ = 32
SX = 32
SY = 16
VMEM_LIMIT = 32 * 1024 * 1024
MAIN = 801.0
GROUPS = ((0, (0,)), (2, (4,)), (1, (1, 2)), (1, (3,)))
MESH = pl.DeviceIdType.MESH


def far_first(*lengths):
    offsets = [()]
    for length in lengths:
        offsets = [(*offset, k) for offset in offsets for k in range(length)]
    hops = {
        offset: sum(min(k, length - k) for k, length in zip(offset, lengths)) for offset in offsets
    }
    return sorted((offset for offset in offsets if any(offset)), key=lambda o: (-hops[o], o))


NEAR = (0, 1, 7)
X_ORDER = far_first(8, 4)
Y_ORDER = far_first(8, 2)


def roll(value, shift, axis):
    axis = axis % value.ndim
    return pltpu.roll(value, shift % value.shape[axis], axis)


def lane_of(shape):
    return lax.broadcasted_iota(jnp.int32, shape, len(shape) - 1)


def row_of(shape):
    return lax.broadcasted_iota(jnp.int32, shape, len(shape) - 2)


def five(value):
    return jnp.concatenate([value[0:1], value[1:2], value[1:2], value[1:2], value[2:3]])


def primitives(q):
    inv = 1.0 / q[0]
    u, v, w = q[1] * inv, q[2] * inv, q[3] * inv
    p = 0.4 * (q[4] - 0.5 * (q[1] * u + q[2] * v + q[3] * w))
    c2 = 1.4 * p * inv
    return inv, u, v, w, p, c2, c2 * lax.rsqrt(c2)


def up_y(value):
    here, after = value[..., 1:9, :, :], value[..., 2:10, :, :]
    return roll(jnp.where(lane_of(here.shape) < 32, after, here), -32, -1)


def down_y(value):
    before, here = value[..., 0:8, :, :], value[..., 1:9, :, :]
    return roll(jnp.where(lane_of(here.shape) >= 96, before, here), 32, -1)


def z_difference(value):
    z = lane_of(value.shape) & 31
    after = jnp.where(z == 31, roll(value, 31, -1), roll(value, -1, -1))
    before = jnp.where(z == 0, roll(value, -31, -1), roll(value, 1, -1))
    return after - before


def y_terms(q, prim):
    inv, u, v, w, p, c2, c = prim
    flux = 0.25 * jnp.stack([q[2], q[1] * v, q[2] * v + p, q[3] * v, v * (q[4] + p)])
    smooth = 400.0 * q
    return smooth - flux, smooth + flux, jnp.stack([v, c])


def z_terms(q, prim):
    inv, u, v, w, p, c2, c = prim
    flux = jnp.stack([q[3], q[1] * w, q[2] * w, q[3] * w + p, w * (q[4] + p)])
    return -1600.0 * q - 0.25 * z_difference(flux)


def x_terms(q, prim):
    inv, u, v, w, p, c2, c = prim
    flux = 0.25 * jnp.stack([q[1], q[1] * u + p, q[2] * u, q[3] * u, u * (q[4] + p)])
    smooth = 400.0 * q
    return smooth - flux, smooth + flux


def join(low, inner, high):
    return jnp.concatenate([low[:, None], inner, high[:, None]], axis=1)


def x_right(res, prim):
    inv, u, v, w, p, c2, c = prim
    kinetic = 0.5 * (u * u + v * v + w * w)
    dp = 0.4 * (res[4] - u * res[1] - v * res[2] - w * res[3] + kinetic * res[0])
    normal = c * (res[1] - u * res[0])
    return jnp.stack(
        [
            dp - normal,
            c2 * res[0] - dp,
            (res[2] - v * res[0]) * inv,
            (res[3] - w * res[0]) * inv,
            dp + normal,
        ]
    )


def eliminate(lower, upper, main_first, main_last):
    n = len(lower)
    m = [1.0 / main_first]
    g = [upper[0] * m[0]]
    p = [-lower[0] * m[0]]
    for k in range(1, n - 1):
        m.append(1.0 / (MAIN - lower[k] * g[k - 1]))
        g.append(upper[k] * m[k])
        p.append(-(lower[k] * p[k - 1]) * m[k])
    q = [None] * (n - 1)
    q[n - 2] = -g[n - 2]
    for k in range(n - 3, -1, -1):
        p[k] = p[k] - g[k] * p[k + 1]
        q[k] = -(g[k] * q[k + 1])
    last = 1.0 / (main_last + lower[n - 1] * q[n - 2])
    m.append(last)
    own = (-(lower[n - 1] * p[n - 2]) * last, -upper[n - 1] * last, p[0], q[0])
    return m, g, p, q, own


def eliminate_right(right, lower, m, g):
    n = len(right)
    d = [right[0] * five(m[0])]
    for k in range(1, n - 1):
        d.append((right[k] - five(lower[k]) * d[k - 1]) * five(m[k]))
    for k in range(n - 3, -1, -1):
        d[k] = d[k] - five(g[k]) * d[k + 1]
    last = (right[n - 1] - five(lower[n - 1]) * d[n - 2]) * five(m[n - 1])
    return d, last


def put_back(d, p, q, before, own):
    cells = [d[k] + five(p[k]) * before + five(q[k]) * own for k in range(len(d))]
    return cells + [own]


def factor(own):
    to_before, to_after, first_before, first_own = own
    rows = to_before.shape[-2]
    den = 1.0 / (1.0 - to_after * roll(first_before, -1, -2))
    a = to_before * den
    c = to_after * roll(first_own, -1, -2) * den
    return den, to_after * den, a, c


def factor_levels(a, c):
    rows = a.shape[-2]
    levels = []
    step = 1
    while step < rows:
        dn = 1.0 / (1.0 - a * roll(c, step, -2) - c * roll(a, -step, -2))
        an, cn = a * dn, c * dn
        levels.append((dn, an, cn))
        a, c = an * roll(a, step, -2), cn * roll(c, -step, -2)
        step *= 2
    return levels


def reduce_levels(d, levels):
    step = 1
    for dn, an, cn in levels:
        d = dn * d + an * roll(d, step, -2) + cn * roll(d, -step, -2)
        step *= 2
    return d


def y_right(s, rc, half_rc_inv):
    dp = 0.5 * (s[0] + s[4])
    normal = rc * s[2]
    return jnp.stack([dp - normal, s[1], (s[4] - s[0]) * half_rc_inv, s[3], dp + normal])


def swap_groups(value):
    lead = value.shape[:-3]
    half = value.reshape(*lead, 2, 2, 2, 8, 128)
    a, b = half[..., 0, :, :, :], half[..., 1, :, :, :]
    low = (lane_of(a.shape) & 64) == 0
    a, b = jnp.where(low, a, roll(b, 64, -1)), jnp.where(low, roll(a, 64, -1), b)
    half = jnp.stack([a, b], axis=len(lead) + 1)
    a, b = half[..., 0, :, :], half[..., 1, :, :]
    low = (lane_of(a.shape) & 32) == 0
    a, b = jnp.where(low, a, roll(b, 32, -1)), jnp.where(low, roll(a, -32, -1), b)
    half = jnp.stack([a, b], axis=len(lead) + 2)
    return half.reshape(*lead, 8, 8, 128)


def y_bands(speeds):
    vm, cm, vp, cp = (speeds[i].reshape(2, 4, 8, 128) for i in range(4))
    low = jnp.stack([vm - cm, vm, vm + cm])
    high = jnp.stack([vp - cp, vp, vp + cp])
    lower = [-0.25 * low[:, :, k] - 400.0 for k in range(4)]
    upper = [0.25 * high[:, :, k] - 400.0 for k in range(4)]
    return lower, upper


def y_join(own):
    row = row_of(own[0].shape)
    den, high, a, c = factor(own)
    p = jnp.where(row == 0, a, 0.0)
    q = jnp.where(row == 7, 1.0, 0.0)
    a = jnp.where((row == 0) | (row == 7), 0.0, a)
    c = jnp.where(row == 7, 0.0, c)
    levels = factor_levels(a, c)
    p = reduce_levels(p, levels)
    q = reduce_levels(q, levels)
    last = 1.0 / (1.0 - own[0] * roll(q, 1, -2))
    joined = (
        own[0] * roll(p, 1, -2) * last,
        own[1] * last,
        own[2] + own[3] * p,
        own[3] * q,
    )
    return den, high, levels, p, q, last, joined


def y_join_right(d0, last_right, own, den, high, levels, last):
    row = row_of(last_right.shape)
    d = five(den) * last_right + five(high) * roll(d0, -1, -2)
    d = jnp.where(row == 7, 0.0, d)
    d = reduce_levels(d, [tuple(five(part) for part in level) for level in levels])
    joined_last = (last_right + five(own[0]) * roll(d, 1, -2)) * five(last)
    joined_first = d0 + five(own[3]) * d
    return d, joined_last, joined_first


def y_weights(segments):
    n = len(segments)
    ones = jnp.ones_like(segments[0][0])
    zero = jnp.zeros_like(ones)
    den, high, a, c = [], [], [], []
    for j, (to_before, to_after, _, _) in enumerate(segments):
        after = segments[j + 1] if j < n - 1 else (zero,) * 4
        den.append(1.0 / (1.0 - to_after * after[2]))
        high.append(to_after * den[j])
        a.append(to_before * den[j])
        c.append(high[j] * after[3])
    left, right = [None] * n, [None] * n
    for j in range(n):
        left[j] = c[j] / (1.0 - a[j] * left[j - 1]) if j else c[j]
    for j in range(n - 1, -1, -1):
        right[j] = a[j] / (1.0 - c[j] * right[j + 1]) if j < n - 1 else a[j]
    gain = []
    for j in range(n):
        rest = ones
        rest = rest - a[j] * left[j - 1] if j else rest
        rest = rest - c[j] * right[j + 1] if j < n - 1 else rest
        gain.append(1.0 / rest)
    down, up = [ones] * n, [ones] * n
    for j in range(1, n):
        down[j] = down[j - 1] * right[j]
    for j in range(n - 2, -1, -1):
        up[j] = up[j + 1] * left[j]
    weights = []
    for j in range(n):
        own_last = gain[j] * den[j]
        own_first = right[j] * gain[j - 1] * high[j - 1] if j else zero
        before_last = left[j - 1] * own_last if j else zero
        before_first = gain[j - 1] * high[j - 1] if j else zero
        down_inv = 1.0 / down[j]
        up_inv = 1.0 / up[j - 1] if j else ones
        weights.append(
            (
                own_last,
                own_first,
                before_last,
                before_first,
                down_inv,
                up_inv,
                down[j - 1] if j else zero,
                up[j],
                right[j],
                left[j - 1] if j else zero,
            )
        )
    return weights


def y_emit(last, first, w):
    own = w[0] * last + w[1] * first
    before = w[2] * last + w[3] * first
    return own, before, own * w[4], before * w[5]


def y_meet(below, above, own, before, w):
    low, high = w[6] * below, w[7] * above
    return low + w[9] * high + before, w[8] * low + own + high


def increments(s, prim, r, half_rc_inv, c2_inv):
    inv, u, v, w, p, c2, c = prim
    dp = 0.5 * (s[0] + s[4])
    dv = (s[4] - s[0]) * half_rc_inv
    dr = (s[1] + dp) * c2_inv
    du, dw = s[2], s[3]
    kinetic = 0.5 * (u * u + v * v + w * w)
    return (
        dr,
        u * dr + r * du,
        v * dr + r * dv,
        w * dr + r * dw,
        kinetic * dr + r * (u * du + v * dv + w * dw) + 2.5 * dp,
    )


def x_code_mask(codes, side):
    ones = (codes[side : side + 1] == 1).astype(jnp.float32)
    spread = jnp.where((lane_of((8, 32)) >> 2) == row_of((8, 32)), ones, 0.0)
    place = jnp.where((row_of((32, 128)) & 3) == (lane_of((32, 128)) >> 5), 1.0, 0.0)
    return jnp.dot(spread, place, preferred_element_type=jnp.float32) > 0.5


def y_code_mask(codes, side):
    ones = jnp.broadcast_to((codes[side : side + 1] == 1).astype(jnp.float32), (8, 8))
    halves = []
    for h in range(2):
        place = jnp.where(row_of((8, 128)) == 4 * h + (lane_of((8, 128)) >> 5), 1.0, 0.0)
        halves.append(jnp.dot(ones, place, preferred_element_type=jnp.float32))
    return jnp.stack(halves) > 0.5


def x_bands(u, c, codes, start, end):
    lam = jnp.stack([u - c, u, u + c])
    lower = [-0.25 * lam[:, k] - 400.0 for k in range(8)]
    upper = [0.25 * lam[:, k + 2] - 400.0 for k in range(8)]
    first = MAIN + jnp.where(x_code_mask(codes, 0)[None] & start, lower[0], 0.0)
    last = MAIN + jnp.where(x_code_mask(codes, 1)[None] & end, upper[7], 0.0)
    lower[0] = jnp.where(start, 0.0, lower[0])
    upper[7] = jnp.where(end, 0.0, upper[7])
    return lower, upper, first, last


def y_ends(lower, upper, codes, start, end):
    row = row_of(lower[0].shape)
    at_start = (row == 0) & start
    at_end = (row == 7) & end
    first = MAIN + jnp.where(at_start & y_code_mask(codes, 0)[None], lower[0], 0.0)
    last = MAIN + jnp.where(at_end & y_code_mask(codes, 1)[None], upper[3], 0.0)
    lower, upper = list(lower), list(upper)
    lower[0] = jnp.where(at_start, 0.0, lower[0])
    upper[3] = jnp.where(at_end, 0.0, upper[3])
    return lower, upper, first, last


def wait_all(ref, sem):
    pltpu.make_async_copy(ref, ref, sem).wait()


def kernel(
    flow,
    x_codes,
    y_codes,
    out,
    q_sc,
    part_sc,
    speed_sc,
    x_send,
    x_low,
    x_high,
    y_low,
    y_high,
    xm_out,
    xr_out,
    xm_in,
    xr_in,
    xs_out,
    xs_in,
    ym_out,
    ym_in,
    y_weight_sc,
    y_weight,
    yr_sc,
    yf_out,
    yc_in,
    yb_out,
    yf_in,
    ys_sc,
    x_code_sc,
    y_code_sc,
    word,
    in_sem,
    code_sem,
    halo_send,
    halo_recv,
    send_sem,
    recv_sem,
):
    gx, gy = lax.axis_index("gx"), lax.axis_index("gy")
    start_x, end_x = gx == 0, gx == SX - 1
    start_y, end_y = gy == 0, gy == SY - 1

    chip_y, chip_x = lax.div(gx, 4), lax.rem(gx, 4)
    chip_z, core = lax.div(gy, 2), lax.rem(gy, 2)
    x_after, x_before = lax.rem(gx + 1, SX), lax.rem(gx + SX - 1, SX)
    y_after, y_before = lax.rem(gy + 1, SY), lax.rem(gy + SY - 1, SY)

    def x_at(dy, dx):
        return 4 * lax.rem(chip_y + dy, 8) + lax.rem(chip_x + dx, 4), gy

    def y_at(dz, dc):
        return gx, 2 * lax.rem(chip_z + dz, 8) + lax.rem(core + dc, 2)

    near = [x_at(dy, dx) for dy, dx in X_ORDER if dy in NEAR]
    near += [y_at(dz, dc) for dz, dc in Y_ORDER if dz in NEAR]
    barrier = pltpu.get_barrier_semaphore()
    for device in near:
        pl.semaphore_signal(barrier, inc=1, device_id=device, device_id_type=MESH)

    for b in range(8):
        pltpu.make_async_copy(
            flow.at[:, :, pl.ds(128 * b, 128)], q_sc.at[:, pl.ds(8 * b, 8), :], in_sem
        ).start()
    code_copies = [
        pltpu.make_async_copy(x_codes, x_code_sc, code_sem.at[0]),
        pltpu.make_async_copy(y_codes, y_code_sc, code_sem.at[1]),
    ]
    for copy in code_copies:
        copy.start()

    def tell(step):
        for k in (step + 1, 7 - step):
            for device in (x_at(k, 0), y_at(k, 0)):
                pl.semaphore_signal(word.at[step], inc=1, device_id=device, device_id_type=MESH)

    def heard(step):
        pl.semaphore_wait(word.at[step], 4)

    pl.semaphore_wait(barrier, len(near))
    tell(0)
    wait_all(q_sc, in_sem)
    for copy in code_copies:
        copy.wait()

    x_send[0] = q_sc[:, pl.ds(7, 8, stride=8), :]
    x_send[1] = q_sc[:, pl.ds(0, 8, stride=8), :]
    halos = [
        (x_send.at[0], x_low, (x_after, gy)),
        (x_send.at[1], x_high, (x_before, gy)),
        (q_sc.at[:, pl.ds(56, 8), :], y_low, (gx, y_after)),
        (q_sc.at[:, pl.ds(0, 8), :], y_high, (gx, y_before)),
    ]
    copies = []
    for i, (source, target, device) in enumerate(halos):
        copy = pltpu.make_async_remote_copy(
            src_ref=source,
            dst_ref=target,
            send_sem=halo_send.at[i],
            recv_sem=halo_recv.at[i],
            device_id=device,
            device_id_type=MESH,
        )
        copy.start()
        copies.append(copy)
    heard(0)
    tell(1)

    two_families = lax.div(gx, 8) == 2

    def by_rows(two, act):
        @pl.when(two)
        def _():
            act(4)

        @pl.when(jnp.logical_not(two))
        def _():
            act(2)

    def send_x(source, target, slot):
        def own(rows):
            mine = pl.ds(gx * 4, rows)
            pltpu.make_async_copy(source.at[mine], target.at[mine], recv_sem.at[slot]).start()

        def one(other, rows):
            pltpu.make_async_remote_copy(
                src_ref=source.at[pl.ds(other * 4, rows)],
                dst_ref=target.at[pl.ds(gx * 4, rows)],
                send_sem=send_sem.at[slot],
                recv_sem=recv_sem.at[slot],
                device_id=(other, gy),
                device_id_type=MESH,
            ).start()

        others = [x_at(dy, dx)[0] for dy, dx in X_ORDER]
        if slot == 0:
            own(4)
            for other in others:
                one(other, 4)
        elif slot == 1:
            by_rows(two_families, own)
            for other in others:
                by_rows(lax.div(other, 8) == 2, functools.partial(one, other))
        else:

            def all_of(rows):
                own(rows)
                for other in others:
                    one(other, rows)

            by_rows(two_families, all_of)

    def others_y():
        for dz, dc in Y_ORDER:
            yield 2 * lax.rem(lax.div(gy, 2) + dz, 8) + lax.rem(lax.rem(gy, 2) + dc, 2)

    blocks = q_sc[...].reshape(5, 8, 8, 128)
    prim_o = primitives(blocks)
    to_before_y, to_after_y, speeds_y = y_terms(blocks, prim_o)
    part_z = z_terms(blocks, prim_o)
    q = jnp.stack([q_sc[:, pl.ds(k, 8, stride=8), :] for k in range(8)], axis=1)
    prim = primitives(q)
    to_before_x, to_after_x = x_terms(q, prim)

    for copy in copies:
        copy.wait_recv()
    low = jnp.where(start_x, q[:, 0], x_low[...])
    high = jnp.where(end_x, q[:, 7], x_high[...])
    prim_low, prim_high = primitives(low), primitives(high)
    u, c = (
        jnp.concatenate([prim_low[i][None], prim[i], prim_high[i][None]]) for i in (1, 6)
    )

    lower, upper, first, last = x_bands(u, c, x_code_sc[...], start_x, end_x)
    xm, xg, xp, xq, x_own = eliminate(lower, upper, first, last)
    for group, (matrix, families) in enumerate(GROUPS):
        for row in range(4):
            xm_out[pl.ds(group * 32 + row, 8, stride=4), :] = x_own[row][matrix]
    heard(1)
    send_x(xm_out, xm_in, 0)

    y_edge_low = jnp.where(start_y, roll(blocks[:, 0], 96, -1), y_low[...])
    y_edge_high = jnp.where(end_y, roll(blocks[:, 7], 32, -1), y_high[...])
    low_terms = y_terms(y_edge_low, primitives(y_edge_low))
    high_terms = y_terms(y_edge_high, primitives(y_edge_high))
    part = (
        up_y(join(low_terms[0], to_before_y, high_terms[0]))
        + down_y(join(low_terms[1], to_after_y, high_terms[1]))
        + part_z
    )
    part_sc[...] = part.reshape(5, 64, 128)
    residual = (
        jnp.concatenate([to_before_x[:, 1:], x_terms(high, prim_high)[0][:, None]], axis=1)
        + jnp.concatenate([x_terms(low, prim_low)[1][:, None], to_after_x[:, :7]], axis=1)
        + jnp.stack([part_sc[:, pl.ds(k, 8, stride=8), :] for k in range(8)], axis=1)
    )
    right = x_right(residual, prim)
    xd, x_last = eliminate_right([right[:, k] for k in range(8)], lower, xm, xg)
    zero = jnp.zeros((8, 128), jnp.float32)
    for group, (matrix, families) in enumerate(GROUPS):
        for i in range(2):
            at = group * 32 + 2 * i
            some = i < len(families)
            xr_out[pl.ds(at, 8, stride=4), :] = x_last[families[i]] if some else zero
            xr_out[pl.ds(at + 1, 8, stride=4), :] = xd[0][families[i]] if some else zero
    send_x(xr_out, xr_in, 1)

    speeds_y = join(low_terms[2], speeds_y, high_terms[2])
    speed_sc[...] = jnp.concatenate([down_y(speeds_y), up_y(speeds_y)]).reshape(4, 64, 128)
    speeds = jnp.stack([speed_sc[:, pl.ds(k, 8, stride=8), :] for k in range(8)], axis=1)
    y_lower, y_upper = y_bands(swap_groups(speeds))
    y_lower, y_upper, first, last = y_ends(y_lower, y_upper, y_code_sc[...], start_y, end_y)
    ym, yg, yp, yq, y_own = eliminate(y_lower, y_upper, first, last)
    y_den, y_high_part, y_lev, y_p, y_q, y_joint, joined = y_join(y_own)
    ym_out[...] = jnp.zeros((32, 128), jnp.float32)
    for kind in range(4):
        line = 7 if kind < 2 else 0
        for matrix in range(3):
            for h in range(2):
                at = kind * 8 + matrix * 2 + h
                ym_out[pl.ds(at, 1), :] = joined[kind][matrix, h, line : line + 1]
    pltpu.make_async_copy(ym_out, ym_in.at[gy], recv_sem.at[3]).start()
    for other in others_y():
        pltpu.make_async_remote_copy(
            src_ref=ym_out,
            dst_ref=ym_in.at[gy],
            send_sem=send_sem.at[3],
            recv_sem=recv_sem.at[3],
            device_id=(gx, other),
            device_id_type=MESH,
        ).start()

    wait_all(xm_in, recv_sem.at[0])
    den, high_part, a, c = factor([xm_in[pl.ds(row, SX, stride=4), :] for row in range(4)])
    levels = factor_levels(a, c)
    by_rows(two_families, lambda rows: wait_all(xr_in.at[pl.ds(0, SX * rows)], recv_sem.at[1]))
    for i in range(2):
        own_last = xr_in[pl.ds(2 * i, SX, stride=4), :]
        own_first = xr_in[pl.ds(2 * i + 1, SX, stride=4), :]
        d = den * own_last + high_part * roll(own_first, -1, 0)
        d = reduce_levels(d, levels)
        xs_out[pl.ds(2 * i, SX, stride=4), :] = roll(d, 1, 0)
        xs_out[pl.ds(2 * i + 1, SX, stride=4), :] = d
    send_x(xs_out, xs_in, 2)

    wait_all(ym_in, recv_sem.at[3])
    segments = [
        tuple(ym_in[j, pl.ds(8 * kind, 8), :] for kind in range(4)) for j in range(SY)
    ]
    for j, weights in enumerate(y_weights(segments)):
        for i, weight in enumerate(weights):
            y_weight_sc[j, i] = weight
    for i in range(10):
        for family, matrix in enumerate((0, 1, 1, 1, 2)):
            y_weight[i, pl.ds(2 * family, 2), :] = y_weight_sc[gy, i, pl.ds(2 * matrix, 2), :]

    r = q[0]
    rc = r * prim[6]
    half_rc_inv = 0.5 / rc
    c2_inv = 1.0 / prim[5]

    wait_all(xs_in.at[pl.ds(0, 80)], recv_sem.at[2])

    def x_value(kind):
        rows = []
        for group, i in ((0, 0), (2, 0), (2, 1), (3, 0), (1, 0)):
            rows.append(xs_in[pl.ds(group * 32 + 2 * i + kind, 8, stride=4), :])
        return jnp.stack(rows)

    solved = jnp.stack(put_back(xd, xp, xq, x_value(0), x_value(1)), axis=1)
    right = swap_groups(y_right(solved, rc, half_rc_inv)).reshape(5, 2, 4, 8, 128)
    yd, y_last = eliminate_right([right[:, :, k] for k in range(4)], y_lower, ym, yg)
    y_d, joined_last, joined_first = y_join_right(
        yd[0], y_last, y_own, y_den, y_high_part, y_lev, y_joint
    )
    for family in range(5):
        for h in range(2):
            yr_sc[0, pl.ds(2 * family + h, 1), :] = joined_last[family, h, 7:8]
            yr_sc[1, pl.ds(2 * family + h, 1), :] = joined_first[family, h, 0:1]
    weights = [y_weight[i] for i in range(10)]
    own_add, before_add, own_out, before_out = y_emit(yr_sc[0], yr_sc[1], weights)
    yf_out[0], yf_out[1] = own_out, before_out
    core_copy = pltpu.make_async_remote_copy(
        src_ref=yf_out.at[:, pl.ds(0, 10)],
        dst_ref=yc_in.at[:, pl.ds(0, 10)],
        send_sem=send_sem.at[5],
        recv_sem=recv_sem.at[5],
        device_id=(gx, 2 * chip_z + 1 - core),
        device_id_type=MESH,
    )
    core_copy.start()
    core_copy.wait_recv()
    yb_out[0], yb_out[1] = own_out + yc_in[0], before_out + yc_in[1]
    for dz, dc in Y_ORDER:
        if dc == 0:
            other = lax.rem(chip_z + dz, 8)
            pltpu.make_async_remote_copy(
                src_ref=yb_out.at[jnp.where(other < chip_z, 1, 0), pl.ds(0, 10)],
                dst_ref=yf_in.at[chip_z, pl.ds(0, 10)],
                send_sem=send_sem.at[4],
                recv_sem=recv_sem.at[4],
                device_id=(gx, 2 * other + core),
                device_id_type=MESH,
            ).start()
    below = jnp.where(core == 1, yc_in[0], 0.0)
    above = jnp.where(core == 0, yc_in[1], 0.0)
    wait_all(yf_in.at[pl.ds(0, 7), pl.ds(0, 10)], recv_sem.at[4])
    for j in range(8):
        below = below + jnp.where(j < chip_z, yf_in[j], 0.0)
        above = above + jnp.where(j > chip_z, yf_in[j], 0.0)
    ys_sc[0], ys_sc[1] = y_meet(below, above, own_add, before_add, weights)

    def y_value(kind):
        return jnp.stack(
            [
                jnp.stack([ys_sc[kind, pl.ds(2 * family + h, 1), :] for h in range(2)])
                for family in range(5)
            ]
        )

    before, own = y_value(0), y_value(1)
    groups = y_d + five(y_p) * before + five(y_q) * own
    previous = jnp.where(row_of(groups.shape) == 0, before, roll(groups, 1, -2))
    solved = jnp.stack(put_back(yd, yp, yq, previous, groups), axis=2)
    solved = swap_groups(solved.reshape(5, 8, 8, 128))
    for field, value in enumerate(increments(solved, prim, r, half_rc_inv, c2_inv)):
        for k in range(8):
            out[field, pl.ds(k, 8, stride=8), :] = value[k]

    for copy in copies:
        copy.wait_send()
    wait_all(xm_out.at[pl.ds(0, 4 * (SX - 1))], send_sem.at[0])
    by_rows(two_families, lambda rows: wait_all(xr_out.at[pl.ds(0, 80 - rows)], send_sem.at[1]))
    by_rows(
        two_families, lambda rows: wait_all(xs_out.at[pl.ds(0, (SX - 1) * rows)], send_sem.at[2])
    )
    wait_all(ym_in.at[pl.ds(0, SY - 1)], send_sem.at[3])
    wait_all(yf_in.at[pl.ds(0, 7), pl.ds(0, 10)], send_sem.at[4])
    core_copy.wait_send()


def local(flow_state, x_codes, y_codes):
    f32 = jnp.float32

    def vmem(*shape):
        return pltpu.VMEM(shape, f32)

    result = pl.pallas_call(
        kernel,
        out_shape=jax.ShapeDtypeStruct((5, 64, 128), f32),
        in_specs=[pl.BlockSpec(memory_space=pltpu.HBM)] * 3,
        out_specs=pl.BlockSpec(memory_space=pltpu.VMEM),
        scratch_shapes=[
            vmem(5, 64, 128),
            vmem(5, 64, 128),
            vmem(4, 64, 128),
            vmem(2, 5, 8, 128),
            vmem(5, 8, 128),
            vmem(5, 8, 128),
            vmem(5, 8, 128),
            vmem(5, 8, 128),
            vmem(4 * SX, 128),
            vmem(4 * SX, 128),
            vmem(4 * SX, 128),
            vmem(4 * SX, 128),
            vmem(4 * SX, 128),
            vmem(4 * SX, 128),
            vmem(32, 128),
            vmem(SY, 32, 128),
            vmem(SY, 10, 8, 128),
            vmem(10, 16, 128),
            vmem(2, 16, 128),
            vmem(2, 16, 128),
            vmem(2, 16, 128),
            vmem(2, 16, 128),
            vmem(8, 16, 128),
            vmem(2, 16, 128),
            pltpu.VMEM((2, 32), jnp.int32),
            pltpu.VMEM((2, 8), jnp.int32),
            pltpu.SemaphoreType.REGULAR((2,)),
            pltpu.SemaphoreType.DMA,
            pltpu.SemaphoreType.DMA((2,)),
            pltpu.SemaphoreType.DMA((4,)),
            pltpu.SemaphoreType.DMA((4,)),
            pltpu.SemaphoreType.DMA((6,)),
            pltpu.SemaphoreType.DMA((6,)),
        ],
        compiler_params=pltpu.CompilerParams(
            collective_id=0, has_side_effects=True, vmem_limit_bytes=VMEM_LIMIT
        ),
        name="step",
    )(*(pltpu.with_memory_space_constraint(v, pltpu.HBM) for v in (flow_state, x_codes, y_codes)))
    result = jnp.transpose(result.reshape(5, 8, 8, 128), (0, 2, 1, 3))
    return result.reshape(flow_state.shape)


def solution(mesh):
    return jax.shard_map(
        local,
        mesh=mesh,
        in_specs=(P(None, "gx", "gy"), P(None, "gy"), P(None, "gx")),
        out_specs=P(None, "gx", "gy"),
        check_vma=False,
    )
```

```python
import functools

import jax
import jax.numpy as jnp
from jax import lax
from jax.experimental import pallas as pl
from jax.experimental.pallas import tpu as pltpu
from jax.sharding import PartitionSpec as P

NZ = 32
SX = 32
SY = 16
VMEM_LIMIT = 32 * 1024 * 1024
MAIN = 801.0
GROUPS = ((0, (0,)), (2, (4,)), (1, (1, 2)), (1, (3,)))
MESH = pl.DeviceIdType.MESH


def far_first(*lengths):
    offsets = [()]
    for length in lengths:
        offsets = [(*offset, k) for offset in offsets for k in range(length)]
    hops = {
        offset: sum(min(k, length - k) for k, length in zip(offset, lengths)) for offset in offsets
    }
    return sorted((offset for offset in offsets if any(offset)), key=lambda o: (-hops[o], o))


NEAR = (0, 1, 7)
X_ORDER = far_first(8, 4)
Y_ORDER = far_first(8, 2)


def roll(value, shift, axis):
    axis = axis % value.ndim
    return pltpu.roll(value, shift % value.shape[axis], axis)


def lane_of(shape):
    return lax.broadcasted_iota(jnp.int32, shape, len(shape) - 1)


def row_of(shape):
    return lax.broadcasted_iota(jnp.int32, shape, len(shape) - 2)


def five(value):
    return jnp.concatenate([value[0:1], value[1:2], value[1:2], value[1:2], value[2:3]])


def primitives(q):
    inv = 1.0 / q[0]
    u, v, w = q[1] * inv, q[2] * inv, q[3] * inv
    p = 0.4 * (q[4] - 0.5 * (q[1] * u + q[2] * v + q[3] * w))
    c2 = 1.4 * p * inv
    return inv, u, v, w, p, c2, c2 * lax.rsqrt(c2)


def up_y(value):
    here, after = value[..., 1:9, :, :], value[..., 2:10, :, :]
    return roll(jnp.where(lane_of(here.shape) < 32, after, here), -32, -1)


def down_y(value):
    before, here = value[..., 0:8, :, :], value[..., 1:9, :, :]
    return roll(jnp.where(lane_of(here.shape) >= 96, before, here), 32, -1)


def z_difference(value):
    z = lane_of(value.shape) & 31
    after = jnp.where(z == 31, roll(value, 31, -1), roll(value, -1, -1))
    before = jnp.where(z == 0, roll(value, -31, -1), roll(value, 1, -1))
    return after - before


def y_terms(q, prim):
    inv, u, v, w, p, c2, c = prim
    flux = 0.25 * jnp.stack([q[2], q[1] * v, q[2] * v + p, q[3] * v, v * (q[4] + p)])
    smooth = 400.0 * q
    return smooth - flux, smooth + flux, jnp.stack([v, c])


def z_terms(q, prim):
    inv, u, v, w, p, c2, c = prim
    flux = jnp.stack([q[3], q[1] * w, q[2] * w, q[3] * w + p, w * (q[4] + p)])
    return -1600.0 * q - 0.25 * z_difference(flux)


def x_terms(q, prim):
    inv, u, v, w, p, c2, c = prim
    flux = 0.25 * jnp.stack([q[1], q[1] * u + p, q[2] * u, q[3] * u, u * (q[4] + p)])
    smooth = 400.0 * q
    return smooth - flux, smooth + flux


def join(low, inner, high):
    return jnp.concatenate([low[:, None], inner, high[:, None]], axis=1)


def x_right(res, prim):
    inv, u, v, w, p, c2, c = prim
    kinetic = 0.5 * (u * u + v * v + w * w)
    dp = 0.4 * (res[4] - u * res[1] - v * res[2] - w * res[3] + kinetic * res[0])
    normal = c * (res[1] - u * res[0])
    return jnp.stack(
        [
            dp - normal,
            c2 * res[0] - dp,
            (res[2] - v * res[0]) * inv,
            (res[3] - w * res[0]) * inv,
            dp + normal,
        ]
    )


def eliminate(lower, upper, main_first, main_last):
    n = len(lower)
    m = [1.0 / main_first]
    g = [upper[0] * m[0]]
    p = [-lower[0] * m[0]]
    for k in range(1, n - 1):
        m.append(1.0 / (MAIN - lower[k] * g[k - 1]))
        g.append(upper[k] * m[k])
        p.append(-(lower[k] * p[k - 1]) * m[k])
    q = [None] * (n - 1)
    q[n - 2] = -g[n - 2]
    for k in range(n - 3, -1, -1):
        p[k] = p[k] - g[k] * p[k + 1]
        q[k] = -(g[k] * q[k + 1])
    last = 1.0 / (main_last + lower[n - 1] * q[n - 2])
    m.append(last)
    own = (-(lower[n - 1] * p[n - 2]) * last, -upper[n - 1] * last, p[0], q[0])
    return m, g, p, q, own


def eliminate_right(right, lower, m, g):
    n = len(right)
    d = [right[0] * five(m[0])]
    for k in range(1, n - 1):
        d.append((right[k] - five(lower[k]) * d[k - 1]) * five(m[k]))
    for k in range(n - 3, -1, -1):
        d[k] = d[k] - five(g[k]) * d[k + 1]
    last = (right[n - 1] - five(lower[n - 1]) * d[n - 2]) * five(m[n - 1])
    return d, last


def put_back(d, p, q, before, own):
    cells = [d[k] + five(p[k]) * before + five(q[k]) * own for k in range(len(d))]
    return cells + [own]


def factor(own):
    to_before, to_after, first_before, first_own = own
    rows = to_before.shape[-2]
    den = 1.0 / (1.0 - to_after * roll(first_before, -1, -2))
    a = to_before * den
    c = to_after * roll(first_own, -1, -2) * den
    return den, to_after * den, a, c


def factor_levels(a, c):
    rows = a.shape[-2]
    levels = []
    step = 1
    while step < rows:
        dn = 1.0 / (1.0 - a * roll(c, step, -2) - c * roll(a, -step, -2))
        an, cn = a * dn, c * dn
        levels.append((dn, an, cn))
        a, c = an * roll(a, step, -2), cn * roll(c, -step, -2)
        step *= 2
    return levels


def reduce_levels(d, levels):
    step = 1
    for dn, an, cn in levels:
        d = dn * d + an * roll(d, step, -2) + cn * roll(d, -step, -2)
        step *= 2
    return d


def y_right(s, rc, half_rc_inv):
    dp = 0.5 * (s[0] + s[4])
    normal = rc * s[2]
    return jnp.stack([dp - normal, s[1], (s[4] - s[0]) * half_rc_inv, s[3], dp + normal])


def swap_groups(value):
    lead = value.shape[:-3]
    half = value.reshape(*lead, 2, 2, 2, 8, 128)
    a, b = half[..., 0, :, :, :], half[..., 1, :, :, :]
    low = (lane_of(a.shape) & 64) == 0
    a, b = jnp.where(low, a, roll(b, 64, -1)), jnp.where(low, roll(a, 64, -1), b)
    half = jnp.stack([a, b], axis=len(lead) + 1)
    a, b = half[..., 0, :, :], half[..., 1, :, :]
    low = (lane_of(a.shape) & 32) == 0
    a, b = jnp.where(low, a, roll(b, 32, -1)), jnp.where(low, roll(a, -32, -1), b)
    half = jnp.stack([a, b], axis=len(lead) + 2)
    return half.reshape(*lead, 8, 8, 128)


def y_bands(speeds):
    vm, cm, vp, cp = (speeds[i].reshape(2, 4, 8, 128) for i in range(4))
    low = jnp.stack([vm - cm, vm, vm + cm])
    high = jnp.stack([vp - cp, vp, vp + cp])
    lower = [-0.25 * low[:, :, k] - 400.0 for k in range(4)]
    upper = [0.25 * high[:, :, k] - 400.0 for k in range(4)]
    return lower, upper


def y_join(own):
    row = row_of(own[0].shape)
    den, high, a, c = factor(own)
    p = jnp.where(row == 0, a, 0.0)
    q = jnp.where(row == 7, 1.0, 0.0)
    a = jnp.where((row == 0) | (row == 7), 0.0, a)
    c = jnp.where(row == 7, 0.0, c)
    levels = factor_levels(a, c)
    p = reduce_levels(p, levels)
    q = reduce_levels(q, levels)
    last = 1.0 / (1.0 - own[0] * roll(q, 1, -2))
    joined = (
        own[0] * roll(p, 1, -2) * last,
        own[1] * last,
        own[2] + own[3] * p,
        own[3] * q,
    )
    return den, high, levels, p, q, last, joined


def y_join_right(d0, last_right, own, den, high, levels, last):
    row = row_of(last_right.shape)
    d = five(den) * last_right + five(high) * roll(d0, -1, -2)
    d = jnp.where(row == 7, 0.0, d)
    d = reduce_levels(d, [tuple(five(part) for part in level) for level in levels])
    joined_last = (last_right + five(own[0]) * roll(d, 1, -2)) * five(last)
    joined_first = d0 + five(own[3]) * d
    return d, joined_last, joined_first


def y_weights(segments):
    n = len(segments)
    ones = jnp.ones_like(segments[0][0])
    zero = jnp.zeros_like(ones)
    den, high, a, c = [], [], [], []
    for j, (to_before, to_after, _, _) in enumerate(segments):
        after = segments[j + 1] if j < n - 1 else (zero,) * 4
        den.append(1.0 / (1.0 - to_after * after[2]))
        high.append(to_after * den[j])
        a.append(to_before * den[j])
        c.append(high[j] * after[3])
    left, right = [None] * n, [None] * n
    for j in range(n):
        left[j] = c[j] / (1.0 - a[j] * left[j - 1]) if j else c[j]
    for j in range(n - 1, -1, -1):
        right[j] = a[j] / (1.0 - c[j] * right[j + 1]) if j < n - 1 else a[j]
    gain = []
    for j in range(n):
        rest = ones
        rest = rest - a[j] * left[j - 1] if j else rest
        rest = rest - c[j] * right[j + 1] if j < n - 1 else rest
        gain.append(1.0 / rest)
    down, up = [ones] * n, [ones] * n
    for j in range(1, n):
        down[j] = down[j - 1] * right[j]
    for j in range(n - 2, -1, -1):
        up[j] = up[j + 1] * left[j]
    weights = []
    for j in range(n):
        own_last = gain[j] * den[j]
        own_first = right[j] * gain[j - 1] * high[j - 1] if j else zero
        before_last = left[j - 1] * own_last if j else zero
        before_first = gain[j - 1] * high[j - 1] if j else zero
        down_inv = 1.0 / down[j]
        up_inv = 1.0 / up[j - 1] if j else ones
        weights.append(
            (
                own_last,
                own_first,
                before_last,
                before_first,
                down_inv,
                up_inv,
                down[j - 1] if j else zero,
                up[j],
                right[j],
                left[j - 1] if j else zero,
            )
        )
    return weights


def y_emit(last, first, w):
    own = w[0] * last + w[1] * first
    before = w[2] * last + w[3] * first
    return own, before, own * w[4], before * w[5]


def y_meet(below, above, own, before, w):
    low, high = w[6] * below, w[7] * above
    return low + w[9] * high + before, w[8] * low + own + high


def increments(s, prim, r, half_rc_inv, c2_inv):
    inv, u, v, w, p, c2, c = prim
    dp = 0.5 * (s[0] + s[4])
    dv = (s[4] - s[0]) * half_rc_inv
    dr = (s[1] + dp) * c2_inv
    du, dw = s[2], s[3]
    kinetic = 0.5 * (u * u + v * v + w * w)
    return (
        dr,
        u * dr + r * du,
        v * dr + r * dv,
        w * dr + r * dw,
        kinetic * dr + r * (u * du + v * dv + w * dw) + 2.5 * dp,
    )


def x_code_mask(codes, side):
    ones = (codes[side : side + 1] == 1).astype(jnp.float32)
    spread = jnp.where((lane_of((8, 32)) >> 2) == row_of((8, 32)), ones, 0.0)
    place = jnp.where((row_of((32, 128)) & 3) == (lane_of((32, 128)) >> 5), 1.0, 0.0)
    return jnp.dot(spread, place, preferred_element_type=jnp.float32) > 0.5


def y_code_mask(codes, side):
    ones = jnp.broadcast_to((codes[side : side + 1] == 1).astype(jnp.float32), (8, 8))
    halves = []
    for h in range(2):
        place = jnp.where(row_of((8, 128)) == 4 * h + (lane_of((8, 128)) >> 5), 1.0, 0.0)
        halves.append(jnp.dot(ones, place, preferred_element_type=jnp.float32))
    return jnp.stack(halves) > 0.5


def x_bands(u, c, codes, start, end):
    lam = jnp.stack([u - c, u, u + c])
    lower = [-0.25 * lam[:, k] - 400.0 for k in range(8)]
    upper = [0.25 * lam[:, k + 2] - 400.0 for k in range(8)]
    first = MAIN + jnp.where(x_code_mask(codes, 0)[None] & start, lower[0], 0.0)
    last = MAIN + jnp.where(x_code_mask(codes, 1)[None] & end, upper[7], 0.0)
    lower[0] = jnp.where(start, 0.0, lower[0])
    upper[7] = jnp.where(end, 0.0, upper[7])
    return lower, upper, first, last


def y_ends(lower, upper, codes, start, end):
    row = row_of(lower[0].shape)
    at_start = (row == 0) & start
    at_end = (row == 7) & end
    first = MAIN + jnp.where(at_start & y_code_mask(codes, 0)[None], lower[0], 0.0)
    last = MAIN + jnp.where(at_end & y_code_mask(codes, 1)[None], upper[3], 0.0)
    lower, upper = list(lower), list(upper)
    lower[0] = jnp.where(at_start, 0.0, lower[0])
    upper[3] = jnp.where(at_end, 0.0, upper[3])
    return lower, upper, first, last


def wait_all(ref, sem):
    pltpu.make_async_copy(ref, ref, sem).wait()


def kernel(
    flow,
    x_codes,
    y_codes,
    out,
    q_sc,
    part_sc,
    speed_sc,
    x_send,
    x_low,
    x_high,
    y_low,
    y_high,
    xm_out,
    xr_out,
    xm_in,
    xr_in,
    xs_out,
    xs_in,
    ym_out,
    ym_in,
    y_weight_sc,
    y_weight,
    yr_sc,
    yf_out,
    yc_in,
    yb_out,
    yf_in,
    ys_sc,
    x_code_sc,
    y_code_sc,
    word,
    in_sem,
    code_sem,
    halo_send,
    halo_recv,
    send_sem,
    recv_sem,
):
    gx, gy = lax.axis_index("gx"), lax.axis_index("gy")
    start_x, end_x = gx == 0, gx == SX - 1
    start_y, end_y = gy == 0, gy == SY - 1

    chip_y, chip_x = lax.div(gx, 4), lax.rem(gx, 4)
    chip_z, core = lax.div(gy, 2), lax.rem(gy, 2)
    x_after, x_before = lax.rem(gx + 1, SX), lax.rem(gx + SX - 1, SX)
    y_after, y_before = lax.rem(gy + 1, SY), lax.rem(gy + SY - 1, SY)

    def x_at(dy, dx):
        return 4 * lax.rem(chip_y + dy, 8) + lax.rem(chip_x + dx, 4), gy

    def y_at(dz, dc):
        return gx, 2 * lax.rem(chip_z + dz, 8) + lax.rem(core + dc, 2)

    near = [x_at(dy, dx) for dy, dx in X_ORDER if dy in NEAR]
    near += [y_at(dz, dc) for dz, dc in Y_ORDER if dz in NEAR]
    barrier = pltpu.get_barrier_semaphore()
    for device in near:
        pl.semaphore_signal(barrier, inc=1, device_id=device, device_id_type=MESH)

    for b in range(8):
        pltpu.make_async_copy(
            flow.at[:, :, pl.ds(128 * b, 128)], q_sc.at[:, pl.ds(8 * b, 8), :], in_sem
        ).start()
    code_copies = [
        pltpu.make_async_copy(x_codes, x_code_sc, code_sem.at[0]),
        pltpu.make_async_copy(y_codes, y_code_sc, code_sem.at[1]),
    ]
    for copy in code_copies:
        copy.start()

    def tell(step):
        for k in (step + 1, 7 - step):
            for device in (x_at(k, 0), y_at(k, 0)):
                pl.semaphore_signal(word.at[step], inc=1, device_id=device, device_id_type=MESH)

    def heard(step):
        pl.semaphore_wait(word.at[step], 4)

    pl.semaphore_wait(barrier, len(near))
    tell(0)
    wait_all(q_sc, in_sem)
    for copy in code_copies:
        copy.wait()

    x_send[0] = q_sc[:, pl.ds(7, 8, stride=8), :]
    x_send[1] = q_sc[:, pl.ds(0, 8, stride=8), :]
    halos = [
        (x_send.at[0], x_low, (x_after, gy)),
        (x_send.at[1], x_high, (x_before, gy)),
        (q_sc.at[:, pl.ds(56, 8), :], y_low, (gx, y_after)),
        (q_sc.at[:, pl.ds(0, 8), :], y_high, (gx, y_before)),
    ]
    copies = []
    for i, (source, target, device) in enumerate(halos):
        copy = pltpu.make_async_remote_copy(
            src_ref=source,
            dst_ref=target,
            send_sem=halo_send.at[i],
            recv_sem=halo_recv.at[i],
            device_id=device,
            device_id_type=MESH,
        )
        copy.start()
        copies.append(copy)
    heard(0)
    tell(1)

    two_families = lax.div(gx, 8) == 2

    def by_rows(two, act):
        @pl.when(two)
        def _():
            act(4)

        @pl.when(jnp.logical_not(two))
        def _():
            act(2)

    def send_x(source, target, slot):
        def own(rows):
            mine = pl.ds(gx * 4, rows)
            pltpu.make_async_copy(source.at[mine], target.at[mine], recv_sem.at[slot]).start()

        def one(other, rows):
            pltpu.make_async_remote_copy(
                src_ref=source.at[pl.ds(other * 4, rows)],
                dst_ref=target.at[pl.ds(gx * 4, rows)],
                send_sem=send_sem.at[slot],
                recv_sem=recv_sem.at[slot],
                device_id=(other, gy),
                device_id_type=MESH,
            ).start()

        others = [x_at(dy, dx)[0] for dy, dx in X_ORDER]
        if slot == 0:
            own(4)
            for other in others:
                one(other, 4)
        elif slot == 1:
            by_rows(two_families, own)
            for other in others:
                by_rows(lax.div(other, 8) == 2, functools.partial(one, other))
        else:

            def all_of(rows):
                own(rows)
                for other in others:
                    one(other, rows)

            by_rows(two_families, all_of)

    def others_y():
        for dz, dc in Y_ORDER:
            yield 2 * lax.rem(lax.div(gy, 2) + dz, 8) + lax.rem(lax.rem(gy, 2) + dc, 2)

    blocks = q_sc[...].reshape(5, 8, 8, 128)
    prim_o = primitives(blocks)
    to_before_y, to_after_y, speeds_y = y_terms(blocks, prim_o)
    part_z = z_terms(blocks, prim_o)
    q = jnp.stack([q_sc[:, pl.ds(k, 8, stride=8), :] for k in range(8)], axis=1)
    prim = primitives(q)
    to_before_x, to_after_x = x_terms(q, prim)

    for copy in copies:
        copy.wait_recv()
    low = jnp.where(start_x, q[:, 0], x_low[...])
    high = jnp.where(end_x, q[:, 7], x_high[...])
    prim_low, prim_high = primitives(low), primitives(high)
    u, c = (
        jnp.concatenate([prim_low[i][None], prim[i], prim_high[i][None]]) for i in (1, 6)
    )

    y_edge_low = jnp.where(start_y, roll(blocks[:, 0], 96, -1), y_low[...])
    y_edge_high = jnp.where(end_y, roll(blocks[:, 7], 32, -1), y_high[...])
    low_terms = y_terms(y_edge_low, primitives(y_edge_low))
    high_terms = y_terms(y_edge_high, primitives(y_edge_high))
    part = (
        up_y(join(low_terms[0], to_before_y, high_terms[0]))
        + down_y(join(low_terms[1], to_after_y, high_terms[1]))
        + part_z
    )
    part_sc[...] = part.reshape(5, 64, 128)
    residual = (
        jnp.concatenate([to_before_x[:, 1:], x_terms(high, prim_high)[0][:, None]], axis=1)
        + jnp.concatenate([x_terms(low, prim_low)[1][:, None], to_after_x[:, :7]], axis=1)
        + jnp.stack([part_sc[:, pl.ds(k, 8, stride=8), :] for k in range(8)], axis=1)
    )
    right = x_right(residual, prim)

    lower, upper, first, last = x_bands(u, c, x_code_sc[...], start_x, end_x)
    xm, xg, xp, xq, x_own = eliminate(lower, upper, first, last)
    for group, (matrix, families) in enumerate(GROUPS):
        for row in range(4):
            xm_out[pl.ds(group * 32 + row, 8, stride=4), :] = x_own[row][matrix]
    heard(1)
    send_x(xm_out, xm_in, 0)

    xd, x_last = eliminate_right([right[:, k] for k in range(8)], lower, xm, xg)
    zero = jnp.zeros((8, 128), jnp.float32)
    for group, (matrix, families) in enumerate(GROUPS):
        for i in range(2):
            at = group * 32 + 2 * i
            some = i < len(families)
            xr_out[pl.ds(at, 8, stride=4), :] = x_last[families[i]] if some else zero
            xr_out[pl.ds(at + 1, 8, stride=4), :] = xd[0][families[i]] if some else zero
    send_x(xr_out, xr_in, 1)

    speeds_y = join(low_terms[2], speeds_y, high_terms[2])
    speed_sc[...] = jnp.concatenate([down_y(speeds_y), up_y(speeds_y)]).reshape(4, 64, 128)
    speeds = jnp.stack([speed_sc[:, pl.ds(k, 8, stride=8), :] for k in range(8)], axis=1)
    y_lower, y_upper = y_bands(swap_groups(speeds))
    y_lower, y_upper, first, last = y_ends(y_lower, y_upper, y_code_sc[...], start_y, end_y)
    ym, yg, yp, yq, y_own = eliminate(y_lower, y_upper, first, last)
    y_den, y_high_part, y_lev, y_p, y_q, y_joint, joined = y_join(y_own)
    ym_out[...] = jnp.zeros((32, 128), jnp.float32)
    for kind in range(4):
        line = 7 if kind < 2 else 0
        for matrix in range(3):
            for h in range(2):
                at = kind * 8 + matrix * 2 + h
                ym_out[pl.ds(at, 1), :] = joined[kind][matrix, h, line : line + 1]
    pltpu.make_async_copy(ym_out, ym_in.at[gy], recv_sem.at[3]).start()
    for other in others_y():
        pltpu.make_async_remote_copy(
            src_ref=ym_out,
            dst_ref=ym_in.at[gy],
            send_sem=send_sem.at[3],
            recv_sem=recv_sem.at[3],
            device_id=(gx, other),
            device_id_type=MESH,
        ).start()

    wait_all(xm_in, recv_sem.at[0])
    den, high_part, a, c = factor([xm_in[pl.ds(row, SX, stride=4), :] for row in range(4)])
    levels = factor_levels(a, c)
    by_rows(two_families, lambda rows: wait_all(xr_in.at[pl.ds(0, SX * rows)], recv_sem.at[1]))
    for i in range(2):
        own_last = xr_in[pl.ds(2 * i, SX, stride=4), :]
        own_first = xr_in[pl.ds(2 * i + 1, SX, stride=4), :]
        d = den * own_last + high_part * roll(own_first, -1, 0)
        d = reduce_levels(d, levels)
        xs_out[pl.ds(2 * i, SX, stride=4), :] = roll(d, 1, 0)
        xs_out[pl.ds(2 * i + 1, SX, stride=4), :] = d
    send_x(xs_out, xs_in, 2)

    wait_all(ym_in, recv_sem.at[3])
    segments = [
        tuple(ym_in[j, pl.ds(8 * kind, 8), :] for kind in range(4)) for j in range(SY)
    ]
    for j, weights in enumerate(y_weights(segments)):
        for i, weight in enumerate(weights):
            y_weight_sc[j, i] = weight
    for i in range(10):
        for family, matrix in enumerate((0, 1, 1, 1, 2)):
            y_weight[i, pl.ds(2 * family, 2), :] = y_weight_sc[gy, i, pl.ds(2 * matrix, 2), :]

    r = q[0]
    rc = r * prim[6]
    half_rc_inv = 0.5 / rc
    c2_inv = 1.0 / prim[5]

    wait_all(xs_in.at[pl.ds(0, 80)], recv_sem.at[2])

    def x_value(kind):
        rows = []
        for group, i in ((0, 0), (2, 0), (2, 1), (3, 0), (1, 0)):
            rows.append(xs_in[pl.ds(group * 32 + 2 * i + kind, 8, stride=4), :])
        return jnp.stack(rows)

    solved = jnp.stack(put_back(xd, xp, xq, x_value(0), x_value(1)), axis=1)
    right = swap_groups(y_right(solved, rc, half_rc_inv)).reshape(5, 2, 4, 8, 128)
    yd, y_last = eliminate_right([right[:, :, k] for k in range(4)], y_lower, ym, yg)
    y_d, joined_last, joined_first = y_join_right(
        yd[0], y_last, y_own, y_den, y_high_part, y_lev, y_joint
    )
    for family in range(5):
        for h in range(2):
            yr_sc[0, pl.ds(2 * family + h, 1), :] = joined_last[family, h, 7:8]
            yr_sc[1, pl.ds(2 * family + h, 1), :] = joined_first[family, h, 0:1]
    weights = [y_weight[i] for i in range(10)]
    own_add, before_add, own_out, before_out = y_emit(yr_sc[0], yr_sc[1], weights)
    yf_out[0], yf_out[1] = own_out, before_out
    core_copy = pltpu.make_async_remote_copy(
        src_ref=yf_out.at[:, pl.ds(0, 10)],
        dst_ref=yc_in.at[:, pl.ds(0, 10)],
        send_sem=send_sem.at[5],
        recv_sem=recv_sem.at[5],
        device_id=(gx, 2 * chip_z + 1 - core),
        device_id_type=MESH,
    )
    core_copy.start()
    core_copy.wait_recv()
    yb_out[0], yb_out[1] = own_out + yc_in[0], before_out + yc_in[1]
    for dz, dc in Y_ORDER:
        if dc == 0:
            other = lax.rem(chip_z + dz, 8)
            pltpu.make_async_remote_copy(
                src_ref=yb_out.at[jnp.where(other < chip_z, 1, 0), pl.ds(0, 10)],
                dst_ref=yf_in.at[chip_z, pl.ds(0, 10)],
                send_sem=send_sem.at[4],
                recv_sem=recv_sem.at[4],
                device_id=(gx, 2 * other + core),
                device_id_type=MESH,
            ).start()
    below = jnp.where(core == 1, yc_in[0], 0.0)
    above = jnp.where(core == 0, yc_in[1], 0.0)
    wait_all(yf_in.at[pl.ds(0, 7), pl.ds(0, 10)], recv_sem.at[4])
    for j in range(8):
        below = below + jnp.where(j < chip_z, yf_in[j], 0.0)
        above = above + jnp.where(j > chip_z, yf_in[j], 0.0)
    ys_sc[0], ys_sc[1] = y_meet(below, above, own_add, before_add, weights)

    def y_value(kind):
        return jnp.stack(
            [
                jnp.stack([ys_sc[kind, pl.ds(2 * family + h, 1), :] for h in range(2)])
                for family in range(5)
            ]
        )

    before, own = y_value(0), y_value(1)
    groups = y_d + five(y_p) * before + five(y_q) * own
    previous = jnp.where(row_of(groups.shape) == 0, before, roll(groups, 1, -2))
    solved = jnp.stack(put_back(yd, yp, yq, previous, groups), axis=2)
    solved = swap_groups(solved.reshape(5, 8, 8, 128))
    for field, value in enumerate(increments(solved, prim, r, half_rc_inv, c2_inv)):
        for k in range(8):
            out[field, pl.ds(k, 8, stride=8), :] = value[k]

    for copy in copies:
        copy.wait_send()
    wait_all(xm_out.at[pl.ds(0, 4 * (SX - 1))], send_sem.at[0])
    by_rows(two_families, lambda rows: wait_all(xr_out.at[pl.ds(0, 80 - rows)], send_sem.at[1]))
    by_rows(
        two_families, lambda rows: wait_all(xs_out.at[pl.ds(0, (SX - 1) * rows)], send_sem.at[2])
    )
    wait_all(ym_in.at[pl.ds(0, SY - 1)], send_sem.at[3])
    wait_all(yf_in.at[pl.ds(0, 7), pl.ds(0, 10)], send_sem.at[4])
    core_copy.wait_send()


def local(flow_state, x_codes, y_codes):
    f32 = jnp.float32

    def vmem(*shape):
        return pltpu.VMEM(shape, f32)

    result = pl.pallas_call(
        kernel,
        out_shape=jax.ShapeDtypeStruct((5, 64, 128), f32),
        in_specs=[pl.BlockSpec(memory_space=pltpu.HBM)] * 3,
        out_specs=pl.BlockSpec(memory_space=pltpu.VMEM),
        scratch_shapes=[
            vmem(5, 64, 128),
            vmem(5, 64, 128),
            vmem(4, 64, 128),
            vmem(2, 5, 8, 128),
            vmem(5, 8, 128),
            vmem(5, 8, 128),
            vmem(5, 8, 128),
            vmem(5, 8, 128),
            vmem(4 * SX, 128),
            vmem(4 * SX, 128),
            vmem(4 * SX, 128),
            vmem(4 * SX, 128),
            vmem(4 * SX, 128),
            vmem(4 * SX, 128),
            vmem(32, 128),
            vmem(SY, 32, 128),
            vmem(SY, 10, 8, 128),
            vmem(10, 16, 128),
            vmem(2, 16, 128),
            vmem(2, 16, 128),
            vmem(2, 16, 128),
            vmem(2, 16, 128),
            vmem(8, 16, 128),
            vmem(2, 16, 128),
            pltpu.VMEM((2, 32), jnp.int32),
            pltpu.VMEM((2, 8), jnp.int32),
            pltpu.SemaphoreType.REGULAR((2,)),
            pltpu.SemaphoreType.DMA,
            pltpu.SemaphoreType.DMA((2,)),
            pltpu.SemaphoreType.DMA((4,)),
            pltpu.SemaphoreType.DMA((4,)),
            pltpu.SemaphoreType.DMA((6,)),
            pltpu.SemaphoreType.DMA((6,)),
        ],
        compiler_params=pltpu.CompilerParams(
            collective_id=0, has_side_effects=True, vmem_limit_bytes=VMEM_LIMIT
        ),
        name="step",
    )(*(pltpu.with_memory_space_constraint(v, pltpu.HBM) for v in (flow_state, x_codes, y_codes)))
    result = jnp.transpose(result.reshape(5, 8, 8, 128), (0, 2, 1, 3))
    return result.reshape(flow_state.shape)


def solution(mesh):
    return jax.shard_map(
        local,
        mesh=mesh,
        in_specs=(P(None, "gx", "gy"), P(None, "gy"), P(None, "gx")),
        out_specs=P(None, "gx", "gy"),
        check_vma=False,
    )
```

```python
import functools

import jax
import jax.numpy as jnp
from jax import lax
from jax.experimental import pallas as pl
from jax.experimental.pallas import tpu as pltpu
from jax.sharding import PartitionSpec as P

NZ = 32
SX = 32
SY = 16
VMEM_LIMIT = 32 * 1024 * 1024
MAIN = 801.0
GROUPS = ((0, (0,)), (2, (4,)), (1, (1, 2)), (1, (3,)))
MESH = pl.DeviceIdType.MESH


def far_first(*lengths):
    offsets = [()]
    for length in lengths:
        offsets = [(*offset, k) for offset in offsets for k in range(length)]
    hops = {
        offset: sum(min(k, length - k) for k, length in zip(offset, lengths)) for offset in offsets
    }
    return sorted((offset for offset in offsets if any(offset)), key=lambda o: (-hops[o], o))


NEAR = (0, 1, 7)
X_ORDER = far_first(8, 4)
Y_ORDER = far_first(8, 2)


def roll(value, shift, axis):
    axis = axis % value.ndim
    return pltpu.roll(value, shift % value.shape[axis], axis)


def lane_of(shape):
    return lax.broadcasted_iota(jnp.int32, shape, len(shape) - 1)


def row_of(shape):
    return lax.broadcasted_iota(jnp.int32, shape, len(shape) - 2)


def five(value):
    return jnp.concatenate([value[0:1], value[1:2], value[1:2], value[1:2], value[2:3]])


def primitives(q):
    inv = 1.0 / q[0]
    u, v, w = q[1] * inv, q[2] * inv, q[3] * inv
    p = 0.4 * (q[4] - 0.5 * (q[1] * u + q[2] * v + q[3] * w))
    c2 = 1.4 * p * inv
    return inv, u, v, w, p, c2, c2 * lax.rsqrt(c2)


def up_y(value):
    here, after = value[..., 1:9, :, :], value[..., 2:10, :, :]
    return roll(jnp.where(lane_of(here.shape) < 32, after, here), -32, -1)


def down_y(value):
    before, here = value[..., 0:8, :, :], value[..., 1:9, :, :]
    return roll(jnp.where(lane_of(here.shape) >= 96, before, here), 32, -1)


def z_difference(value):
    z = lane_of(value.shape) & 31
    after = jnp.where(z == 31, roll(value, 31, -1), roll(value, -1, -1))
    before = jnp.where(z == 0, roll(value, -31, -1), roll(value, 1, -1))
    return after - before


def y_terms(q, prim):
    inv, u, v, w, p, c2, c = prim
    flux = 0.25 * jnp.stack([q[2], q[1] * v, q[2] * v + p, q[3] * v, v * (q[4] + p)])
    smooth = 400.0 * q
    return smooth - flux, smooth + flux, jnp.stack([v, c])


def z_terms(q, prim):
    inv, u, v, w, p, c2, c = prim
    flux = jnp.stack([q[3], q[1] * w, q[2] * w, q[3] * w + p, w * (q[4] + p)])
    return -1600.0 * q - 0.25 * z_difference(flux)


def x_terms(q, prim):
    inv, u, v, w, p, c2, c = prim
    flux = 0.25 * jnp.stack([q[1], q[1] * u + p, q[2] * u, q[3] * u, u * (q[4] + p)])
    smooth = 400.0 * q
    return smooth - flux, smooth + flux


def join(low, inner, high):
    return jnp.concatenate([low[:, None], inner, high[:, None]], axis=1)


def x_right(res, prim):
    inv, u, v, w, p, c2, c = prim
    kinetic = 0.5 * (u * u + v * v + w * w)
    dp = 0.4 * (res[4] - u * res[1] - v * res[2] - w * res[3] + kinetic * res[0])
    normal = c * (res[1] - u * res[0])
    return jnp.stack(
        [
            dp - normal,
            c2 * res[0] - dp,
            (res[2] - v * res[0]) * inv,
            (res[3] - w * res[0]) * inv,
            dp + normal,
        ]
    )


def eliminate(lower, upper, main_first, main_last):
    n = len(lower)
    m = [1.0 / main_first]
    g = [upper[0] * m[0]]
    p = [-lower[0] * m[0]]
    for k in range(1, n - 1):
        m.append(1.0 / (MAIN - lower[k] * g[k - 1]))
        g.append(upper[k] * m[k])
        p.append(-(lower[k] * p[k - 1]) * m[k])
    q = [None] * (n - 1)
    q[n - 2] = -g[n - 2]
    for k in range(n - 3, -1, -1):
        p[k] = p[k] - g[k] * p[k + 1]
        q[k] = -(g[k] * q[k + 1])
    last = 1.0 / (main_last + lower[n - 1] * q[n - 2])
    m.append(last)
    own = (-(lower[n - 1] * p[n - 2]) * last, -upper[n - 1] * last, p[0], q[0])
    return m, g, p, q, own


def eliminate_right(right, lower, m, g):
    n = len(right)
    d = [right[0] * five(m[0])]
    for k in range(1, n - 1):
        d.append((right[k] - five(lower[k]) * d[k - 1]) * five(m[k]))
    for k in range(n - 3, -1, -1):
        d[k] = d[k] - five(g[k]) * d[k + 1]
    last = (right[n - 1] - five(lower[n - 1]) * d[n - 2]) * five(m[n - 1])
    return d, last


def put_back(d, p, q, before, own):
    cells = [d[k] + five(p[k]) * before + five(q[k]) * own for k in range(len(d))]
    return cells + [own]


def factor(own):
    to_before, to_after, first_before, first_own = own
    rows = to_before.shape[-2]
    den = 1.0 / (1.0 - to_after * roll(first_before, -1, -2))
    a = to_before * den
    c = to_after * roll(first_own, -1, -2) * den
    return den, to_after * den, a, c


def factor_levels(a, c):
    rows = a.shape[-2]
    levels = []
    step = 1
    while step < rows:
        dn = 1.0 / (1.0 - a * roll(c, step, -2) - c * roll(a, -step, -2))
        an, cn = a * dn, c * dn
        levels.append((dn, an, cn))
        a, c = an * roll(a, step, -2), cn * roll(c, -step, -2)
        step *= 2
    return levels


def reduce_levels(d, levels):
    step = 1
    for dn, an, cn in levels:
        d = dn * d + an * roll(d, step, -2) + cn * roll(d, -step, -2)
        step *= 2
    return d


def y_right(s, rc, half_rc_inv):
    dp = 0.5 * (s[0] + s[4])
    normal = rc * s[2]
    return jnp.stack([dp - normal, s[1], (s[4] - s[0]) * half_rc_inv, s[3], dp + normal])


def swap_groups(value):
    lead = value.shape[:-3]
    half = value.reshape(*lead, 2, 2, 2, 8, 128)
    a, b = half[..., 0, :, :, :], half[..., 1, :, :, :]
    low = (lane_of(a.shape) & 64) == 0
    a, b = jnp.where(low, a, roll(b, 64, -1)), jnp.where(low, roll(a, 64, -1), b)
    half = jnp.stack([a, b], axis=len(lead) + 1)
    a, b = half[..., 0, :, :], half[..., 1, :, :]
    low = (lane_of(a.shape) & 32) == 0
    a, b = jnp.where(low, a, roll(b, 32, -1)), jnp.where(low, roll(a, -32, -1), b)
    half = jnp.stack([a, b], axis=len(lead) + 2)
    return half.reshape(*lead, 8, 8, 128)


def y_bands(speeds):
    vm, cm, vp, cp = (speeds[i].reshape(2, 4, 8, 128) for i in range(4))
    low = jnp.stack([vm - cm, vm, vm + cm])
    high = jnp.stack([vp - cp, vp, vp + cp])
    lower = [-0.25 * low[:, :, k] - 400.0 for k in range(4)]
    upper = [0.25 * high[:, :, k] - 400.0 for k in range(4)]
    return lower, upper


def y_join(own):
    row = row_of(own[0].shape)
    den, high, a, c = factor(own)
    p = jnp.where(row == 0, a, 0.0)
    q = jnp.where(row == 7, 1.0, 0.0)
    a = jnp.where((row == 0) | (row == 7), 0.0, a)
    c = jnp.where(row == 7, 0.0, c)
    levels = factor_levels(a, c)
    p = reduce_levels(p, levels)
    q = reduce_levels(q, levels)
    last = 1.0 / (1.0 - own[0] * roll(q, 1, -2))
    joined = (
        own[0] * roll(p, 1, -2) * last,
        own[1] * last,
        own[2] + own[3] * p,
        own[3] * q,
    )
    return den, high, levels, p, q, last, joined


def y_join_right(d0, last_right, own, den, high, levels, last):
    row = row_of(last_right.shape)
    d = five(den) * last_right + five(high) * roll(d0, -1, -2)
    d = jnp.where(row == 7, 0.0, d)
    d = reduce_levels(d, [tuple(five(part) for part in level) for level in levels])
    joined_last = (last_right + five(own[0]) * roll(d, 1, -2)) * five(last)
    joined_first = d0 + five(own[3]) * d
    return d, joined_last, joined_first


def y_weights(segments):
    n = len(segments)
    ones = jnp.ones_like(segments[0][0])
    zero = jnp.zeros_like(ones)
    den, high, a, c = [], [], [], []
    for j, (to_before, to_after, _, _) in enumerate(segments):
        after = segments[j + 1] if j < n - 1 else (zero,) * 4
        den.append(1.0 / (1.0 - to_after * after[2]))
        high.append(to_after * den[j])
        a.append(to_before * den[j])
        c.append(high[j] * after[3])
    left, right = [None] * n, [None] * n
    for j in range(n):
        left[j] = c[j] / (1.0 - a[j] * left[j - 1]) if j else c[j]
    for j in range(n - 1, -1, -1):
        right[j] = a[j] / (1.0 - c[j] * right[j + 1]) if j < n - 1 else a[j]
    gain = []
    for j in range(n):
        rest = ones
        rest = rest - a[j] * left[j - 1] if j else rest
        rest = rest - c[j] * right[j + 1] if j < n - 1 else rest
        gain.append(1.0 / rest)
    down, up = [ones] * n, [ones] * n
    for j in range(1, n):
        down[j] = down[j - 1] * right[j]
    for j in range(n - 2, -1, -1):
        up[j] = up[j + 1] * left[j]
    weights = []
    for j in range(n):
        own_last = gain[j] * den[j]
        own_first = right[j] * gain[j - 1] * high[j - 1] if j else zero
        before_last = left[j - 1] * own_last if j else zero
        before_first = gain[j - 1] * high[j - 1] if j else zero
        down_inv = 1.0 / down[j]
        up_inv = 1.0 / up[j - 1] if j else ones
        weights.append(
            (
                own_last,
                own_first,
                before_last,
                before_first,
                down_inv,
                up_inv,
                down[j - 1] if j else zero,
                up[j],
                right[j],
                left[j - 1] if j else zero,
            )
        )
    return weights


def y_emit(last, first, w):
    own = w[0] * last + w[1] * first
    before = w[2] * last + w[3] * first
    return own, before, own * w[4], before * w[5]


def y_meet(below, above, own, before, w):
    low, high = w[6] * below, w[7] * above
    return low + w[9] * high + before, w[8] * low + own + high


def increments(s, prim, r, half_rc_inv, c2_inv):
    inv, u, v, w, p, c2, c = prim
    dp = 0.5 * (s[0] + s[4])
    dv = (s[4] - s[0]) * half_rc_inv
    dr = (s[1] + dp) * c2_inv
    du, dw = s[2], s[3]
    kinetic = 0.5 * (u * u + v * v + w * w)
    return (
        dr,
        u * dr + r * du,
        v * dr + r * dv,
        w * dr + r * dw,
        kinetic * dr + r * (u * du + v * dv + w * dw) + 2.5 * dp,
    )


def x_code_mask(codes, side):
    ones = (codes[side : side + 1] == 1).astype(jnp.float32)
    spread = jnp.where((lane_of((8, 32)) >> 2) == row_of((8, 32)), ones, 0.0)
    place = jnp.where((row_of((32, 128)) & 3) == (lane_of((32, 128)) >> 5), 1.0, 0.0)
    return jnp.dot(spread, place, preferred_element_type=jnp.float32) > 0.5


def y_code_mask(codes, side):
    ones = jnp.broadcast_to((codes[side : side + 1] == 1).astype(jnp.float32), (8, 8))
    halves = []
    for h in range(2):
        place = jnp.where(row_of((8, 128)) == 4 * h + (lane_of((8, 128)) >> 5), 1.0, 0.0)
        halves.append(jnp.dot(ones, place, preferred_element_type=jnp.float32))
    return jnp.stack(halves) > 0.5


def x_bands(u, c, codes, start, end):
    lam = jnp.stack([u - c, u, u + c])
    lower = [-0.25 * lam[:, k] - 400.0 for k in range(8)]
    upper = [0.25 * lam[:, k + 2] - 400.0 for k in range(8)]
    first = MAIN + jnp.where(x_code_mask(codes, 0)[None] & start, lower[0], 0.0)
    last = MAIN + jnp.where(x_code_mask(codes, 1)[None] & end, upper[7], 0.0)
    lower[0] = jnp.where(start, 0.0, lower[0])
    upper[7] = jnp.where(end, 0.0, upper[7])
    return lower, upper, first, last


def y_ends(lower, upper, codes, start, end):
    row = row_of(lower[0].shape)
    at_start = (row == 0) & start
    at_end = (row == 7) & end
    first = MAIN + jnp.where(at_start & y_code_mask(codes, 0)[None], lower[0], 0.0)
    last = MAIN + jnp.where(at_end & y_code_mask(codes, 1)[None], upper[3], 0.0)
    lower, upper = list(lower), list(upper)
    lower[0] = jnp.where(at_start, 0.0, lower[0])
    upper[3] = jnp.where(at_end, 0.0, upper[3])
    return lower, upper, first, last


def wait_all(ref, sem):
    pltpu.make_async_copy(ref, ref, sem).wait()


def kernel(
    flow,
    x_codes,
    y_codes,
    out,
    q_sc,
    part_sc,
    speed_sc,
    x_send,
    x_low,
    x_high,
    y_low,
    y_high,
    xm_out,
    xr_out,
    xm_in,
    xr_in,
    xs_out,
    xs_in,
    ym_out,
    ym_in,
    y_weight_sc,
    y_weight,
    yr_sc,
    yf_out,
    yc_in,
    yb_out,
    yf_in,
    ys_sc,
    x_code_sc,
    y_code_sc,
    word,
    in_sem,
    code_sem,
    halo_send,
    halo_recv,
    send_sem,
    recv_sem,
):
    gx, gy = lax.axis_index("gx"), lax.axis_index("gy")
    start_x, end_x = gx == 0, gx == SX - 1
    start_y, end_y = gy == 0, gy == SY - 1

    chip_y, chip_x = lax.div(gx, 4), lax.rem(gx, 4)
    chip_z, core = lax.div(gy, 2), lax.rem(gy, 2)
    x_after, x_before = lax.rem(gx + 1, SX), lax.rem(gx + SX - 1, SX)
    y_after, y_before = lax.rem(gy + 1, SY), lax.rem(gy + SY - 1, SY)

    def x_at(dy, dx):
        return 4 * lax.rem(chip_y + dy, 8) + lax.rem(chip_x + dx, 4), gy

    def y_at(dz, dc):
        return gx, 2 * lax.rem(chip_z + dz, 8) + lax.rem(core + dc, 2)

    near = [x_at(dy, dx) for dy, dx in X_ORDER if dy in NEAR]
    near += [y_at(dz, dc) for dz, dc in Y_ORDER if dz in NEAR]
    barrier = pltpu.get_barrier_semaphore()
    for device in near:
        pl.semaphore_signal(barrier, inc=1, device_id=device, device_id_type=MESH)

    for b in range(8):
        pltpu.make_async_copy(
            flow.at[:, :, pl.ds(128 * b, 128)], q_sc.at[:, pl.ds(8 * b, 8), :], in_sem
        ).start()
    code_copies = [
        pltpu.make_async_copy(x_codes, x_code_sc, code_sem.at[0]),
        pltpu.make_async_copy(y_codes, y_code_sc, code_sem.at[1]),
    ]
    for copy in code_copies:
        copy.start()

    def tell(step):
        for k in (step + 1, 7 - step):
            for device in (x_at(k, 0), y_at(k, 0)):
                pl.semaphore_signal(word.at[step], inc=1, device_id=device, device_id_type=MESH)

    def heard(step):
        pl.semaphore_wait(word.at[step], 4)

    pl.semaphore_wait(barrier, len(near))
    tell(0)
    wait_all(q_sc, in_sem)
    for copy in code_copies:
        copy.wait()

    x_send[0] = q_sc[:, pl.ds(7, 8, stride=8), :]
    x_send[1] = q_sc[:, pl.ds(0, 8, stride=8), :]
    halos = [
        (x_send.at[0], x_low, (x_after, gy)),
        (x_send.at[1], x_high, (x_before, gy)),
        (q_sc.at[:, pl.ds(56, 8), :], y_low, (gx, y_after)),
        (q_sc.at[:, pl.ds(0, 8), :], y_high, (gx, y_before)),
    ]
    copies = []
    for i, (source, target, device) in enumerate(halos):
        copy = pltpu.make_async_remote_copy(
            src_ref=source,
            dst_ref=target,
            send_sem=halo_send.at[i],
            recv_sem=halo_recv.at[i],
            device_id=device,
            device_id_type=MESH,
        )
        copy.start()
        copies.append(copy)
    heard(0)
    tell(1)

    two_families = lax.div(gx, 8) == 2

    def by_rows(two, act):
        @pl.when(two)
        def _():
            act(4)

        @pl.when(jnp.logical_not(two))
        def _():
            act(2)

    def send_x(source, target, slot):
        def own(rows):
            mine = pl.ds(gx * 4, rows)
            pltpu.make_async_copy(source.at[mine], target.at[mine], recv_sem.at[slot]).start()

        def one(other, rows):
            pltpu.make_async_remote_copy(
                src_ref=source.at[pl.ds(other * 4, rows)],
                dst_ref=target.at[pl.ds(gx * 4, rows)],
                send_sem=send_sem.at[slot],
                recv_sem=recv_sem.at[slot],
                device_id=(other, gy),
                device_id_type=MESH,
            ).start()

        others = [x_at(dy, dx)[0] for dy, dx in X_ORDER]
        if slot == 0:
            own(4)
            for other in others:
                one(other, 4)
        elif slot == 1:
            by_rows(two_families, own)
            for other in others:
                by_rows(lax.div(other, 8) == 2, functools.partial(one, other))
        else:

            def all_of(rows):
                own(rows)
                for other in others:
                    one(other, rows)

            by_rows(two_families, all_of)

    def others_y():
        for dz, dc in Y_ORDER:
            yield 2 * lax.rem(lax.div(gy, 2) + dz, 8) + lax.rem(lax.rem(gy, 2) + dc, 2)

    blocks = q_sc[...].reshape(5, 8, 8, 128)
    prim_o = primitives(blocks)
    to_before_y, to_after_y, speeds_y = y_terms(blocks, prim_o)
    part_z = z_terms(blocks, prim_o)
    q = jnp.stack([q_sc[:, pl.ds(k, 8, stride=8), :] for k in range(8)], axis=1)
    prim = primitives(q)
    to_before_x, to_after_x = x_terms(q, prim)

    for copy in copies:
        copy.wait_recv()
    low = jnp.where(start_x, q[:, 0], x_low[...])
    high = jnp.where(end_x, q[:, 7], x_high[...])
    prim_low, prim_high = primitives(low), primitives(high)
    u, c = (
        jnp.concatenate([prim_low[i][None], prim[i], prim_high[i][None]]) for i in (1, 6)
    )

    y_edge_low = jnp.where(start_y, roll(blocks[:, 0], 96, -1), y_low[...])
    y_edge_high = jnp.where(end_y, roll(blocks[:, 7], 32, -1), y_high[...])
    low_terms = y_terms(y_edge_low, primitives(y_edge_low))
    high_terms = y_terms(y_edge_high, primitives(y_edge_high))
    part = (
        up_y(join(low_terms[0], to_before_y, high_terms[0]))
        + down_y(join(low_terms[1], to_after_y, high_terms[1]))
        + part_z
    )
    part_sc[...] = part.reshape(5, 64, 128)
    residual = (
        jnp.concatenate([to_before_x[:, 1:], x_terms(high, prim_high)[0][:, None]], axis=1)
        + jnp.concatenate([x_terms(low, prim_low)[1][:, None], to_after_x[:, :7]], axis=1)
        + jnp.stack([part_sc[:, pl.ds(k, 8, stride=8), :] for k in range(8)], axis=1)
    )
    right = x_right(residual, prim)

    lower, upper, first, last = x_bands(u, c, x_code_sc[...], start_x, end_x)
    xm, xg, xp, xq, x_own = eliminate(lower, upper, first, last)
    for group, (matrix, families) in enumerate(GROUPS):
        for row in range(4):
            xm_out[pl.ds(group * 32 + row, 8, stride=4), :] = x_own[row][matrix]
    heard(1)
    send_x(xm_out, xm_in, 0)

    xd, x_last = eliminate_right([right[:, k] for k in range(8)], lower, xm, xg)
    zero = jnp.zeros((8, 128), jnp.float32)
    for group, (matrix, families) in enumerate(GROUPS):
        for i in range(2):
            at = group * 32 + 2 * i
            some = i < len(families)
            xr_out[pl.ds(at, 8, stride=4), :] = x_last[families[i]] if some else zero
            xr_out[pl.ds(at + 1, 8, stride=4), :] = xd[0][families[i]] if some else zero
    send_x(xr_out, xr_in, 1)

    speeds_y = join(low_terms[2], speeds_y, high_terms[2])
    speed_sc[...] = jnp.concatenate([down_y(speeds_y), up_y(speeds_y)]).reshape(4, 64, 128)
    speeds = jnp.stack([speed_sc[:, pl.ds(k, 8, stride=8), :] for k in range(8)], axis=1)
    y_lower, y_upper = y_bands(swap_groups(speeds))
    y_lower, y_upper, first, last = y_ends(y_lower, y_upper, y_code_sc[...], start_y, end_y)
    ym, yg, yp, yq, y_own = eliminate(y_lower, y_upper, first, last)
    y_den, y_high_part, y_lev, y_p, y_q, y_joint, joined = y_join(y_own)
    ym_out[...] = jnp.zeros((32, 128), jnp.float32)
    for kind in range(4):
        line = 7 if kind < 2 else 0
        for matrix in range(3):
            for h in range(2):
                at = kind * 8 + matrix * 2 + h
                ym_out[pl.ds(at, 1), :] = joined[kind][matrix, h, line : line + 1]
    pltpu.make_async_copy(ym_out, ym_in.at[gy], recv_sem.at[3]).start()
    for other in others_y():
        pltpu.make_async_remote_copy(
            src_ref=ym_out,
            dst_ref=ym_in.at[gy],
            send_sem=send_sem.at[3],
            recv_sem=recv_sem.at[3],
            device_id=(gx, other),
            device_id_type=MESH,
        ).start()

    wait_all(xm_in, recv_sem.at[0])
    den, high_part, a, c = factor([xm_in[pl.ds(row, SX, stride=4), :] for row in range(4)])
    levels = factor_levels(a, c)
    by_rows(two_families, lambda rows: wait_all(xr_in.at[pl.ds(0, SX * rows)], recv_sem.at[1]))

    def solve_x(rows):
        for i in range(rows // 2):
            own_last = xr_in[pl.ds(2 * i, SX, stride=4), :]
            own_first = xr_in[pl.ds(2 * i + 1, SX, stride=4), :]
            d = den * own_last + high_part * roll(own_first, -1, 0)
            d = reduce_levels(d, levels)
            xs_out[pl.ds(2 * i, SX, stride=4), :] = roll(d, 1, 0)
            xs_out[pl.ds(2 * i + 1, SX, stride=4), :] = d

    by_rows(two_families, solve_x)
    send_x(xs_out, xs_in, 2)

    wait_all(ym_in, recv_sem.at[3])
    segments = [
        tuple(ym_in[j, pl.ds(8 * kind, 8), :] for kind in range(4)) for j in range(SY)
    ]
    for j, weights in enumerate(y_weights(segments)):
        for i, weight in enumerate(weights):
            y_weight_sc[j, i] = weight
    for i in range(10):
        for family, matrix in enumerate((0, 1, 1, 1, 2)):
            y_weight[i, pl.ds(2 * family, 2), :] = y_weight_sc[gy, i, pl.ds(2 * matrix, 2), :]

    r = q[0]
    rc = r * prim[6]
    half_rc_inv = 0.5 / rc
    c2_inv = 1.0 / prim[5]

    wait_all(xs_in.at[pl.ds(0, 80)], recv_sem.at[2])

    def x_value(kind):
        rows = []
        for group, i in ((0, 0), (2, 0), (2, 1), (3, 0), (1, 0)):
            rows.append(xs_in[pl.ds(group * 32 + 2 * i + kind, 8, stride=4), :])
        return jnp.stack(rows)

    solved = jnp.stack(put_back(xd, xp, xq, x_value(0), x_value(1)), axis=1)
    right = swap_groups(y_right(solved, rc, half_rc_inv)).reshape(5, 2, 4, 8, 128)
    yd, y_last = eliminate_right([right[:, :, k] for k in range(4)], y_lower, ym, yg)
    y_d, joined_last, joined_first = y_join_right(
        yd[0], y_last, y_own, y_den, y_high_part, y_lev, y_joint
    )
    for family in range(5):
        for h in range(2):
            yr_sc[0, pl.ds(2 * family + h, 1), :] = joined_last[family, h, 7:8]
            yr_sc[1, pl.ds(2 * family + h, 1), :] = joined_first[family, h, 0:1]
    weights = [y_weight[i] for i in range(10)]
    own_add, before_add, own_out, before_out = y_emit(yr_sc[0], yr_sc[1], weights)
    yf_out[0], yf_out[1] = own_out, before_out
    core_copy = pltpu.make_async_remote_copy(
        src_ref=yf_out.at[:, pl.ds(0, 10)],
        dst_ref=yc_in.at[:, pl.ds(0, 10)],
        send_sem=send_sem.at[5],
        recv_sem=recv_sem.at[5],
        device_id=(gx, 2 * chip_z + 1 - core),
        device_id_type=MESH,
    )
    core_copy.start()
    core_copy.wait_recv()
    yb_out[0], yb_out[1] = own_out + yc_in[0], before_out + yc_in[1]
    for dz, dc in Y_ORDER:
        if dc == 0:
            other = lax.rem(chip_z + dz, 8)
            pltpu.make_async_remote_copy(
                src_ref=yb_out.at[jnp.where(other < chip_z, 1, 0), pl.ds(0, 10)],
                dst_ref=yf_in.at[chip_z, pl.ds(0, 10)],
                send_sem=send_sem.at[4],
                recv_sem=recv_sem.at[4],
                device_id=(gx, 2 * other + core),
                device_id_type=MESH,
            ).start()
    below = jnp.where(core == 1, yc_in[0], 0.0)
    above = jnp.where(core == 0, yc_in[1], 0.0)
    wait_all(yf_in.at[pl.ds(0, 7), pl.ds(0, 10)], recv_sem.at[4])
    for j in range(8):
        below = below + jnp.where(j < chip_z, yf_in[j], 0.0)
        above = above + jnp.where(j > chip_z, yf_in[j], 0.0)
    ys_sc[0], ys_sc[1] = y_meet(below, above, own_add, before_add, weights)

    def y_value(kind):
        return jnp.stack(
            [
                jnp.stack([ys_sc[kind, pl.ds(2 * family + h, 1), :] for h in range(2)])
                for family in range(5)
            ]
        )

    before, own = y_value(0), y_value(1)
    groups = y_d + five(y_p) * before + five(y_q) * own
    previous = jnp.where(row_of(groups.shape) == 0, before, roll(groups, 1, -2))
    solved = jnp.stack(put_back(yd, yp, yq, previous, groups), axis=2)
    solved = swap_groups(solved.reshape(5, 8, 8, 128))
    for field, value in enumerate(increments(solved, prim, r, half_rc_inv, c2_inv)):
        for k in range(8):
            out[field, pl.ds(k, 8, stride=8), :] = value[k]

    for copy in copies:
        copy.wait_send()
    wait_all(xm_out.at[pl.ds(0, 4 * (SX - 1))], send_sem.at[0])
    by_rows(two_families, lambda rows: wait_all(xr_out.at[pl.ds(0, 80 - rows)], send_sem.at[1]))
    by_rows(
        two_families, lambda rows: wait_all(xs_out.at[pl.ds(0, (SX - 1) * rows)], send_sem.at[2])
    )
    wait_all(ym_in.at[pl.ds(0, SY - 1)], send_sem.at[3])
    wait_all(yf_in.at[pl.ds(0, 7), pl.ds(0, 10)], send_sem.at[4])
    core_copy.wait_send()


def local(flow_state, x_codes, y_codes):
    f32 = jnp.float32

    def vmem(*shape):
        return pltpu.VMEM(shape, f32)

    result = pl.pallas_call(
        kernel,
        out_shape=jax.ShapeDtypeStruct((5, 64, 128), f32),
        in_specs=[pl.BlockSpec(memory_space=pltpu.HBM)] * 3,
        out_specs=pl.BlockSpec(memory_space=pltpu.VMEM),
        scratch_shapes=[
            vmem(5, 64, 128),
            vmem(5, 64, 128),
            vmem(4, 64, 128),
            vmem(2, 5, 8, 128),
            vmem(5, 8, 128),
            vmem(5, 8, 128),
            vmem(5, 8, 128),
            vmem(5, 8, 128),
            vmem(4 * SX, 128),
            vmem(4 * SX, 128),
            vmem(4 * SX, 128),
            vmem(4 * SX, 128),
            vmem(4 * SX, 128),
            vmem(4 * SX, 128),
            vmem(32, 128),
            vmem(SY, 32, 128),
            vmem(SY, 10, 8, 128),
            vmem(10, 16, 128),
            vmem(2, 16, 128),
            vmem(2, 16, 128),
            vmem(2, 16, 128),
            vmem(2, 16, 128),
            vmem(8, 16, 128),
            vmem(2, 16, 128),
            pltpu.VMEM((2, 32), jnp.int32),
            pltpu.VMEM((2, 8), jnp.int32),
            pltpu.SemaphoreType.REGULAR((2,)),
            pltpu.SemaphoreType.DMA,
            pltpu.SemaphoreType.DMA((2,)),
            pltpu.SemaphoreType.DMA((4,)),
            pltpu.SemaphoreType.DMA((4,)),
            pltpu.SemaphoreType.DMA((6,)),
            pltpu.SemaphoreType.DMA((6,)),
        ],
        compiler_params=pltpu.CompilerParams(
            collective_id=0, has_side_effects=True, vmem_limit_bytes=VMEM_LIMIT
        ),
        name="step",
    )(*(pltpu.with_memory_space_constraint(v, pltpu.HBM) for v in (flow_state, x_codes, y_codes)))
    result = jnp.transpose(result.reshape(5, 8, 8, 128), (0, 2, 1, 3))
    return result.reshape(flow_state.shape)


def solution(mesh):
    return jax.shard_map(
        local,
        mesh=mesh,
        in_specs=(P(None, "gx", "gy"), P(None, "gy"), P(None, "gx")),
        out_specs=P(None, "gx", "gy"),
        check_vma=False,
    )
```
